32 devices in a mesh: groups: 2 (over x), dom: 16 (over z, y, core).
Axes of the slice: x: 2, y: 2, z: 4, core: 2. Of those that a mesh axis runs over, the one named last changes fastest.
Arguments:
- nodes: bfloat16 [4096, 256], P(('groups', 'dom')), parts along dimension 0, may hold values from -6 to 6
- cotangent: bfloat16 [4096, 256], P(('groups', 'dom')), parts along dimension 0, may hold values from -6 to 6
- fine_weights: bfloat16 [3, 256, 256], replicated, may hold values from -0.375 to 0.375
- coarse_weights: bfloat16 [3, 256, 256], replicated, may hold values from -0.375 to 0.375
- biases: float32 [2, 256], replicated, may hold values from -4 to 4
- send_lists: int32 [4, 256], P('groups', 'dom'), parts along dimension 0, may hold values from 0 to 127
- edge_ends: int32 [4, 24576], P('groups', 'dom'), parts along dimension 0, may hold values from 0 to 159, as said below
- live_blocks: int32 [32], P(('groups', 'dom')), parts along dimension 0, may hold values from 4 to 12, as said below
- pool_members: int32 [16, 256], P('groups', 'dom'), parts along dimension 0, may hold values from 0 to 127
- parents: int32 [4096], P(('groups', 'dom')), parts along dimension 0, may hold values from 0 to 15
- coarse_ends: int32 [4, 768], P('groups', 'dom'), parts along dimension 0, may hold values from 0 to 255
Outputs:
- moved_nodes: float32 [4096, 256], P(('groups', 'dom')), parts along dimension 0
- node_grads: float32 [4096, 256], P(('groups', 'dom')), parts along dimension 0
- fine_grads: float32 [6, 256, 256], P('groups'), parts along dimension 0
- coarse_grads: float32 [6, 256, 256], P('groups'), parts along dimension 0
- bias_grads: float32 [4, 256], P('groups'), parts along dimension 0
The draws below stay inside these ranges and needn't reach their ends.
There are 2 independent parts, one for each index of `groups`. The reference program is written for one: setup_inputs(seed, part) draws one part's arguments, and reference() takes and returns one part's arrays. A program takes and returns all parts, laid end to end along the dimension named above; an argument that names none is the same for every part. Nothing has to cross between parts.
Inputs may be any that keep to these rules, and one draw needn't show every extreme that they name: `edge_ends`: row 0 indexes the partition's extended table and never a row that is zeros; row 1 indexes a local node. `live_blocks`: some partition has all 12 blocks live.
All inputs are finite; a program needn't handle non-finite values.
Results may differ from the reference program's by a relative error of at most 0.0061.
Values may be sent and summed in bfloat16 or wider, within the bound.
No kernel may reach another device: no remote copies, remote signals or barrier semaphores. Data moves between devices by JAX's collectives and lax.ppermute only.
A program may use at most 64 MiB of HBM per device.

```python
import jax
import jax.numpy as jnp
from jax import lax

W = 256
NF = 128
K = 8
H = 16
NC = 16
EBMAX = 12
EDEV = 1536
NF_ALL = 2048
NCALL = 256
EDGES = 24576
EC = 768
N_DOM = 16


def draw_edge_ends(key, part):
    key = jax.random.fold_in(key, 11)
    first, second = jax.random.split(key)
    position = jnp.arange(EDGES)
    device = position // EDEV
    senders = jax.random.randint(first, (EDGES,), 0, NF + 2 * H)
    senders = jnp.where((device == 0) & (senders < H), senders + H, senders)
    senders = jnp.where((device == EDGES // EDEV - 1) & (senders >= NF + H), senders - H, senders)
    receivers = jax.random.randint(second, (EDGES,), 0, NF)
    return jnp.stack([senders, receivers]).astype(jnp.int32)


def draw_live_blocks(key, part):
    key = jax.random.fold_in(key, 12)
    first, second = jax.random.split(key)
    count = EDGES // EDEV
    blocks = jax.random.randint(first, (count,), EBMAX // 3, EBMAX + 1)
    chosen = jax.random.randint(second, (), 0, count)
    blocks = jnp.where(jnp.arange(count) == chosen, EBMAX, blocks)
    return blocks.astype(jnp.int32)


def place_ends(drawn, own_key, least, high):
    longest = drawn.shape.index(max(drawn.shape))
    spots = []
    for shift in (0, 1):
        where = [jax.random.randint(jax.random.fold_in(own_key, axis), (), 0, length) for axis, length in enumerate(drawn.shape)]
        where[longest] = (where[longest] + shift) % drawn.shape[longest]
        spots.append(tuple(where))
    return drawn.at[spots[0]].set(least).at[spots[1]].set(high)


def steps_of(stream_key, dims, cuts, smallest, high):
    gain, own = 1.0, jax.random.fold_in(stream_key, 6)
    for dim, shards_of in cuts:
        heights = jnp.exp(jax.random.uniform(jax.random.fold_in(own, dim), (shards_of,), jnp.float32, smallest / len(cuts), high / len(cuts)))
        gain = gain * jnp.repeat(heights, dims[dim] // shards_of).reshape([-1 if axis == dim else 1 for axis in range(len(dims))])
    return gain


def normal_values(rng, shape, scale, limit, cuts=(), kind=jnp.bfloat16):
    entries = scale * jax.random.normal(rng, shape, jnp.float32)
    if cuts:
        entries = entries * steps_of(rng, shape, cuts, -0.22, 0.18)
    return jnp.clip(entries, -limit, limit).astype(kind)


def setup_inputs(seed: int = 0, part: int = 0) -> dict:
    key_of = jax.random.split(jax.random.key(seed), 12)
    part_keys = jax.random.split(jax.random.fold_in(key_of[11], part), 12)
    return {
        "nodes": normal_values(part_keys[0], (NF_ALL, W), 1.0, 6.0, ((0, 16),)),
        "cotangent": normal_values(part_keys[1], (NF_ALL, W), 1.0, 6.0, ((0, 16),)),
        "fine_weights": normal_values(key_of[2], (3, W, W), W ** -0.5, 0.375),
        "coarse_weights": normal_values(key_of[3], (3, W, W), W ** -0.5, 0.375),
        "biases": normal_values(key_of[4], (2, W), 1.0, 4.0, (), jnp.float32),
        "send_lists": place_ends(jax.random.randint(part_keys[5], (2, N_DOM * H), 0, NF), jax.random.fold_in(part_keys[5], 1), 0, NF - 1).astype(jnp.int32),
        "edge_ends": draw_edge_ends(jax.random.fold_in(jax.random.fold_in(key_of[11], part), 71), part),
        "live_blocks": draw_live_blocks(jax.random.fold_in(jax.random.fold_in(key_of[11], part), 71), part),
        "pool_members": place_ends(jax.random.randint(part_keys[8], (K, NCALL), 0, NF), jax.random.fold_in(part_keys[8], 1), 0, NF - 1).astype(jnp.int32),
        "parents": place_ends(jax.random.randint(part_keys[9], (NF_ALL,), 0, NC), jax.random.fold_in(part_keys[9], 1), 0, NC - 1).astype(jnp.int32),
        "coarse_ends": place_ends(jax.random.randint(part_keys[10], (2, EC), 0, NCALL), jax.random.fold_in(part_keys[10], 1), 0, NCALL - 1).astype(jnp.int32),
    }


def silu_slope(value):
    sig = jax.nn.sigmoid(value)
    return sig * (1.0 + value * (1.0 - sig))


def precise_dot(left, right):
    return jnp.dot(left, right, precision=lax.Precision.HIGHEST)


def take_rows(table, index):
    return table[index]


def segment_rows(values, index, count):
    return jax.ops.segment_sum(values, index, count)


def reference(nodes, cotangent, fine_weights, coarse_weights, biases, send_lists, edge_ends, live_blocks, pool_members, parents, coarse_ends):
    width = W
    node_sets = nodes.reshape(N_DOM, NF, width)
    lists = send_lists.reshape(2, N_DOM, H)
    to_lower = jax.vmap(take_rows)(node_sets, lists[0])
    to_upper = jax.vmap(take_rows)(node_sets, lists[1])
    blank = jnp.zeros((1, H, width), nodes.dtype)
    lower_rim = jnp.concatenate([blank, to_upper[:-1]], 0)
    upper_rim = jnp.concatenate([to_lower[1:], blank], 0)
    extended = jnp.concatenate([lower_rim, node_sets, upper_rim], 1)
    rows_ext = NF + 2 * H
    fine_src, fine_dst, fine_out = fine_weights[0], fine_weights[1], fine_weights[2]
    src_proj = jnp.dot(extended.reshape(-1, width), fine_src, preferred_element_type=jnp.float32).astype(jnp.bfloat16).reshape(N_DOM, rows_ext, width)
    dst_proj = jnp.dot(nodes, fine_dst, preferred_element_type=jnp.float32).astype(jnp.bfloat16).reshape(N_DOM, NF, width)
    ends = edge_ends.reshape(2, N_DOM, EDEV)
    senders, receivers = ends[0], ends[1]
    live_mask = ((jnp.arange(EDEV) // 128)[None, :] < live_blocks[:, None]).astype(jnp.float32)[..., None]
    pre_act = jax.vmap(take_rows)(src_proj, senders).astype(jnp.float32) + jax.vmap(take_rows)(dst_proj, receivers).astype(jnp.float32) + biases[0]
    messages = jax.nn.silu(pre_act) * live_mask
    summed = jax.vmap(lambda m, r: segment_rows(m, r, NF))(messages, receivers).astype(jnp.bfloat16)
    updated = node_sets.astype(jnp.float32) + jnp.dot(summed.reshape(-1, width), fine_out, preferred_element_type=jnp.float32).reshape(N_DOM, NF, width)
    members = pool_members.reshape(K, N_DOM, NC)
    gathered = jax.vmap(lambda m: jax.vmap(take_rows)(updated, m))(members)
    coarse = (jnp.sum(gathered, 0) / K).astype(jnp.bfloat16).reshape(NCALL, width)
    coarse_src, coarse_dst, coarse_out = coarse_weights[0], coarse_weights[1], coarse_weights[2]
    src2 = jnp.dot(coarse, coarse_src, preferred_element_type=jnp.float32).astype(jnp.bfloat16)
    dst2 = jnp.dot(coarse, coarse_dst, preferred_element_type=jnp.float32).astype(jnp.bfloat16)
    senders2, receivers2 = coarse_ends[0], coarse_ends[1]
    pre2 = src2[senders2].astype(jnp.float32) + dst2[receivers2].astype(jnp.float32) + biases[1]
    coarse_sum = segment_rows(jax.nn.silu(pre2), receivers2, NCALL).astype(jnp.bfloat16)
    coarse_new = coarse.astype(jnp.float32) + jnp.dot(coarse_sum, coarse_out, preferred_element_type=jnp.float32)
    parent_sets = parents.reshape(N_DOM, NF)
    moved = updated + jax.vmap(take_rows)(coarse_new.reshape(N_DOM, NC, width), parent_sets)

    upstream = cotangent.astype(jnp.float32).reshape(N_DOM, NF, width)
    parent_grad = jax.vmap(lambda g, p: segment_rows(g, p, NC))(upstream, parent_sets).astype(jnp.bfloat16).reshape(NCALL, width)
    parent_all = parent_grad.astype(jnp.float32)
    grad_out2 = precise_dot(coarse_sum.astype(jnp.float32).T, parent_all)
    grad_agg2 = precise_dot(parent_all, coarse_out.astype(jnp.float32).T)
    slope2 = grad_agg2[receivers2] * silu_slope(pre2)
    bias2 = jnp.sum(slope2, 0)
    grad_src2 = segment_rows(slope2, senders2, NCALL)
    grad_dst2 = segment_rows(slope2, receivers2, NCALL)
    coarse_f32 = coarse.astype(jnp.float32)
    grad_s2 = precise_dot(coarse_f32.T, grad_src2)
    grad_r2 = precise_dot(coarse_f32.T, grad_dst2)
    coarse_grad = parent_all + precise_dot(grad_src2, coarse_src.astype(jnp.float32).T) + precise_dot(grad_dst2, coarse_dst.astype(jnp.float32).T)
    spread = jnp.broadcast_to((coarse_grad / K).reshape(1, N_DOM, NC, width), (K, N_DOM, NC, width))
    spread = jnp.transpose(spread, (1, 0, 2, 3)).reshape(N_DOM, K * NC, width)
    member_flat = jnp.transpose(members, (1, 0, 2)).reshape(N_DOM, K * NC)
    grad_updated = upstream + jax.vmap(lambda v, i: segment_rows(v, i, NF))(spread, member_flat)
    grad_flat = grad_updated.reshape(-1, width)
    grad_u = precise_dot(summed.astype(jnp.float32).reshape(-1, width).T, grad_flat)
    grad_summed = precise_dot(grad_flat, fine_out.astype(jnp.float32).T).reshape(N_DOM, NF, width)
    slope = jax.vmap(take_rows)(grad_summed, receivers) * live_mask * silu_slope(pre_act)
    bias1 = jnp.sum(slope, (0, 1))
    grad_src = jax.vmap(lambda v, i: segment_rows(v, i, rows_ext))(slope, senders)
    grad_dst = jax.vmap(lambda v, i: segment_rows(v, i, NF))(slope, receivers)
    grad_s = precise_dot(extended.astype(jnp.float32).reshape(-1, width).T, grad_src.reshape(-1, width))
    grad_r = precise_dot(node_sets.astype(jnp.float32).reshape(-1, width).T, grad_dst.reshape(-1, width))
    grad_ext = precise_dot(grad_src.reshape(-1, width), fine_src.astype(jnp.float32).T).reshape(N_DOM, rows_ext, width)
    zero_rows = jnp.zeros((1, H, width), jnp.float32)
    from_lower = jnp.concatenate([zero_rows, grad_ext[:-1, NF + H:]], 0)
    from_upper = jnp.concatenate([grad_ext[1:, :H], zero_rows], 0)
    node_grads = grad_updated + grad_ext[:, H:H + NF] + precise_dot(grad_dst.reshape(-1, width), fine_dst.astype(jnp.float32).T).reshape(N_DOM, NF, width)
    node_grads = node_grads + jax.vmap(lambda v, i: segment_rows(v, i, NF))(from_lower, lists[0])
    node_grads = node_grads + jax.vmap(lambda v, i: segment_rows(v, i, NF))(from_upper, lists[1])
    return (moved.reshape(NF_ALL, width), node_grads.reshape(NF_ALL, width), jnp.stack([grad_s, grad_r, grad_u]), jnp.stack([grad_s2, grad_r2, grad_out2]), jnp.stack([bias1, bias2]))
```

```python
import functools

import jax
import jax.numpy as jnp
from jax import lax
from jax.experimental import pallas as pl
from jax.experimental.pallas import tpu as pltpu
from jax.sharding import PartitionSpec as P

BF16 = jnp.bfloat16
F32 = jnp.float32
EDGE_BLOCK = 128
ROW_TILE = 16
VMEM_LIMIT = 56 * 1024 * 1024


def dot(left, right):
    return jnp.dot(left, right, preferred_element_type=F32)


def dot_tn(left, right):
    return lax.dot_general(left, right, (((0,), (0,)), ((), ())), preferred_element_type=F32)


def dot_nt(left, right):
    return lax.dot_general(left, right, (((1,), (1,)), ((), ())), preferred_element_type=F32)


def split(value):
    high = value.astype(BF16)
    return high, (value - high.astype(F32)).astype(BF16)


def one_hot_rows(index_row, count):
    spots = lax.broadcasted_iota(jnp.int32, (count, index_row.shape[1]), 0)
    return jnp.where(spots == index_row, 1.0, 0.0).astype(BF16)


def one_hot_cols(index_col, count):
    spots = lax.broadcasted_iota(jnp.int32, (index_col.shape[0], count), 1)
    return jnp.where(spots == index_col, 1.0, 0.0).astype(BF16)


def to_column(index_row):
    return jnp.transpose(jnp.broadcast_to(index_row, (8, index_row.shape[1])))[:, :1]


def silu_and_slope(value):
    sig = 0.5 * jnp.tanh(0.5 * value) + 0.5
    message = value * sig
    return message, sig + message * (1.0 - sig)


def membership(members, node_count):
    spots = lax.broadcasted_iota(jnp.int32, (node_count, members.shape[1]), 0)
    total = jnp.zeros(spots.shape, F32)
    for row in range(members.shape[0]):
        total = total + jnp.where(spots == members[row : row + 1], 1.0, 0.0)
    return total.astype(BF16)


def place():
    me = lax.axis_index("dom")
    return me, lax.rem(me, 2), lax.div(me, 2)


def live_rows(ends_ref, live_ref, row):
    index = ends_ref[row : row + 1, :]
    slot = lax.broadcasted_iota(jnp.int32, index.shape, 1)
    return jnp.where(slot < live_ref[0] * EDGE_BLOCK, index, -1)


def pick_kernel(nodes_ref, lists_ref, near_ref, far_ref):
    _, odd, _ = place()
    lists = lists_ref[...]
    near = jnp.where(odd == 1, lists[0:1], lists[1:2])
    far = jnp.where(odd == 1, lists[1:2], lists[0:1])
    nodes = nodes_ref[...]
    near_ref[...] = dot_tn(one_hot_rows(near, nodes.shape[0]), nodes).astype(BF16)
    far_ref[...] = dot_tn(one_hot_rows(far, nodes.shape[0]), nodes).astype(BF16)


def extend(nodes, near, far, odd):
    low = jnp.where(odd == 1, near, far)
    high = jnp.where(odd == 1, far, near)
    return jnp.concatenate([low, nodes, high], 0)


def forward_kernel(
    ndom,
    nodes_ref,
    near_ref,
    far_ref,
    weights_ref,
    biases_ref,
    ends_ref,
    live_ref,
    members_ref,
    parents_ref,
    cotangent_ref,
    links_ref,
    updated_ref,
    summed_ref,
    slopes_sum_ref,
    slopes_ref,
    packet_ref,
    message_ref,
    link_ref,
):
    me, odd, _ = place()
    nodes = nodes_ref[...]
    node_count, width = nodes.shape
    coarse_count = members_ref.shape[1]
    extended = extend(nodes, near_ref[...], far_ref[...], odd)
    src_proj = dot(extended, weights_ref[0]).astype(BF16)
    dst_proj = dot(nodes, weights_ref[1]).astype(BF16)
    slots = ends_ref.shape[1]
    chunk = 2 * EDGE_BLOCK
    bias = biases_ref[0:1, :]
    for start in range(0, slots, chunk):
        senders = to_column(ends_ref[0:1, start : start + chunk])
        receivers = to_column(ends_ref[1:2, start : start + chunk])
        pre = (
            dot(one_hot_cols(senders, extended.shape[0]), src_proj)
            + dot(one_hot_cols(receivers, node_count), dst_proj)
            + bias
        )
        message, slope = silu_and_slope(pre)
        message_ref[start : start + chunk, :] = message.astype(BF16)
        slopes_ref[start : start + chunk, :] = slope.astype(BF16)
    into = one_hot_rows(live_rows(ends_ref, live_ref, 1), node_count)
    summed = dot(into, message_ref[...]).astype(BF16)
    slopes_sum_ref[...] = dot(into, slopes_ref[...])
    summed_ref[...] = summed
    updated = nodes.astype(F32) + dot(summed, weights_ref[2])
    updated_ref[...] = updated

    share = membership(members_ref[...], node_count)
    high, low = split(updated)
    pooled = dot_tn(share, high) + dot_tn(share, low)
    coarse = (pooled / members_ref.shape[0]).astype(BF16)
    family = one_hot_rows(parents_ref[...], coarse_count)
    parent_grad = dot(family, cotangent_ref[...]).astype(BF16)

    links = links_ref[...]
    own = links.shape[1]
    rows = link_ref.shape[0]
    pieces = -(-own * ndom // width)
    spot = lax.broadcasted_iota(jnp.int32, (own, pieces * width), 1)
    source = lax.broadcasted_iota(jnp.int32, (own, pieces * width), 0)
    spread = jnp.where(spot == source + me * own, 1.0, 0.0).astype(BF16)
    coded = (
        dot((links >> 8).astype(F32).astype(BF16), spread),
        dot((links & 255).astype(F32).astype(BF16), spread),
    )
    link_ref[...] = jnp.zeros(link_ref.shape, F32)
    for part in range(2):
        for end in range(2):
            for piece in range(pieces):
                row = (part * 2 + end) * pieces + piece
                link_ref[row : row + 1, :] = coded[part][
                    end : end + 1, piece * width : (piece + 1) * width
                ]
    coded_links = link_ref[...].astype(BF16)
    for chip in range(packet_ref.shape[0]):
        packet_ref[chip, :coarse_count, :] = coarse
        packet_ref[chip, coarse_count : 2 * coarse_count, :] = parent_grad
        packet_ref[chip, 2 * coarse_count : 2 * coarse_count + rows, :] = coded_links


def ordered(mine_ref, theirs_ref, odd, start, count):
    blocks = []
    for chip in range(mine_ref.shape[0]):
        mine = mine_ref[chip, start : start + count, :]
        theirs = theirs_ref[chip, start : start + count, :]
        blocks.append(jnp.where(odd == 1, theirs, mine))
        blocks.append(jnp.where(odd == 1, mine, theirs))
    return blocks


def backward_kernel(
    ndom,
    edge_count2,
    mine_ref,
    theirs_ref,
    coarse_weights_ref,
    biases_ref,
    nodes_ref,
    near_ref,
    far_ref,
    weights_ref,
    ends_ref,
    live_ref,
    members_ref,
    parents_ref,
    cotangent_ref,
    updated_ref,
    summed_ref,
    slopes_sum_ref,
    slopes_ref,
    moved_ref,
    node_part_ref,
    coarse_grads_ref,
    bias2_ref,
    send_ref,
    keep_ref,
    link_ref,
    message2_ref,
    slope2_ref,
    edge2_ref,
    own_ref,
    grads_ref,
    edge_ref,
):
    me, odd, _ = place()
    nodes = nodes_ref[...]
    node_count, width = nodes.shape
    coarse_count = members_ref.shape[1]
    member_count = members_ref.shape[0]
    total = ndom * coarse_count

    coarse = jnp.concatenate(ordered(mine_ref, theirs_ref, odd, 0, coarse_count), 0)
    parent_all = jnp.concatenate(
        ordered(mine_ref, theirs_ref, odd, coarse_count, coarse_count), 0
    )
    link_rows = link_ref.shape[0]
    gathered = jnp.zeros(link_ref.shape, F32)
    for chip in range(mine_ref.shape[0]):
        for ref in (mine_ref, theirs_ref):
            gathered = gathered + ref[
                chip, 2 * coarse_count : 2 * coarse_count + link_rows, :
            ].astype(F32)
    link_ref[...] = gathered
    pieces = -(-edge_count2 // width)
    ends2 = []
    for end in range(2):
        rows = []
        for piece in range(pieces):
            top = end * pieces + piece
            bottom = (2 + end) * pieces + piece
            code = 256.0 * link_ref[top : top + 1, :] + link_ref[bottom : bottom + 1, :]
            spot = lax.broadcasted_iota(jnp.int32, code.shape, 1) + piece * width
            rows.append(jnp.where(spot < edge_count2, code.astype(jnp.int32), -1))
        ends2.append(rows)
    src2 = dot(coarse, coarse_weights_ref[0]).astype(BF16)
    dst2 = dot(coarse, coarse_weights_ref[1]).astype(BF16)
    grad_agg2 = dot_nt(parent_all, coarse_weights_ref[2])
    grad_agg2_near = grad_agg2.astype(BF16)
    bias = biases_ref[1:2, :]
    for piece in range(pieces):
        span = slice(piece * width, (piece + 1) * width)
        from_nodes = one_hot_cols(to_column(ends2[0][piece]), total)
        to_nodes = one_hot_cols(to_column(ends2[1][piece]), total)
        pre = dot(from_nodes, src2) + dot(to_nodes, dst2) + bias
        message, slope = silu_and_slope(pre)
        message2_ref[span, :] = message.astype(BF16)
        slope2_ref[span, :] = slope.astype(BF16)
        edge2_ref[span, :] = (dot(to_nodes, grad_agg2_near) * slope).astype(BF16)
    into = jnp.concatenate([one_hot_rows(row, total) for row in ends2[1]], 1)
    coarse_sum = dot(into, message2_ref[...]).astype(BF16)
    grad_dst2 = dot(into, slope2_ref[...]) * grad_agg2
    back = jnp.concatenate([one_hot_rows(row, total) for row in ends2[0]], 1)
    grad_src2 = dot(back, edge2_ref[...])
    bias2_ref[...] = jnp.sum(grad_dst2, 0, keepdims=True)
    grad_src2 = grad_src2.astype(BF16)
    grad_dst2 = grad_dst2.astype(BF16)
    coarse_grads_ref[0] = dot_tn(coarse, grad_src2)
    coarse_grads_ref[1] = dot_tn(coarse, grad_dst2)
    coarse_grads_ref[2] = dot_tn(coarse_sum, parent_all)

    own_ref[0] = coarse
    own_ref[1] = parent_all
    own_ref[2] = coarse_sum
    own_ref[3] = grad_src2
    own_ref[4] = grad_dst2
    rows = pl.ds(pl.multiple_of(me * coarse_count, coarse_count), coarse_count)
    coarse_new = own_ref[0, rows, :].astype(F32) + dot(own_ref[2, rows, :], coarse_weights_ref[2])
    coarse_grad = (
        own_ref[1, rows, :].astype(F32)
        + dot_nt(own_ref[3, rows, :], coarse_weights_ref[0])
        + dot_nt(own_ref[4, rows, :], coarse_weights_ref[1])
    )
    family = one_hot_rows(parents_ref[...], coarse_count)
    high, low = split(coarse_new)
    moved_ref[...] = updated_ref[...] + dot_tn(family, high) + dot_tn(family, low)
    share = membership(members_ref[...], node_count)
    high, low = split(coarse_grad / member_count)
    grad_updated = cotangent_ref[...].astype(F32) + dot(share, high) + dot(share, low)

    extended = extend(nodes, near_ref[...], far_ref[...], odd)
    rim = near_ref.shape[0]
    slots = ends_ref.shape[1]
    grad_updated_near = grad_updated.astype(BF16)
    grad_summed = dot_nt(grad_updated_near, weights_ref[2])
    grad_summed_near = grad_summed.astype(BF16)
    grad_dst = slopes_sum_ref[...] * grad_summed
    chunk = 2 * EDGE_BLOCK
    for start in range(0, slots, chunk):
        receivers = to_column(ends_ref[1:2, start : start + chunk])
        slope = slopes_ref[start : start + chunk, :].astype(F32)
        edge = dot(one_hot_cols(receivers, node_count), grad_summed_near) * slope
        edge_ref[start : start + chunk, :] = edge.astype(BF16)
    back = one_hot_rows(live_rows(ends_ref, live_ref, 0), extended.shape[0])
    grad_src = dot(back, edge_ref[...]).astype(BF16)
    bias1 = jnp.sum(grad_dst, 0, keepdims=True)
    grad_dst = grad_dst.astype(BF16)
    both = jnp.concatenate([grad_src[rim : rim + node_count], grad_dst], 1)
    node_part_ref[...] = grad_updated + dot_nt(
        both, jnp.concatenate([weights_ref[0], weights_ref[1]], 1)
    )
    low = dot_nt(grad_src[:rim], weights_ref[0]).astype(BF16)
    high = dot_nt(grad_src[rim + node_count :], weights_ref[0]).astype(BF16)
    grads_ref[0:width, :] = dot_tn(extended, grad_src).astype(BF16)
    grads_ref[width : 2 * width, :] = dot_tn(nodes, grad_dst).astype(BF16)
    grads_ref[2 * width : 3 * width, :] = dot_tn(summed_ref[...], grad_updated_near).astype(BF16)
    if grads_ref.shape[0] > 3 * width:
        grads_ref[3 * width :, :] = jnp.zeros((grads_ref.shape[0] - 3 * width, width), BF16)
    half = grads_ref.shape[0] // 2
    keep_ref[:half, :] = grads_ref[pl.ds(pl.multiple_of(odd * half, ROW_TILE), half), :]
    send_ref[:half, :] = grads_ref[pl.ds(pl.multiple_of((1 - odd) * half, ROW_TILE), half), :]
    bias_rows = two_rows(bias1)
    keep_ref[half : half + ROW_TILE, :] = bias_rows
    send_ref[half : half + ROW_TILE, :] = bias_rows
    base = half + ROW_TILE
    send_ref[base : base + rim, :] = jnp.where(odd == 1, low, high)
    send_ref[base + rim : base + 2 * rim, :] = jnp.where(odd == 1, high, low)


def two_rows(value):
    high = value.astype(BF16).astype(F32)
    row = lax.broadcasted_iota(jnp.int32, (ROW_TILE, value.shape[1]), 0)
    return jnp.where(row == 0, high, jnp.where(row == 1, value - high, 0.0)).astype(BF16)


def pair_kernel(keep_ref, came_ref, blocks_ref):
    half = keep_ref.shape[0] - ROW_TILE
    chips, depth, _ = blocks_ref.shape
    rim = came_ref.shape[0] - half - ROW_TILE
    rim = rim // 2
    rows = half // chips
    bias = keep_ref[half:, :].astype(F32) + came_ref[half : half + ROW_TILE, :].astype(F32)
    bias = two_rows(jnp.sum(bias, 0, keepdims=True))
    far = came_ref[half + ROW_TILE + rim :, :]
    for chip in range(chips):
        span = slice(chip * rows, (chip + 1) * rows)
        blocks_ref[chip, :rows, :] = (
            keep_ref[span, :].astype(F32) + came_ref[span, :].astype(F32)
        ).astype(BF16)
        blocks_ref[chip, rows : rows + ROW_TILE, :] = bias
        blocks_ref[chip, rows + ROW_TILE :, :] = far


def sum_kernel(
    blocks_ref, came_ref, node_part_ref, lists_ref, bias2_ref, part_ref, node_grads_ref, bias_ref
):
    _, odd, chip = place()
    chips, rows, _ = part_ref.shape
    rim = lists_ref.shape[1]
    half = chips * rows
    total = blocks_ref[0, : rows + ROW_TILE, :].astype(F32)
    for other in range(1, chips):
        total = total + blocks_ref[other, : rows + ROW_TILE, :].astype(F32)
    part = total[:rows].astype(BF16)
    for other in range(chips):
        part_ref[other] = part
    bias_ref[0:1, :] = jnp.sum(total[rows:], 0, keepdims=True)
    bias_ref[1:2, :] = bias2_ref[...]
    lists = lists_ref[...]
    near_list = jnp.where(odd == 1, lists[0:1], lists[1:2])
    far_list = jnp.where(odd == 1, lists[1:2], lists[0:1])
    origin = jnp.where(odd == 1, chip + 1, chip - 1)
    inside = jnp.logical_and(origin >= 0, origin < chips)
    far_list = jnp.where(inside, far_list, -1)
    origin = jnp.clip(origin, 0, chips - 1)
    near = came_ref[half + ROW_TILE : half + ROW_TILE + rim, :]
    far = blocks_ref[origin, rows + ROW_TILE : rows + ROW_TILE + rim, :]
    node_count = node_part_ref.shape[0]
    node_grads_ref[...] = (
        node_part_ref[...]
        + dot(one_hot_rows(near_list, node_count), near)
        + dot(one_hot_rows(far_list, node_count), far)
    )


def join_kernel(mine_ref, theirs_ref, out_ref):
    _, odd, _ = place()
    chips, rows, _ = mine_ref.shape
    limit = out_ref.shape[0]
    for side in range(2):
        for chip in range(chips):
            start = (side * chips + chip) * rows
            count = min(rows, limit - start)
            if count <= 0:
                continue
            mine = mine_ref[chip, :count, :]
            theirs = theirs_ref[chip, :count, :]
            out_ref[start : start + count, :] = jnp.where(odd == side, mine, theirs).astype(F32)


def call(kernel, outs, args, scratch=(), scalars=()):
    whole = pl.BlockSpec(memory_space=pltpu.VMEM)
    scalar = pl.BlockSpec(memory_space=pltpu.SMEM)
    return pl.pallas_call(
        kernel,
        out_shape=[jax.ShapeDtypeStruct(shape, kind) for shape, kind in outs],
        in_specs=[scalar if spot in scalars else whole for spot in range(len(args))],
        out_specs=[whole] * len(outs),
        scratch_shapes=[pltpu.VMEM(shape, kind) for shape, kind in scratch],
        compiler_params=pltpu.CompilerParams(vmem_limit_bytes=VMEM_LIMIT),
    )(*args)


def round_up(value, unit):
    return -(-value // unit) * unit


def shards(
    nodes,
    cotangent,
    fine_weights,
    coarse_weights,
    biases,
    send_lists,
    edge_ends,
    live_blocks,
    pool_members,
    parents,
    coarse_ends,
):
    ndom = lax.axis_size("dom")
    chips = ndom // 2
    node_count, width = nodes.shape
    rim = send_lists.shape[1]
    coarse_count = pool_members.shape[1]
    slots = edge_ends.shape[1]
    edge_count2 = coarse_ends.shape[1] * ndom
    total = coarse_count * ndom
    parents = parents.reshape(1, node_count)
    pairs = [(i, i ^ 1) for i in range(ndom)]
    across = [(i, i + 1) for i in range(1, ndom - 1, 2)]
    across = across + [(target, source) for source, target in across]
    same_core = [[2 * chip + core for chip in range(chips)] for core in range(2)]

    def swap(value):
        return lax.ppermute(value, "dom", pairs)

    def exchange(value):
        return lax.all_to_all(value, "dom", 0, 0, axis_index_groups=same_core)

    near, far = call(
        pick_kernel, [((rim, width), BF16), ((rim, width), BF16)], (nodes, send_lists)
    )
    far = lax.ppermute(far, "dom", across)
    near = swap(near)

    pieces = -(-edge_count2 // width)
    link_rows = round_up(4 * pieces, ROW_TILE)
    packet_rows = 2 * coarse_count + link_rows
    updated, summed, slopes_sum, slopes, packet = call(
        functools.partial(forward_kernel, ndom),
        [
            ((node_count, width), F32),
            ((node_count, width), BF16),
            ((node_count, width), F32),
            ((slots, width), BF16),
            ((chips, packet_rows, width), BF16),
        ],
        (
            nodes,
            near,
            far,
            fine_weights,
            biases,
            edge_ends,
            live_blocks,
            pool_members,
            parents,
            cotangent,
            coarse_ends,
        ),
        scratch=[((slots, width), BF16), ((link_rows, width), F32)],
        scalars=(6,),
    )
    mine = exchange(packet)
    theirs = swap(mine)

    rows = round_up(-(-3 * width // ndom), ROW_TILE)
    half = rows * chips
    edges2 = pieces * width
    moved, node_part, coarse_grads, bias2, send, keep = call(
        functools.partial(backward_kernel, ndom, edge_count2),
        [
            ((node_count, width), F32),
            ((node_count, width), F32),
            ((3, width, width), F32),
            ((1, width), F32),
            ((half + ROW_TILE + 2 * rim, width), BF16),
            ((half + ROW_TILE, width), BF16),
        ],
        (
            mine,
            theirs,
            coarse_weights,
            biases,
            nodes,
            near,
            far,
            fine_weights,
            edge_ends,
            live_blocks,
            pool_members,
            parents,
            cotangent,
            updated,
            summed,
            slopes_sum,
            slopes,
        ),
        scratch=[
            ((link_rows, width), F32),
            ((edges2, width), BF16),
            ((edges2, width), BF16),
            ((edges2, width), BF16),
            ((5, total, width), BF16),
            ((2 * half, width), BF16),
            ((slots, width), BF16),
        ],
        scalars=(9,),
    )
    came = swap(send)
    (blocks,) = call(
        pair_kernel, [((chips, rows + ROW_TILE + rim, width), BF16)], (keep, came)
    )
    blocks = exchange(blocks)
    part, node_grads, bias_grads = call(
        sum_kernel,
        [
            ((chips, rows, width), BF16),
            ((node_count, width), F32),
            ((2, width), F32),
        ],
        (blocks, came, node_part, send_lists, bias2),
    )
    mine = exchange(part)
    theirs = swap(mine)
    (fine_grads,) = call(join_kernel, [((3 * width, width), F32)], (mine, theirs))
    return moved, node_grads, fine_grads.reshape(3, width, width), coarse_grads, bias_grads


def solution(mesh):
    return jax.shard_map(
        shards,
        mesh=mesh,
        in_specs=(
            P(("groups", "dom"), None),
            P(("groups", "dom"), None),
            P(),
            P(),
            P(),
            P("groups", "dom"),
            P("groups", "dom"),
            P(("groups", "dom")),
            P("groups", "dom"),
            P(("groups", "dom")),
            P("groups", "dom"),
        ),
        out_specs=(
            P(("groups", "dom"), None),
            P(("groups", "dom"), None),
            P("groups", None, None),
            P("groups", None, None),
            P("groups", None),
        ),
        check_vma=False,
    )
```

```python
import functools

import jax
import jax.numpy as jnp
from jax import lax
from jax.experimental import pallas as pl
from jax.experimental.pallas import tpu as pltpu
from jax.sharding import PartitionSpec as P

BF16 = jnp.bfloat16
F32 = jnp.float32
EDGE_BLOCK = 128
ROW_TILE = 16
MIB = 1024 * 1024


def dot(left, right):
    return jnp.dot(left, right, preferred_element_type=F32)


def dot_tn(left, right):
    return lax.dot_general(left, right, (((0,), (0,)), ((), ())), preferred_element_type=F32)


def dot_nt(left, right):
    return lax.dot_general(left, right, (((1,), (1,)), ((), ())), preferred_element_type=F32)


def split(value):
    high = value.astype(BF16)
    return high, (value - high.astype(F32)).astype(BF16)


def one_hot_rows(index_row, count):
    spots = lax.broadcasted_iota(jnp.int32, (count, index_row.shape[1]), 0)
    return jnp.where(spots == index_row, 1.0, 0.0).astype(BF16)


def one_hot_cols(index_col, count):
    spots = lax.broadcasted_iota(jnp.int32, (index_col.shape[0], count), 1)
    return jnp.where(spots == index_col, 1.0, 0.0).astype(BF16)


def to_column(index_row):
    return jnp.transpose(jnp.broadcast_to(index_row, (8, index_row.shape[1])))[:, :1]


def silu_and_slope(value):
    sig = 0.5 * jnp.tanh(0.5 * value) + 0.5
    message = value * sig
    return message, sig + message * (1.0 - sig)


def membership(members, node_count):
    spots = lax.broadcasted_iota(jnp.int32, (node_count, members.shape[1]), 0)
    total = jnp.zeros(spots.shape, F32)
    for row in range(members.shape[0]):
        total = total + jnp.where(spots == members[row : row + 1], 1.0, 0.0)
    return total.astype(BF16)


def place():
    me = lax.axis_index("dom")
    return me, lax.rem(me, 2), lax.div(me, 2)


def live_rows(ends_ref, live_ref, row):
    index = ends_ref[row : row + 1, :]
    slot = lax.broadcasted_iota(jnp.int32, index.shape, 1)
    return jnp.where(slot < live_ref[0] * EDGE_BLOCK, index, -1)


def pick_kernel(nodes_ref, lists_ref, near_ref, far_ref):
    _, odd, _ = place()
    lists = lists_ref[...]
    near = jnp.where(odd == 1, lists[0:1], lists[1:2])
    far = jnp.where(odd == 1, lists[1:2], lists[0:1])
    nodes = nodes_ref[...]
    near_ref[...] = dot_tn(one_hot_rows(near, nodes.shape[0]), nodes).astype(BF16)
    far_ref[...] = dot_tn(one_hot_rows(far, nodes.shape[0]), nodes).astype(BF16)


def extend(nodes, near, far, odd):
    low = jnp.where(odd == 1, near, far)
    high = jnp.where(odd == 1, far, near)
    return jnp.concatenate([low, nodes, high], 0)


def forward_kernel(
    ndom,
    nodes_ref,
    near_ref,
    far_ref,
    weights_ref,
    biases_ref,
    ends_ref,
    live_ref,
    members_ref,
    parents_ref,
    cotangent_ref,
    links_ref,
    updated_ref,
    summed_ref,
    slopes_sum_ref,
    slopes_ref,
    packet_ref,
    message_ref,
    link_ref,
):
    me, odd, _ = place()
    nodes = nodes_ref[...]
    node_count, width = nodes.shape
    coarse_count = members_ref.shape[1]
    extended = extend(nodes, near_ref[...], far_ref[...], odd)
    src_proj = dot(extended, weights_ref[0]).astype(BF16)
    dst_proj = dot(nodes, weights_ref[1]).astype(BF16)
    slots = ends_ref.shape[1]
    chunk = 2 * EDGE_BLOCK
    bias = biases_ref[0:1, :]
    for start in range(0, slots, chunk):
        senders = to_column(ends_ref[0:1, start : start + chunk])
        receivers = to_column(ends_ref[1:2, start : start + chunk])
        pre = (
            dot(one_hot_cols(senders, extended.shape[0]), src_proj)
            + dot(one_hot_cols(receivers, node_count), dst_proj)
            + bias
        )
        message, slope = silu_and_slope(pre)
        message_ref[start : start + chunk, :] = message.astype(BF16)
        slopes_ref[start : start + chunk, :] = slope.astype(BF16)
    into = one_hot_rows(live_rows(ends_ref, live_ref, 1), node_count)
    summed = dot(into, message_ref[...]).astype(BF16)
    slopes_sum_ref[...] = dot(into, slopes_ref[...])
    summed_ref[...] = summed
    updated = nodes.astype(F32) + dot(summed, weights_ref[2])
    updated_ref[...] = updated

    share = membership(members_ref[...], node_count)
    high, low = split(updated)
    pooled = dot_tn(share, high) + dot_tn(share, low)
    coarse = (pooled / members_ref.shape[0]).astype(BF16)
    family = one_hot_rows(parents_ref[...], coarse_count)
    parent_grad = dot(family, cotangent_ref[...]).astype(BF16)

    links = links_ref[...]
    own = links.shape[1]
    rows = link_ref.shape[0]
    pieces = -(-own * ndom // width)
    spot = lax.broadcasted_iota(jnp.int32, (own, pieces * width), 1)
    source = lax.broadcasted_iota(jnp.int32, (own, pieces * width), 0)
    spread = jnp.where(spot == source + me * own, 1.0, 0.0).astype(BF16)
    coded = (
        dot((links >> 8).astype(F32).astype(BF16), spread),
        dot((links & 255).astype(F32).astype(BF16), spread),
    )
    link_ref[...] = jnp.zeros(link_ref.shape, F32)
    for part in range(2):
        for end in range(2):
            for piece in range(pieces):
                row = (part * 2 + end) * pieces + piece
                link_ref[row : row + 1, :] = coded[part][
                    end : end + 1, piece * width : (piece + 1) * width
                ]
    coded_links = link_ref[...].astype(BF16)
    for chip in range(packet_ref.shape[0]):
        packet_ref[chip, :coarse_count, :] = coarse
        packet_ref[chip, coarse_count : 2 * coarse_count, :] = parent_grad
        packet_ref[chip, 2 * coarse_count : 2 * coarse_count + rows, :] = coded_links


def ordered(mine_ref, theirs_ref, odd, start, count):
    blocks = []
    for chip in range(mine_ref.shape[0]):
        mine = mine_ref[chip, start : start + count, :]
        theirs = theirs_ref[chip, start : start + count, :]
        blocks.append(jnp.where(odd == 1, theirs, mine))
        blocks.append(jnp.where(odd == 1, mine, theirs))
    return blocks


def backward_kernel(
    ndom,
    edge_count2,
    mine_ref,
    theirs_ref,
    coarse_weights_ref,
    biases_ref,
    nodes_ref,
    near_ref,
    far_ref,
    weights_ref,
    ends_ref,
    live_ref,
    members_ref,
    parents_ref,
    cotangent_ref,
    updated_ref,
    summed_ref,
    slopes_sum_ref,
    slopes_ref,
    moved_ref,
    node_part_ref,
    coarse_grads_ref,
    bias2_ref,
    send_ref,
    keep_ref,
    link_ref,
    message2_ref,
    slope2_ref,
    edge2_ref,
    own_ref,
    grads_ref,
    edge_ref,
):
    me, odd, _ = place()
    nodes = nodes_ref[...]
    node_count, width = nodes.shape
    coarse_count = members_ref.shape[1]
    member_count = members_ref.shape[0]
    total = ndom * coarse_count

    coarse = jnp.concatenate(ordered(mine_ref, theirs_ref, odd, 0, coarse_count), 0)
    parent_all = jnp.concatenate(
        ordered(mine_ref, theirs_ref, odd, coarse_count, coarse_count), 0
    )
    link_rows = link_ref.shape[0]
    gathered = jnp.zeros(link_ref.shape, F32)
    for chip in range(mine_ref.shape[0]):
        for ref in (mine_ref, theirs_ref):
            gathered = gathered + ref[
                chip, 2 * coarse_count : 2 * coarse_count + link_rows, :
            ].astype(F32)
    link_ref[...] = gathered
    pieces = -(-edge_count2 // width)
    ends2 = []
    for end in range(2):
        rows = []
        for piece in range(pieces):
            top = end * pieces + piece
            bottom = (2 + end) * pieces + piece
            code = 256.0 * link_ref[top : top + 1, :] + link_ref[bottom : bottom + 1, :]
            spot = lax.broadcasted_iota(jnp.int32, code.shape, 1) + piece * width
            rows.append(jnp.where(spot < edge_count2, code.astype(jnp.int32), -1))
        ends2.append(rows)
    src2 = dot(coarse, coarse_weights_ref[0]).astype(BF16)
    dst2 = dot(coarse, coarse_weights_ref[1]).astype(BF16)
    grad_agg2 = dot_nt(parent_all, coarse_weights_ref[2])
    grad_agg2_near = grad_agg2.astype(BF16)
    bias = biases_ref[1:2, :]
    for piece in range(pieces):
        span = slice(piece * width, (piece + 1) * width)
        from_nodes = one_hot_cols(to_column(ends2[0][piece]), total)
        to_nodes = one_hot_cols(to_column(ends2[1][piece]), total)
        pre = dot(from_nodes, src2) + dot(to_nodes, dst2) + bias
        message, slope = silu_and_slope(pre)
        message2_ref[span, :] = message.astype(BF16)
        slope2_ref[span, :] = slope.astype(BF16)
        edge2_ref[span, :] = (dot(to_nodes, grad_agg2_near) * slope).astype(BF16)
    into = jnp.concatenate([one_hot_rows(row, total) for row in ends2[1]], 1)
    coarse_sum = dot(into, message2_ref[...]).astype(BF16)
    grad_dst2 = dot(into, slope2_ref[...]) * grad_agg2
    back = jnp.concatenate([one_hot_rows(row, total) for row in ends2[0]], 1)
    grad_src2 = dot(back, edge2_ref[...])
    bias2_ref[...] = jnp.sum(grad_dst2, 0, keepdims=True)
    grad_src2 = grad_src2.astype(BF16)
    grad_dst2 = grad_dst2.astype(BF16)
    coarse_grads_ref[0] = dot_tn(coarse, grad_src2)
    coarse_grads_ref[1] = dot_tn(coarse, grad_dst2)
    coarse_grads_ref[2] = dot_tn(coarse_sum, parent_all)

    own_ref[0] = coarse
    own_ref[1] = parent_all
    own_ref[2] = coarse_sum
    own_ref[3] = grad_src2
    own_ref[4] = grad_dst2
    rows = pl.ds(pl.multiple_of(me * coarse_count, coarse_count), coarse_count)
    coarse_new = own_ref[0, rows, :].astype(F32) + dot(own_ref[2, rows, :], coarse_weights_ref[2])
    coarse_grad = (
        own_ref[1, rows, :].astype(F32)
        + dot_nt(own_ref[3, rows, :], coarse_weights_ref[0])
        + dot_nt(own_ref[4, rows, :], coarse_weights_ref[1])
    )
    family = one_hot_rows(parents_ref[...], coarse_count)
    high, low = split(coarse_new)
    moved_ref[...] = updated_ref[...] + dot_tn(family, high) + dot_tn(family, low)
    share = membership(members_ref[...], node_count)
    high, low = split(coarse_grad / member_count)
    grad_updated = cotangent_ref[...].astype(F32) + dot(share, high) + dot(share, low)

    extended = extend(nodes, near_ref[...], far_ref[...], odd)
    rim = near_ref.shape[0]
    slots = ends_ref.shape[1]
    grad_updated_near = grad_updated.astype(BF16)
    grad_summed = dot_nt(grad_updated_near, weights_ref[2])
    grad_summed_near = grad_summed.astype(BF16)
    grad_dst = slopes_sum_ref[...] * grad_summed
    chunk = 2 * EDGE_BLOCK
    for start in range(0, slots, chunk):
        receivers = to_column(ends_ref[1:2, start : start + chunk])
        slope = slopes_ref[start : start + chunk, :].astype(F32)
        edge = dot(one_hot_cols(receivers, node_count), grad_summed_near) * slope
        edge_ref[start : start + chunk, :] = edge.astype(BF16)
    back = one_hot_rows(live_rows(ends_ref, live_ref, 0), extended.shape[0])
    grad_src = dot(back, edge_ref[...]).astype(BF16)
    bias1 = jnp.sum(grad_dst, 0, keepdims=True)
    grad_dst = grad_dst.astype(BF16)
    both = jnp.concatenate([grad_src[rim : rim + node_count], grad_dst], 1)
    node_part_ref[...] = grad_updated + dot_nt(
        both, jnp.concatenate([weights_ref[0], weights_ref[1]], 1)
    )
    low = dot_nt(grad_src[:rim], weights_ref[0]).astype(BF16)
    high = dot_nt(grad_src[rim + node_count :], weights_ref[0]).astype(BF16)
    grads_ref[0:width, :] = dot_tn(extended, grad_src).astype(BF16)
    grads_ref[width : 2 * width, :] = dot_tn(nodes, grad_dst).astype(BF16)
    grads_ref[2 * width : 3 * width, :] = dot_tn(summed_ref[...], grad_updated_near).astype(BF16)
    if grads_ref.shape[0] > 3 * width:
        grads_ref[3 * width :, :] = jnp.zeros((grads_ref.shape[0] - 3 * width, width), BF16)
    half = grads_ref.shape[0] // 2
    keep_ref[:half, :] = grads_ref[pl.ds(pl.multiple_of(odd * half, ROW_TILE), half), :]
    send_ref[:half, :] = grads_ref[pl.ds(pl.multiple_of((1 - odd) * half, ROW_TILE), half), :]
    bias_rows = two_rows(bias1)
    keep_ref[half : half + ROW_TILE, :] = bias_rows
    send_ref[half : half + ROW_TILE, :] = bias_rows
    base = half + ROW_TILE
    send_ref[base : base + rim, :] = jnp.where(odd == 1, low, high)
    send_ref[base + rim : base + 2 * rim, :] = jnp.where(odd == 1, high, low)


def two_rows(value):
    high = value.astype(BF16).astype(F32)
    row = lax.broadcasted_iota(jnp.int32, (ROW_TILE, value.shape[1]), 0)
    return jnp.where(row == 0, high, jnp.where(row == 1, value - high, 0.0)).astype(BF16)


def pair_kernel(keep_ref, came_ref, blocks_ref):
    half = keep_ref.shape[0] - ROW_TILE
    chips, depth, _ = blocks_ref.shape
    rim = came_ref.shape[0] - half - ROW_TILE
    rim = rim // 2
    rows = half // chips
    bias = keep_ref[half:, :].astype(F32) + came_ref[half : half + ROW_TILE, :].astype(F32)
    bias = two_rows(jnp.sum(bias, 0, keepdims=True))
    far = came_ref[half + ROW_TILE + rim :, :]
    for chip in range(chips):
        span = slice(chip * rows, (chip + 1) * rows)
        blocks_ref[chip, :rows, :] = (
            keep_ref[span, :].astype(F32) + came_ref[span, :].astype(F32)
        ).astype(BF16)
        blocks_ref[chip, rows : rows + ROW_TILE, :] = bias
        blocks_ref[chip, rows + ROW_TILE :, :] = far


def sum_kernel(
    blocks_ref, came_ref, node_part_ref, lists_ref, bias2_ref, part_ref, node_grads_ref, bias_ref
):
    _, odd, chip = place()
    chips, rows, _ = part_ref.shape
    rim = lists_ref.shape[1]
    half = chips * rows
    total = blocks_ref[0, : rows + ROW_TILE, :].astype(F32)
    for other in range(1, chips):
        total = total + blocks_ref[other, : rows + ROW_TILE, :].astype(F32)
    part = total[:rows].astype(BF16)
    for other in range(chips):
        part_ref[other] = part
    bias_ref[0:1, :] = jnp.sum(total[rows:], 0, keepdims=True)
    bias_ref[1:2, :] = bias2_ref[...]
    lists = lists_ref[...]
    near_list = jnp.where(odd == 1, lists[0:1], lists[1:2])
    far_list = jnp.where(odd == 1, lists[1:2], lists[0:1])
    origin = jnp.where(odd == 1, chip + 1, chip - 1)
    inside = jnp.logical_and(origin >= 0, origin < chips)
    far_list = jnp.where(inside, far_list, -1)
    origin = jnp.clip(origin, 0, chips - 1)
    near = came_ref[half + ROW_TILE : half + ROW_TILE + rim, :]
    far = blocks_ref[origin, rows + ROW_TILE : rows + ROW_TILE + rim, :]
    node_count = node_part_ref.shape[0]
    node_grads_ref[...] = (
        node_part_ref[...]
        + dot(one_hot_rows(near_list, node_count), near)
        + dot(one_hot_rows(far_list, node_count), far)
    )


def join_kernel(mine_ref, theirs_ref, out_ref):
    _, odd, _ = place()
    chips, rows, _ = mine_ref.shape
    limit = out_ref.shape[0]
    for side in range(2):
        for chip in range(chips):
            start = (side * chips + chip) * rows
            count = min(rows, limit - start)
            if count <= 0:
                continue
            mine = mine_ref[chip, :count, :]
            theirs = theirs_ref[chip, :count, :]
            out_ref[start : start + count, :] = jnp.where(odd == side, mine, theirs).astype(F32)


def call(kernel, outs, args, room, scratch=(), scalars=()):
    whole = pl.BlockSpec(memory_space=pltpu.VMEM)
    scalar = pl.BlockSpec(memory_space=pltpu.SMEM)
    return pl.pallas_call(
        kernel,
        out_shape=[jax.ShapeDtypeStruct(shape, kind) for shape, kind in outs],
        in_specs=[scalar if spot in scalars else whole for spot in range(len(args))],
        out_specs=[whole] * len(outs),
        scratch_shapes=[pltpu.VMEM(shape, kind) for shape, kind in scratch],
        compiler_params=pltpu.CompilerParams(vmem_limit_bytes=room * MIB),
    )(*args)


def round_up(value, unit):
    return -(-value // unit) * unit


def shards(
    nodes,
    cotangent,
    fine_weights,
    coarse_weights,
    biases,
    send_lists,
    edge_ends,
    live_blocks,
    pool_members,
    parents,
    coarse_ends,
):
    ndom = lax.axis_size("dom")
    chips = ndom // 2
    node_count, width = nodes.shape
    rim = send_lists.shape[1]
    coarse_count = pool_members.shape[1]
    slots = edge_ends.shape[1]
    edge_count2 = coarse_ends.shape[1] * ndom
    total = coarse_count * ndom
    parents = parents.reshape(1, node_count)
    pairs = [(i, i ^ 1) for i in range(ndom)]
    across = [(i, i + 1) for i in range(1, ndom - 1, 2)]
    across = across + [(target, source) for source, target in across]
    same_core = [[2 * chip + core for chip in range(chips)] for core in range(2)]

    def swap(value):
        return lax.ppermute(value, "dom", pairs)

    def exchange(value):
        return lax.all_to_all(value, "dom", 0, 0, axis_index_groups=same_core)

    near, far = call(
        pick_kernel, [((rim, width), BF16), ((rim, width), BF16)], (nodes, send_lists), 2
    )
    far = lax.ppermute(far, "dom", across)
    near = swap(near)

    pieces = -(-edge_count2 // width)
    link_rows = round_up(4 * pieces, ROW_TILE)
    packet_rows = 2 * coarse_count + link_rows
    updated, summed, slopes_sum, slopes, packet = call(
        functools.partial(forward_kernel, ndom),
        [
            ((node_count, width), F32),
            ((node_count, width), BF16),
            ((node_count, width), F32),
            ((slots, width), BF16),
            ((chips, packet_rows, width), BF16),
        ],
        (
            nodes,
            near,
            far,
            fine_weights,
            biases,
            edge_ends,
            live_blocks,
            pool_members,
            parents,
            cotangent,
            coarse_ends,
        ),
        16,
        scratch=[((slots, width), BF16), ((link_rows, width), F32)],
        scalars=(6,),
    )
    mine = exchange(packet)
    theirs = swap(mine)

    rows = round_up(-(-3 * width // ndom), ROW_TILE)
    half = rows * chips
    edges2 = pieces * width
    moved, node_part, coarse_grads, bias2, send, keep = call(
        functools.partial(backward_kernel, ndom, edge_count2),
        [
            ((node_count, width), F32),
            ((node_count, width), F32),
            ((3, width, width), F32),
            ((1, width), F32),
            ((half + ROW_TILE + 2 * rim, width), BF16),
            ((half + ROW_TILE, width), BF16),
        ],
        (
            mine,
            theirs,
            coarse_weights,
            biases,
            nodes,
            near,
            far,
            fine_weights,
            edge_ends,
            live_blocks,
            pool_members,
            parents,
            cotangent,
            updated,
            summed,
            slopes_sum,
            slopes,
        ),
        20 if total <= 256 else 56,
        scratch=[
            ((link_rows, width), F32),
            ((edges2, width), BF16),
            ((edges2, width), BF16),
            ((edges2, width), BF16),
            ((5, total, width), BF16),
            ((2 * half, width), BF16),
            ((slots, width), BF16),
        ],
        scalars=(9,),
    )
    came = swap(send)
    (blocks,) = call(
        pair_kernel, [((chips, rows + ROW_TILE + rim, width), BF16)], (keep, came), 4
    )
    blocks = exchange(blocks)
    part, node_grads, bias_grads = call(
        sum_kernel,
        [
            ((chips, rows, width), BF16),
            ((node_count, width), F32),
            ((2, width), F32),
        ],
        (blocks, came, node_part, send_lists, bias2),
        4,
    )
    mine = exchange(part)
    theirs = swap(mine)
    (fine_grads,) = call(join_kernel, [((3 * width, width), F32)], (mine, theirs), 4)
    return moved, node_grads, fine_grads.reshape(3, width, width), coarse_grads, bias_grads


def solution(mesh):
    return jax.shard_map(
        shards,
        mesh=mesh,
        in_specs=(
            P(("groups", "dom"), None),
            P(("groups", "dom"), None),
            P(),
            P(),
            P(),
            P("groups", "dom"),
            P("groups", "dom"),
            P(("groups", "dom")),
            P("groups", "dom"),
            P(("groups", "dom")),
            P("groups", "dom"),
        ),
        out_specs=(
            P(("groups", "dom"), None),
            P(("groups", "dom"), None),
            P("groups", None, None),
            P("groups", None, None),
            P("groups", None),
        ),
        check_vma=False,
    )
```

```python
import functools
import math

import jax
import jax.numpy as jnp
from jax import lax
from jax.experimental import pallas as pl
from jax.experimental.pallas import tpu as pltpu
from jax.sharding import PartitionSpec as P

BF16 = jnp.bfloat16
F32 = jnp.float32
EDGE_BLOCK = 128
ROW_TILE = 16
MIB = 1024 * 1024


def dot(left, right):
    return jnp.dot(left, right, preferred_element_type=F32)


def dot_tn(left, right):
    return lax.dot_general(left, right, (((0,), (0,)), ((), ())), preferred_element_type=F32)


def dot_nt(left, right):
    return lax.dot_general(left, right, (((1,), (1,)), ((), ())), preferred_element_type=F32)


def split(value):
    high = value.astype(BF16)
    return high, (value - high.astype(F32)).astype(BF16)


def one_hot_rows(index_row, count):
    spots = lax.broadcasted_iota(jnp.int32, (count, index_row.shape[1]), 0)
    return jnp.where(spots == index_row, 1.0, 0.0).astype(BF16)


def one_hot_cols(index_col, count):
    spots = lax.broadcasted_iota(jnp.int32, (index_col.shape[0], count), 1)
    return jnp.where(spots == index_col, 1.0, 0.0).astype(BF16)


def to_column(index_row):
    return jnp.transpose(jnp.broadcast_to(index_row, (8, index_row.shape[1])))[:, :1]


def silu_and_slope(value):
    sig = 0.5 * jnp.tanh(0.5 * value) + 0.5
    message = value * sig
    return message, sig + message * (1.0 - sig)


def membership(members, node_count):
    spots = lax.broadcasted_iota(jnp.int32, (node_count, members.shape[1]), 0)
    total = jnp.zeros(spots.shape, F32)
    for row in range(members.shape[0]):
        total = total + jnp.where(spots == members[row : row + 1], 1.0, 0.0)
    return total.astype(BF16)


def place():
    me = lax.axis_index("dom")
    return me, lax.rem(me, 2), lax.div(me, 2)


def live_rows(ends_ref, live_ref, row):
    index = ends_ref[row : row + 1, :]
    slot = lax.broadcasted_iota(jnp.int32, index.shape, 1)
    return jnp.where(slot < live_ref[0] * EDGE_BLOCK, index, -1)


def pick_kernel(nodes_ref, lists_ref, near_ref, far_ref, nodes_out, lists_out, sems):
    copies = (
        pltpu.make_async_copy(nodes_ref, nodes_out, sems.at[0]),
        pltpu.make_async_copy(lists_ref, lists_out, sems.at[1]),
    )
    for copy in copies:
        copy.start()
    for copy in copies:
        copy.wait()
    _, odd, _ = place()
    lists = lists_out[...]
    near = jnp.where(odd == 1, lists[0:1], lists[1:2])
    far = jnp.where(odd == 1, lists[1:2], lists[0:1])
    nodes = nodes_out[...]
    near_ref[...] = dot_tn(one_hot_rows(near, nodes.shape[0]), nodes).astype(BF16)
    far_ref[...] = dot_tn(one_hot_rows(far, nodes.shape[0]), nodes).astype(BF16)


def rims(near, far, odd):
    return jnp.where(odd == 1, near, far), jnp.where(odd == 1, far, near)


def prepare_kernel(
    ndom,
    rim,
    nodes_ref,
    weights_hbm,
    biases_hbm,
    ends_hbm,
    live_ref,
    members_hbm,
    parents_hbm,
    cotangent_hbm,
    links_hbm,
    weights_ref,
    ends_ref,
    cotangent_ref,
    pre_ref,
    rim_hot_ref,
    to_nodes_ref,
    into_ref,
    share_ref,
    family_ref,
    side_ref,
    biases_ref,
    members_ref,
    parents_ref,
    links_ref,
    link_ref,
    sems,
):
    pairs = (
        (ends_hbm, ends_ref),
        (weights_hbm, weights_ref),
        (biases_hbm, biases_ref),
        (members_hbm, members_ref),
        (parents_hbm, parents_ref),
        (cotangent_hbm, cotangent_ref),
        (links_hbm, links_ref),
    )
    copies = [
        pltpu.make_async_copy(source, target, sems.at[spot])
        for spot, (source, target) in enumerate(pairs)
    ]
    for copy in copies:
        copy.start()
    for copy in copies:
        copy.wait()
    me, _, _ = place()
    nodes = nodes_ref[...]
    node_count, width = nodes.shape
    coarse_count = family_ref.shape[0]
    slots = ends_ref.shape[1]
    src_proj = dot(nodes, weights_ref[0]).astype(BF16)
    dst_proj = dot(nodes, weights_ref[1]).astype(BF16)
    bias = biases_ref[0:1, :]
    chunk = 2 * EDGE_BLOCK
    for start in range(0, slots, chunk):
        span = slice(start, start + chunk)
        senders = to_column(ends_ref[0:1, span])
        receivers = to_column(ends_ref[1:2, span])
        to_nodes = one_hot_cols(receivers, node_count)
        to_nodes_ref[span, :] = to_nodes
        inner = one_hot_cols(senders - rim, node_count)
        spot = jnp.where(
            senders < rim, senders, jnp.where(senders < rim + node_count, -1, senders - node_count)
        )
        rim_hot_ref[span, :] = one_hot_cols(spot, 2 * rim)
        pre_ref[span, :] = dot(inner, src_proj) + dot(to_nodes, dst_proj) + bias
    into_ref[...] = one_hot_rows(live_rows(ends_ref, live_ref, 1), node_count)
    share_ref[...] = membership(members_ref[...], node_count)
    family = one_hot_rows(parents_ref[...], coarse_count)
    family_ref[...] = family
    side_ref[:coarse_count, :] = dot(family, cotangent_ref[...]).astype(BF16)

    links = links_ref[...]
    own = links.shape[1]
    pieces = -(-own * ndom // width)
    spot = lax.broadcasted_iota(jnp.int32, (own, pieces * width), 1)
    source = lax.broadcasted_iota(jnp.int32, (own, pieces * width), 0)
    spread = jnp.where(spot == source + me * own, 1.0, 0.0).astype(BF16)
    coded = (
        dot((links >> 8).astype(F32).astype(BF16), spread),
        dot((links & 255).astype(F32).astype(BF16), spread),
    )
    link_ref[...] = jnp.zeros(link_ref.shape, F32)
    for part in range(2):
        for end in range(2):
            for piece in range(pieces):
                row = (part * 2 + end) * pieces + piece
                link_ref[row : row + 1, :] = coded[part][
                    end : end + 1, piece * width : (piece + 1) * width
                ]
    side_ref[coarse_count:, :] = link_ref[...].astype(BF16)


def forward_kernel(
    member_count,
    nodes_ref,
    near_ref,
    far_ref,
    weights_ref,
    pre_ref,
    rim_hot_ref,
    into_ref,
    share_ref,
    side_ref,
    updated_ref,
    summed_ref,
    slopes_ref,
    packet_ref,
    message_ref,
):
    _, odd, _ = place()
    nodes = nodes_ref[...]
    low, high = rims(near_ref[...], far_ref[...], odd)
    rim_proj = dot(jnp.concatenate([low, high], 0), weights_ref[0]).astype(BF16)
    slots = pre_ref.shape[0]
    chunk = 2 * EDGE_BLOCK
    for start in range(0, slots, chunk):
        span = slice(start, start + chunk)
        pre = pre_ref[span, :] + dot(rim_hot_ref[span, :], rim_proj)
        message, slope = silu_and_slope(pre)
        message_ref[span, :] = message.astype(BF16)
        slopes_ref[span, :] = slope.astype(BF16)
    summed = dot(into_ref[...], message_ref[...]).astype(BF16)
    summed_ref[...] = summed
    updated = nodes.astype(F32) + dot(summed, weights_ref[2])
    updated_ref[...] = updated
    share = share_ref[...]
    high, low = split(updated)
    pooled = dot_tn(share, high) + dot_tn(share, low)
    coarse = (pooled / member_count).astype(BF16)
    coarse_count = coarse.shape[0]
    side = side_ref[...]
    for chip in range(packet_ref.shape[0]):
        packet_ref[chip, :coarse_count, :] = coarse
        packet_ref[chip, coarse_count:, :] = side


def between_kernel(into_ref, slopes_ref, ends_ref, live_ref, slopes_sum_ref, back_ref):
    slopes_sum_ref[...] = dot(into_ref[...], slopes_ref[...])
    back_ref[...] = one_hot_rows(live_rows(ends_ref, live_ref, 0), back_ref.shape[0])


def ordered(mine_ref, theirs_ref, odd, start, count):
    blocks = []
    for chip in range(mine_ref.shape[0]):
        mine = mine_ref[chip, start : start + count, :]
        theirs = theirs_ref[chip, start : start + count, :]
        blocks.append(jnp.where(odd == 1, theirs, mine))
        blocks.append(jnp.where(odd == 1, mine, theirs))
    return blocks


def backward_kernel(
    ndom,
    edge_count2,
    member_count,
    mine_ref,
    theirs_ref,
    coarse_weights_ref,
    biases_ref,
    nodes_ref,
    near_ref,
    far_ref,
    weights_ref,
    share_ref,
    cotangent_ref,
    summed_ref,
    slopes_sum_ref,
    slopes_ref,
    to_nodes_ref,
    back_ref,
    send_ref,
    keep_ref,
    far_grad_ref,
    coarse_ref,
    parent_ref,
    coarse_sum_ref,
    grad_src2_ref,
    grad_dst2_ref,
    bias2_ref,
    grad_updated_ref,
    grad_src_ref,
    grad_dst_ref,
    link_ref,
    message2_ref,
    slope2_ref,
    edge2_ref,
    grads_ref,
    edge_ref,
):
    me, odd, _ = place()
    nodes = nodes_ref[...]
    node_count, width = nodes.shape
    coarse_count = share_ref.shape[1]
    total = ndom * coarse_count

    coarse = jnp.concatenate(ordered(mine_ref, theirs_ref, odd, 0, coarse_count), 0)
    parent_all = jnp.concatenate(
        ordered(mine_ref, theirs_ref, odd, coarse_count, coarse_count), 0
    )
    link_rows = link_ref.shape[0]
    gathered = jnp.zeros(link_ref.shape, F32)
    for chip in range(mine_ref.shape[0]):
        for ref in (mine_ref, theirs_ref):
            gathered = gathered + ref[
                chip, 2 * coarse_count : 2 * coarse_count + link_rows, :
            ].astype(F32)
    link_ref[...] = gathered
    pieces = -(-edge_count2 // width)
    ends2 = []
    for end in range(2):
        rows = []
        for piece in range(pieces):
            top = end * pieces + piece
            bottom = (2 + end) * pieces + piece
            code = 256.0 * link_ref[top : top + 1, :] + link_ref[bottom : bottom + 1, :]
            spot = lax.broadcasted_iota(jnp.int32, code.shape, 1) + piece * width
            rows.append(jnp.where(spot < edge_count2, code.astype(jnp.int32), -1))
        ends2.append(rows)
    src2 = dot(coarse, coarse_weights_ref[0]).astype(BF16)
    dst2 = dot(coarse, coarse_weights_ref[1]).astype(BF16)
    grad_agg2 = dot_nt(parent_all, coarse_weights_ref[2])
    grad_agg2_near = grad_agg2.astype(BF16)
    bias = biases_ref[1:2, :]
    for piece in range(pieces):
        span = slice(piece * width, (piece + 1) * width)
        from_nodes = one_hot_cols(to_column(ends2[0][piece]), total)
        to_nodes = one_hot_cols(to_column(ends2[1][piece]), total)
        pre = dot(from_nodes, src2) + dot(to_nodes, dst2) + bias
        message, slope = silu_and_slope(pre)
        message2_ref[span, :] = message.astype(BF16)
        slope2_ref[span, :] = slope.astype(BF16)
        edge2_ref[span, :] = (dot(to_nodes, grad_agg2_near) * slope).astype(BF16)
    into = jnp.concatenate([one_hot_rows(row, total) for row in ends2[1]], 1)
    coarse_sum_ref[...] = dot(into, message2_ref[...]).astype(BF16)
    grad_dst2 = dot(into, slope2_ref[...]) * grad_agg2
    back = jnp.concatenate([one_hot_rows(row, total) for row in ends2[0]], 1)
    grad_src2 = dot(back, edge2_ref[...])
    bias2_ref[...] = jnp.sum(grad_dst2, 0, keepdims=True)
    grad_src2_ref[...] = grad_src2.astype(BF16)
    grad_dst2_ref[...] = grad_dst2.astype(BF16)
    coarse_ref[...] = coarse
    parent_ref[...] = parent_all

    rows = pl.ds(pl.multiple_of(me * coarse_count, coarse_count), coarse_count)
    coarse_grad = (
        parent_ref[rows, :].astype(F32)
        + dot_nt(grad_src2_ref[rows, :], coarse_weights_ref[0])
        + dot_nt(grad_dst2_ref[rows, :], coarse_weights_ref[1])
    )
    share = share_ref[...]
    high, low = split(coarse_grad / member_count)
    grad_updated = cotangent_ref[...].astype(F32) + dot(share, high) + dot(share, low)
    grad_updated_ref[...] = grad_updated

    low, high = rims(near_ref[...], far_ref[...], odd)
    extended = jnp.concatenate([low, nodes, high], 0)
    rim = low.shape[0]
    slots = slopes_ref.shape[0]
    grad_updated_near = grad_updated.astype(BF16)
    grad_summed = dot_nt(grad_updated_near, weights_ref[2])
    grad_summed_near = grad_summed.astype(BF16)
    grad_dst = slopes_sum_ref[...] * grad_summed
    chunk = 2 * EDGE_BLOCK
    for start in range(0, slots, chunk):
        span = slice(start, start + chunk)
        slope = slopes_ref[span, :].astype(F32)
        edge_ref[span, :] = (dot(to_nodes_ref[span, :], grad_summed_near) * slope).astype(BF16)
    grad_src = dot(back_ref[...], edge_ref[...]).astype(BF16)
    bias1 = jnp.sum(grad_dst, 0, keepdims=True)
    grad_dst = grad_dst.astype(BF16)
    grad_src_ref[...] = grad_src
    grad_dst_ref[...] = grad_dst
    low = dot_nt(grad_src[:rim], weights_ref[0]).astype(BF16)
    high = dot_nt(grad_src[rim + node_count :], weights_ref[0]).astype(BF16)
    grads_ref[0:width, :] = dot_tn(extended, grad_src).astype(BF16)
    grads_ref[width : 2 * width, :] = dot_tn(nodes, grad_dst).astype(BF16)
    grads_ref[2 * width : 3 * width, :] = dot_tn(summed_ref[...], grad_updated_near).astype(BF16)
    if grads_ref.shape[0] > 3 * width:
        grads_ref[3 * width :, :] = jnp.zeros((grads_ref.shape[0] - 3 * width, width), BF16)
    half = grads_ref.shape[0] // 2
    keep_ref[:half, :] = grads_ref[pl.ds(pl.multiple_of(odd * half, ROW_TILE), half), :]
    send_ref[:half, :] = grads_ref[pl.ds(pl.multiple_of((1 - odd) * half, ROW_TILE), half), :]
    bias_rows = two_rows(bias1, ROW_TILE)
    keep_ref[half : half + ROW_TILE, :] = bias_rows
    send_ref[half : half + ROW_TILE, :] = bias_rows
    send_ref[half + ROW_TILE :, :] = jnp.where(odd == 1, low, high)
    far_grad_ref[...] = jnp.where(odd == 1, high, low)


def two_rows(value, count):
    high = value.astype(BF16).astype(F32)
    row = lax.broadcasted_iota(jnp.int32, (count, value.shape[1]), 0)
    return jnp.where(row == 0, high, jnp.where(row == 1, value - high, 0.0)).astype(BF16)


def pair_kernel(keep_ref, came_ref, blocks_ref):
    half = keep_ref.shape[0] - ROW_TILE
    chips, depth, _ = blocks_ref.shape
    rows = half // chips
    bias = keep_ref[half:, :].astype(F32) + came_ref[half : half + ROW_TILE, :].astype(F32)
    bias = two_rows(jnp.sum(bias, 0, keepdims=True), depth - rows)
    for chip in range(chips):
        span = slice(chip * rows, (chip + 1) * rows)
        blocks_ref[chip, :rows, :] = (
            keep_ref[span, :].astype(F32) + came_ref[span, :].astype(F32)
        ).astype(BF16)
        blocks_ref[chip, rows:, :] = bias


def coarse_kernel(
    coarse_weights_ref,
    weights_ref,
    coarse_ref,
    parent_ref,
    coarse_sum_ref,
    grad_src2_ref,
    grad_dst2_ref,
    updated_ref,
    family_ref,
    grad_updated_ref,
    grad_src_ref,
    grad_dst_ref,
    lists_ref,
    came_ref,
    moved_ref,
    coarse_grads_ref,
    node_part_ref,
):
    me, odd, _ = place()
    node_count = updated_ref.shape[0]
    coarse_count = family_ref.shape[0]
    rim = lists_ref.shape[1]
    rows = pl.ds(pl.multiple_of(me * coarse_count, coarse_count), coarse_count)
    coarse_new = coarse_ref[rows, :].astype(F32) + dot(
        coarse_sum_ref[rows, :], coarse_weights_ref[2]
    )
    family = family_ref[...]
    high, low = split(coarse_new)
    moved_ref[...] = updated_ref[...] + dot_tn(family, high) + dot_tn(family, low)
    coarse = coarse_ref[...]
    coarse_grads_ref[0] = dot_tn(coarse, grad_src2_ref[...])
    coarse_grads_ref[1] = dot_tn(coarse, grad_dst2_ref[...])
    coarse_grads_ref[2] = dot_tn(coarse_sum_ref[...], parent_ref[...])
    lists = lists_ref[...]
    near_list = jnp.where(odd == 1, lists[0:1], lists[1:2])
    near = came_ref[came_ref.shape[0] - rim :, :]
    both = jnp.concatenate([grad_src_ref[rim : rim + node_count, :], grad_dst_ref[...]], 1)
    node_part_ref[...] = grad_updated_ref[...] + dot_nt(
        both, jnp.concatenate([weights_ref[0], weights_ref[1]], 1)
    )
    node_part_ref[...] += dot(one_hot_rows(near_list, node_count), near)


def sum_kernel(blocks_ref, node_part_ref, far_grad_ref, part_ref, bias1_ref):
    chips, rows, _ = part_ref.shape
    total = blocks_ref[0].astype(F32)
    for other in range(1, chips):
        total = total + blocks_ref[other].astype(F32)
    part = total[:rows].astype(BF16)
    for other in range(chips):
        part_ref[other] = part
    bias1_ref[...] = jnp.sum(total[rows:], 0, keepdims=True)


def finish_kernel(
    node_part_ref, far_grad_ref, lists_ref, bias1_ref, bias2_ref, node_grads_ref, bias_ref
):
    _, odd, _ = place()
    lists = lists_ref[...]
    far_list = jnp.where(odd == 1, lists[1:2], lists[0:1])
    node_count = node_part_ref.shape[0]
    node_grads_ref[...] = node_part_ref[...] + dot(
        one_hot_rows(far_list, node_count), far_grad_ref[...]
    )
    bias_ref[0:1, :] = bias1_ref[...]
    bias_ref[1:2, :] = bias2_ref[...]


def join_kernel(mine_ref, theirs_ref, out_ref):
    _, odd, _ = place()
    chips, rows, _ = mine_ref.shape
    limit = out_ref.shape[0]
    for side in range(2):
        for chip in range(chips):
            start = (side * chips + chip) * rows
            count = min(rows, limit - start)
            if count <= 0:
                continue
            mine = mine_ref[chip, :count, :]
            theirs = theirs_ref[chip, :count, :]
            out_ref[start : start + count, :] = jnp.where(odd == side, mine, theirs).astype(F32)


def call(kernel, outs, args, room, scratch=(), scalars=(), outside=(), copies=0, flops=0):
    vmem = pl.BlockSpec(memory_space=pltpu.VMEM)
    scalar = pl.BlockSpec(memory_space=pltpu.SMEM)
    hbm = pl.BlockSpec(memory_space=pltpu.HBM)
    specs = [
        scalar if spot in scalars else hbm if spot in outside else vmem for spot in range(len(args))
    ]
    args = [
        pltpu.with_memory_space_constraint(value, pltpu.HBM) if spot in outside else value
        for spot, value in enumerate(args)
    ]
    moved = sum(value.size * value.dtype.itemsize for value in args)
    moved += sum(math.prod(shape) * jnp.dtype(kind).itemsize for shape, kind in outs)
    scratch = [pltpu.VMEM(shape, kind) for shape, kind in scratch]
    if copies:
        scratch.append(pltpu.SemaphoreType.DMA((copies,)))
    return pl.pallas_call(
        kernel,
        out_shape=[jax.ShapeDtypeStruct(shape, kind) for shape, kind in outs],
        in_specs=specs,
        out_specs=[vmem] * len(outs),
        scratch_shapes=scratch,
        compiler_params=pltpu.CompilerParams(vmem_limit_bytes=room * MIB),
        cost_estimate=pl.CostEstimate(flops=flops, bytes_accessed=moved, transcendentals=0),
    )(*args)


def round_up(value, unit):
    return -(-value // unit) * unit


def shards(
    nodes,
    cotangent,
    fine_weights,
    coarse_weights,
    biases,
    send_lists,
    edge_ends,
    live_blocks,
    pool_members,
    parents,
    coarse_ends,
):
    ndom = lax.axis_size("dom")
    chips = ndom // 2
    node_count, width = nodes.shape
    rim = send_lists.shape[1]
    member_count, coarse_count = pool_members.shape
    slots = edge_ends.shape[1]
    edge_count2 = coarse_ends.shape[1] * ndom
    total = coarse_count * ndom
    parents = parents.reshape(1, node_count)
    pairs = [(i, i ^ 1) for i in range(ndom)]
    across = [(i, i + 1) for i in range(1, ndom - 1, 2)]
    across = across + [(target, source) for source, target in across]
    same_core = [[2 * chip + core for chip in range(chips)] for core in range(2)]

    def swap(value):
        return lax.ppermute(value, "dom", pairs)

    def exchange(value):
        return lax.all_to_all(value, "dom", 0, 0, axis_index_groups=same_core)

    rim_rows = ((rim, width), BF16)
    square = ((width, width), BF16)
    near, far, nodes, lists = call(
        pick_kernel,
        [rim_rows, rim_rows, (nodes.shape, BF16), (send_lists.shape, jnp.int32)],
        (nodes, send_lists),
        2,
        outside=(0, 1),
        copies=2,
    )
    far = lax.ppermute(far, "dom", across)
    near = swap(near)

    pieces = -(-edge_count2 // width)
    link_rows = round_up(4 * pieces, ROW_TILE)
    side_rows = coarse_count + link_rows
    fine, ends, upstream, pre, rim_hot, to_nodes, into, share, family, side = call(
        functools.partial(prepare_kernel, ndom, rim),
        [
            (fine_weights.shape, BF16),
            (edge_ends.shape, jnp.int32),
            (cotangent.shape, BF16),
            ((slots, width), F32),
            ((slots, 2 * rim), BF16),
            ((slots, node_count), BF16),
            ((node_count, slots), BF16),
            ((node_count, coarse_count), BF16),
            ((coarse_count, node_count), BF16),
            ((side_rows, width), BF16),
        ],
        (
            nodes,
            fine_weights,
            biases,
            edge_ends,
            live_blocks,
            pool_members,
            parents,
            cotangent,
            coarse_ends,
        ),
        10,
        scratch=[
            (biases.shape, F32),
            (pool_members.shape, jnp.int32),
            (parents.shape, jnp.int32),
            (coarse_ends.shape, jnp.int32),
            ((link_rows, width), F32),
        ],
        scalars=(4,),
        outside=(1, 2, 3, 5, 6, 7, 8),
        copies=7,
        flops=2 * slots * width * (2 * node_count + 2 * rim),
    )
    updated, summed, slopes, packet = call(
        functools.partial(forward_kernel, member_count),
        [
            ((node_count, width), F32),
            ((node_count, width), BF16),
            ((slots, width), BF16),
            ((chips, coarse_count + side_rows, width), BF16),
        ],
        (nodes, near, far, fine, pre, rim_hot, into, share, side),
        10,
        scratch=[((slots, width), BF16)],
    )
    mine = exchange(packet)
    slopes_sum, back = call(
        between_kernel,
        [((node_count, width), F32), ((node_count + 2 * rim, slots), BF16)],
        (into, slopes, ends, live_blocks),
        8,
        scalars=(3,),
        flops=2 * slots * width * node_count,
    )
    theirs = swap(mine)

    rows = round_up(-(-3 * width // ndom), ROW_TILE)
    half = rows * chips
    edges2 = pieces * width
    coarse_whole = ((total, width), BF16)
    (
        send,
        keep,
        far_grad,
        coarse,
        parent_all,
        coarse_sum,
        grad_src2,
        grad_dst2,
        bias2,
        grad_updated,
        grad_src,
        grad_dst,
    ) = call(
        functools.partial(backward_kernel, ndom, edge_count2, member_count),
        [
            ((half + ROW_TILE + rim, width), BF16),
            ((half + ROW_TILE, width), BF16),
            rim_rows,
            coarse_whole,
            coarse_whole,
            coarse_whole,
            coarse_whole,
            coarse_whole,
            ((1, width), F32),
            ((node_count, width), F32),
            ((node_count + 2 * rim, width), BF16),
            ((node_count, width), BF16),
        ],
        (
            mine,
            theirs,
            coarse_weights,
            biases,
            nodes,
            near,
            far,
            fine,
            share,
            upstream,
            summed,
            slopes_sum,
            slopes,
            to_nodes,
            back,
        ),
        20 if total <= 256 else 48,
        scratch=[
            ((link_rows, width), F32),
            ((edges2, width), BF16),
            ((edges2, width), BF16),
            ((edges2, width), BF16),
            ((2 * half, width), BF16),
            ((slots, width), BF16),
        ],
    )
    came = swap(send)
    (blocks,) = call(pair_kernel, [((chips, rows + 8, width), BF16)], (keep, came), 4)
    blocks = exchange(blocks)
    far_grad = lax.ppermute(far_grad, "dom", across)
    moved, coarse_grads, node_part = call(
        coarse_kernel,
        [
            ((node_count, width), F32),
            ((3, width, width), F32),
            ((node_count, width), F32),
        ],
        (
            coarse_weights,
            fine,
            coarse,
            parent_all,
            coarse_sum,
            grad_src2,
            grad_dst2,
            updated,
            family,
            grad_updated,
            grad_src,
            grad_dst,
            lists,
            came,
        ),
        8,
        flops=6 * total * width * width,
    )
    part, bias1 = call(
        sum_kernel,
        [((chips, rows, width), BF16), ((1, width), F32)],
        (blocks, node_part, far_grad),
        4,
    )
    mine = exchange(part)
    node_grads, bias_grads = call(
        finish_kernel,
        [((node_count, width), F32), ((2, width), F32)],
        (node_part, far_grad, lists, bias1, bias2),
        4,
    )
    theirs = swap(mine)
    (fine_grads,) = call(join_kernel, [((3 * width, width), F32)], (mine, theirs), 4)
    return moved, node_grads, fine_grads.reshape(3, width, width), coarse_grads, bias_grads


def solution(mesh):
    return jax.shard_map(
        shards,
        mesh=mesh,
        in_specs=(
            P(("groups", "dom"), None),
            P(("groups", "dom"), None),
            P(),
            P(),
            P(),
            P("groups", "dom"),
            P("groups", "dom"),
            P(("groups", "dom")),
            P("groups", "dom"),
            P(("groups", "dom")),
            P("groups", "dom"),
        ),
        out_specs=(
            P(("groups", "dom"), None),
            P(("groups", "dom"), None),
            P("groups", None, None),
            P("groups", None, None),
            P("groups", None),
        ),
        check_vma=False,
    )
```

```python
import functools
import math

import jax
import jax.numpy as jnp
from jax import lax
from jax.experimental import pallas as pl
from jax.experimental.pallas import tpu as pltpu
from jax.sharding import PartitionSpec as P

BF16 = jnp.bfloat16
F32 = jnp.float32
EDGE_BLOCK = 128
ROW_TILE = 16
MIB = 1024 * 1024


def dot(left, right):
    return jnp.dot(left, right, preferred_element_type=F32)


def dot_tn(left, right):
    return lax.dot_general(left, right, (((0,), (0,)), ((), ())), preferred_element_type=F32)


def dot_nt(left, right):
    return lax.dot_general(left, right, (((1,), (1,)), ((), ())), preferred_element_type=F32)


def split(value):
    high = value.astype(BF16)
    return high, (value - high.astype(F32)).astype(BF16)


def one_hot_rows(index_row, count):
    spots = lax.broadcasted_iota(jnp.int32, (count, index_row.shape[1]), 0)
    return jnp.where(spots == index_row, 1.0, 0.0).astype(BF16)


def column(row, lanes):
    upright = jnp.transpose(jnp.broadcast_to(row, (8, row.shape[1])))[:, :1]
    return jnp.broadcast_to(upright, (row.shape[1], lanes))


def silu_and_slope(value):
    sig = 0.5 * jnp.tanh(0.5 * value) + 0.5
    message = value * sig
    return message, sig + message * (1.0 - sig)


def membership(members, node_count):
    spots = lax.broadcasted_iota(jnp.int32, (node_count, members.shape[1]), 0)
    total = jnp.zeros(spots.shape, F32)
    for row in range(members.shape[0]):
        total = total + jnp.where(spots == members[row : row + 1], 1.0, 0.0)
    return total.astype(BF16)


def place():
    me = lax.axis_index("dom")
    return me, lax.rem(me, 2), lax.div(me, 2)


def live_rows(ends_ref, live_ref, row):
    index = ends_ref[row : row + 1, :]
    slot = lax.broadcasted_iota(jnp.int32, index.shape, 1)
    return jnp.where(slot < live_ref[0] * EDGE_BLOCK, index, -1)


def pick_kernel(*refs):
    count = (len(refs) - 3) // 2
    inputs, (near_ref, far_ref), outputs = refs[:count], refs[count : count + 2], refs[count + 2 : -1]
    copies = [
        pltpu.make_async_copy(source, target, refs[-1].at[spot])
        for spot, (source, target) in enumerate(zip(inputs, outputs, strict=True))
    ]
    for copy in copies:
        copy.start()
    for copy in copies[:2]:
        copy.wait()
    _, odd, _ = place()
    lists = outputs[1][...]
    near = jnp.where(odd == 1, lists[0:1], lists[1:2])
    far = jnp.where(odd == 1, lists[1:2], lists[0:1])
    nodes = outputs[0][...]
    rim = near_ref.shape[0]
    near = dot_tn(one_hot_rows(near, nodes.shape[0]), nodes).astype(BF16)
    near_ref[...] = near
    far = dot_tn(one_hot_rows(far, nodes.shape[0]), nodes).astype(BF16)
    for start in range(0, far_ref.shape[0], rim):
        far_ref[start : start + rim, :] = far
    for copy in copies[2:]:
        copy.wait()


def rims(near_ref, far_ref, odd):
    near = near_ref[...]
    far = far_ref[: near.shape[0], :]
    return jnp.where(odd == 1, near, far), jnp.where(odd == 1, far, near)


def prepare_kernel(
    ndom,
    rim,
    nodes_ref,
    weights_ref,
    biases_ref,
    ends_ref,
    live_ref,
    members_ref,
    parents_ref,
    cotangent_ref,
    links_ref,
    pre_ref,
    outof_ref,
    into_ref,
    share_ref,
    family_ref,
    side_ref,
    upright_ref,
    pooled_ref,
    link_ref,
):
    me, _, _ = place()
    node_count, width = nodes_ref.shape
    coarse_count = family_ref.shape[0]
    slots = ends_ref.shape[1]
    lanes = link_ref.shape[1]
    outof_ref[...] = one_hot_rows(live_rows(ends_ref, live_ref, 0), node_count + 2 * rim)
    into_ref[...] = one_hot_rows(live_rows(ends_ref, live_ref, 1), node_count)
    nodes = nodes_ref[...]
    src_proj = jnp.transpose(dot(nodes, weights_ref[0])).astype(BF16)
    dst_proj = jnp.transpose(dot(nodes, weights_ref[1])).astype(BF16)
    chunk = 2 * EDGE_BLOCK
    bias = column(biases_ref[0:1, :], chunk)
    for start in range(0, slots, chunk):
        span = slice(start, start + chunk)
        pre_ref[:, span] = (
            dot(src_proj, outof_ref[rim : rim + node_count, span])
            + dot(dst_proj, into_ref[:, span])
            + bias
        )
    upright_ref[...] = jnp.transpose(weights_ref[0].astype(F32)).astype(BF16)
    share = membership(members_ref[...], node_count)
    share_ref[...] = share
    pooled_ref[...] = dot_tn(share, nodes)
    family = one_hot_rows(parents_ref[...], coarse_count)
    family_ref[...] = family
    parent_grad = dot(family, cotangent_ref[...]).astype(BF16)
    side_ref[:coarse_count, :] = parent_grad[:, :lanes]
    side_ref[coarse_count : 2 * coarse_count, :] = parent_grad[:, lanes:]

    links = links_ref[...]
    own = links.shape[1]
    pieces = -(-own * ndom // lanes)
    spot = lax.broadcasted_iota(jnp.int32, (own, pieces * lanes), 1)
    source = lax.broadcasted_iota(jnp.int32, (own, pieces * lanes), 0)
    spread = jnp.where(spot == source + me * own, 1.0, 0.0).astype(BF16)
    coded = (
        dot((links >> 8).astype(F32).astype(BF16), spread),
        dot((links & 255).astype(F32).astype(BF16), spread),
    )
    link_ref[...] = jnp.zeros(link_ref.shape, F32)
    for part in range(2):
        for end in range(2):
            for piece in range(pieces):
                row = (part * 2 + end) * pieces + piece
                link_ref[row : row + 1, :] = coded[part][
                    end : end + 1, piece * lanes : (piece + 1) * lanes
                ]
    side_ref[2 * coarse_count :, :] = link_ref[...].astype(BF16)


def forward_kernel(
    member_count,
    near_ref,
    far_ref,
    upright_ref,
    weights_ref,
    pre_ref,
    outof_ref,
    into_ref,
    share_ref,
    pooled_ref,
    side_ref,
    summed_ref,
    slopes_ref,
    packet_ref,
    message_ref,
):
    _, odd, _ = place()
    low, high = rims(near_ref, far_ref, odd)
    rim = low.shape[0]
    node_count = into_ref.shape[0]
    rim_proj = dot_nt(upright_ref[...], jnp.concatenate([low, high], 0)).astype(BF16)
    slots = pre_ref.shape[1]
    chunk = 2 * EDGE_BLOCK
    for start in range(0, slots, chunk):
        span = slice(start, start + chunk)
        at_rim = jnp.concatenate([outof_ref[:rim, span], outof_ref[rim + node_count :, span]], 0)
        message, slope = silu_and_slope(pre_ref[:, span] + dot(rim_proj, at_rim))
        message_ref[:, span] = message.astype(BF16)
        slopes_ref[:, span] = slope.astype(BF16)
    summed = dot_nt(into_ref[...], message_ref[...]).astype(BF16)
    summed_ref[...] = summed
    high, low = split(dot_tn(share_ref[...], summed))
    pooled = pooled_ref[...] + dot(high, weights_ref[2]) + dot(low, weights_ref[2])
    coarse = (pooled / member_count).astype(BF16)
    count = coarse.shape[0]
    lanes = packet_ref.shape[2]
    side = side_ref[...]
    for chip in range(packet_ref.shape[0]):
        packet_ref[chip, :count, :] = coarse[:, :lanes]
        packet_ref[chip, count : 2 * count, :] = coarse[:, lanes:]
        packet_ref[chip, 2 * count :, :] = side


def between_kernel(
    into_ref,
    slopes_ref,
    nodes_ref,
    summed_ref,
    weights_ref,
    coarse_weights_ref,
    slopes_sum_ref,
    updated_ref,
    upright2_ref,
):
    for spot in range(2):
        upright2_ref[spot] = jnp.transpose(coarse_weights_ref[spot].astype(F32)).astype(BF16)
    slopes_sum_ref[...] = dot_nt(into_ref[...], slopes_ref[...])
    updated_ref[...] = nodes_ref[...].astype(F32) + dot(summed_ref[...], weights_ref[2])


def ordered(mine_ref, theirs_ref, odd, start, count):
    blocks = []
    for chip in range(mine_ref.shape[0]):
        halves = []
        for half in range(2):
            span = slice(start + half * count, start + (half + 1) * count)
            mine = mine_ref[chip, span, :]
            theirs = theirs_ref[chip, span, :]
            halves.append((jnp.where(odd == 1, theirs, mine), jnp.where(odd == 1, mine, theirs)))
        for core in range(2):
            blocks.append(jnp.concatenate([halves[0][core], halves[1][core]], 1))
    return jnp.concatenate(blocks, 0)


def backward_kernel(
    ndom,
    edge_count2,
    member_count,
    mine_ref,
    theirs_ref,
    coarse_weights_ref,
    upright2_ref,
    biases_ref,
    nodes_ref,
    near_ref,
    far_ref,
    weights_ref,
    share_ref,
    cotangent_ref,
    summed_ref,
    slopes_sum_ref,
    slopes_ref,
    outof_ref,
    into_ref,
    send_ref,
    keep_ref,
    far_grad_ref,
    coarse_ref,
    parent_ref,
    into2_ref,
    message2_ref,
    grad_src2_ref,
    grad_dst2_ref,
    bias2_ref,
    grad_updated_ref,
    grad_src_ref,
    grad_dst_ref,
    link_ref,
    slope2_ref,
    edge2_ref,
    outof2_ref,
    grads_ref,
):
    me, odd, _ = place()
    nodes = nodes_ref[...]
    node_count, width = nodes.shape
    coarse_count = share_ref.shape[1]
    total = ndom * coarse_count

    coarse = ordered(mine_ref, theirs_ref, odd, 0, coarse_count)
    parent_all = ordered(mine_ref, theirs_ref, odd, 2 * coarse_count, coarse_count)
    link_rows, lanes = link_ref.shape
    gathered = jnp.zeros(link_ref.shape, F32)
    for chip in range(mine_ref.shape[0]):
        for ref in (mine_ref, theirs_ref):
            gathered = gathered + ref[chip, 4 * coarse_count :, :].astype(F32)
    link_ref[...] = gathered
    pieces = -(-edge_count2 // lanes)
    ends2 = []
    for end in range(2):
        rows = []
        for piece in range(pieces):
            top = end * pieces + piece
            bottom = (2 + end) * pieces + piece
            code = 256.0 * link_ref[top : top + 1, :] + link_ref[bottom : bottom + 1, :]
            spot = lax.broadcasted_iota(jnp.int32, code.shape, 1) + piece * lanes
            rows.append(jnp.where(spot < edge_count2, code.astype(jnp.int32), -1))
        ends2.append(rows)
    src2 = dot_nt(upright2_ref[0], coarse).astype(BF16)
    dst2 = dot_nt(upright2_ref[1], coarse).astype(BF16)
    grad_agg2 = dot_nt(parent_all, coarse_weights_ref[2])
    grad_agg2_near = dot_nt(coarse_weights_ref[2], parent_all).astype(BF16)
    bias = column(biases_ref[1:2, :], width)
    step = 2 * lanes
    for start in range(0, message2_ref.shape[1], step):
        span = slice(start, start + step)
        first = start // lanes
        outof, into = (
            one_hot_rows(jnp.concatenate(rows[first : first + 2], 1), total) for rows in ends2
        )
        outof2_ref[:, span] = outof
        into2_ref[:, span] = into
        message, slope = silu_and_slope(dot(src2, outof) + dot(dst2, into) + bias)
        message2_ref[:, span] = message.astype(BF16)
        slope2_ref[:, span] = slope.astype(BF16)
        edge2_ref[:, span] = (dot(grad_agg2_near, into) * slope).astype(BF16)
    grad_dst2 = dot_nt(into2_ref[...], slope2_ref[...]) * grad_agg2
    grad_src2 = dot_nt(outof2_ref[...], edge2_ref[...])
    bias2_ref[...] = jnp.sum(grad_dst2, 0, keepdims=True)
    grad_src2_ref[...] = grad_src2.astype(BF16)
    grad_dst2_ref[...] = grad_dst2.astype(BF16)
    coarse_ref[...] = coarse
    parent_ref[...] = parent_all

    rows = pl.ds(pl.multiple_of(me * coarse_count, coarse_count), coarse_count)
    coarse_grad = (
        parent_ref[rows, :].astype(F32)
        + dot_nt(grad_src2_ref[rows, :], coarse_weights_ref[0])
        + dot_nt(grad_dst2_ref[rows, :], coarse_weights_ref[1])
    )
    share = share_ref[...]
    high, low = split(coarse_grad / member_count)
    grad_updated = cotangent_ref[...].astype(F32) + dot(share, high) + dot(share, low)
    grad_updated_ref[...] = grad_updated

    low, high = rims(near_ref, far_ref, odd)
    extended = jnp.concatenate([low, nodes, high], 0)
    rim = low.shape[0]
    slots = slopes_ref.shape[1]
    grad_updated_near = grad_updated.astype(BF16)
    grad_dst = slopes_sum_ref[...] * dot_nt(grad_updated_near, weights_ref[2])
    grad_summed = dot_nt(weights_ref[2], grad_updated_near).astype(BF16)
    chunk = 2 * EDGE_BLOCK
    grad_src = jnp.zeros((outof_ref.shape[0], width), F32)
    for start in range(0, slots, chunk):
        span = slice(start, start + chunk)
        slope = slopes_ref[:, span].astype(F32)
        edge = (dot(grad_summed, into_ref[:, span]) * slope).astype(BF16)
        grad_src = grad_src + dot_nt(outof_ref[:, span], edge)
    grad_src = grad_src.astype(BF16)
    bias1 = jnp.sum(grad_dst, 0, keepdims=True)
    grad_dst = grad_dst.astype(BF16)
    grad_src_ref[...] = grad_src
    grad_dst_ref[...] = grad_dst
    low = dot_nt(grad_src[:rim], weights_ref[0]).astype(BF16)
    high = dot_nt(grad_src[rim + node_count :], weights_ref[0]).astype(BF16)
    grads_ref[0:width, :] = dot_tn(extended, grad_src).astype(BF16)
    grads_ref[width : 2 * width, :] = dot_tn(nodes, grad_dst).astype(BF16)
    grads_ref[2 * width : 3 * width, :] = dot_tn(summed_ref[...], grad_updated_near).astype(BF16)
    if grads_ref.shape[0] > 3 * width:
        grads_ref[3 * width :, :] = jnp.zeros((grads_ref.shape[0] - 3 * width, width), BF16)
    half = grads_ref.shape[0] // 2
    keep_ref[:half, :] = grads_ref[pl.ds(pl.multiple_of(odd * half, ROW_TILE), half), :]
    send_ref[:half, :] = grads_ref[pl.ds(pl.multiple_of((1 - odd) * half, ROW_TILE), half), :]
    bias_rows = two_rows(bias1, ROW_TILE)
    keep_ref[half : half + ROW_TILE, :] = bias_rows
    send_ref[half : half + ROW_TILE, :] = bias_rows
    send_ref[half + ROW_TILE :, :] = jnp.where(odd == 1, low, high)
    far_grad_ref[...] = jnp.where(odd == 1, high, low)


def two_rows(value, count):
    high = value.astype(BF16).astype(F32)
    row = lax.broadcasted_iota(jnp.int32, (count, value.shape[1]), 0)
    return jnp.where(row == 0, high, jnp.where(row == 1, value - high, 0.0)).astype(BF16)


def pair_kernel(keep_ref, came_ref, blocks_ref):
    half = keep_ref.shape[0] - ROW_TILE
    chips, _, lanes = blocks_ref.shape
    rows = half // chips
    bias = keep_ref[half:, :].astype(F32) + came_ref[half : half + ROW_TILE, :].astype(F32)
    bias = jnp.sum(bias, 0, keepdims=True)
    row = lax.broadcasted_iota(jnp.int32, (8, lanes), 0)
    tail = jnp.zeros((8, lanes), F32)
    for side in range(2):
        value = bias[:, side * lanes : (side + 1) * lanes]
        high = value.astype(BF16).astype(F32)
        tail = jnp.where(row == 2 * side, high, jnp.where(row == 2 * side + 1, value - high, tail))
    tail = tail.astype(BF16)
    for chip in range(chips):
        span = slice(chip * rows, (chip + 1) * rows)
        total = (keep_ref[span, :].astype(F32) + came_ref[span, :].astype(F32)).astype(BF16)
        blocks_ref[chip, :rows, :] = total[:, :lanes]
        blocks_ref[chip, rows : 2 * rows, :] = total[:, lanes:]
        blocks_ref[chip, 2 * rows :, :] = tail


def coarse_kernel(
    coarse_weights_ref,
    weights_ref,
    coarse_ref,
    parent_ref,
    into2_ref,
    message2_ref,
    grad_src2_ref,
    grad_dst2_ref,
    updated_ref,
    family_ref,
    grad_updated_ref,
    grad_src_ref,
    grad_dst_ref,
    lists_ref,
    came_ref,
    moved_ref,
    coarse_grads_ref,
    node_part_ref,
    coarse_sum_ref,
):
    me, odd, _ = place()
    node_count = updated_ref.shape[0]
    coarse_count = family_ref.shape[0]
    rim = lists_ref.shape[1]
    rows = pl.ds(pl.multiple_of(me * coarse_count, coarse_count), coarse_count)
    coarse_sum_ref[...] = dot_nt(into2_ref[...], message2_ref[...]).astype(BF16)
    coarse_new = coarse_ref[rows, :].astype(F32) + dot(
        coarse_sum_ref[rows, :], coarse_weights_ref[2]
    )
    family = family_ref[...]
    high, low = split(coarse_new)
    moved_ref[...] = updated_ref[...] + dot_tn(family, high) + dot_tn(family, low)
    coarse = coarse_ref[...]
    coarse_grads_ref[0] = dot_tn(coarse, grad_src2_ref[...])
    coarse_grads_ref[1] = dot_tn(coarse, grad_dst2_ref[...])
    coarse_grads_ref[2] = dot_tn(coarse_sum_ref[...], parent_ref[...])
    lists = lists_ref[...]
    near_list = jnp.where(odd == 1, lists[0:1], lists[1:2])
    near = came_ref[came_ref.shape[0] - rim :, :]
    both = jnp.concatenate([grad_src_ref[rim : rim + node_count, :], grad_dst_ref[...]], 1)
    node_part_ref[...] = grad_updated_ref[...] + dot_nt(
        both, jnp.concatenate([weights_ref[0], weights_ref[1]], 1)
    )
    node_part_ref[...] += dot(one_hot_rows(near_list, node_count), near)


def sum_kernel(blocks_ref, node_part_ref, far_grad_ref, part_ref, bias1_ref):
    chips, rows, _ = part_ref.shape
    total = blocks_ref[0].astype(F32)
    for other in range(1, chips):
        total = total + blocks_ref[other].astype(F32)
    part = jnp.concatenate([total[:rows], total[rows : 2 * rows]], 1).astype(BF16)
    for other in range(chips):
        part_ref[other] = part
    lanes = total.shape[1]
    for side in range(2):
        row = 2 * rows + 2 * side
        bias1_ref[:, side * lanes : (side + 1) * lanes] = jnp.sum(
            total[row : row + 2], 0, keepdims=True
        )


def finish_kernel(
    node_part_ref, far_grad_ref, lists_ref, bias1_ref, bias2_ref, node_grads_ref, bias_ref
):
    _, odd, _ = place()
    lists = lists_ref[...]
    far_list = jnp.where(odd == 1, lists[1:2], lists[0:1])
    node_count = node_part_ref.shape[0]
    node_grads_ref[...] = node_part_ref[...] + dot(
        one_hot_rows(far_list, node_count), far_grad_ref[...]
    )
    bias_ref[0:1, :] = bias1_ref[...]
    bias_ref[1:2, :] = bias2_ref[...]


def join_kernel(mine_ref, theirs_ref, out_ref):
    _, odd, _ = place()
    chips, rows, _ = mine_ref.shape
    limit = out_ref.shape[0]
    for side in range(2):
        for chip in range(chips):
            start = (side * chips + chip) * rows
            count = min(rows, limit - start)
            if count <= 0:
                continue
            mine = mine_ref[chip, :count, :]
            theirs = theirs_ref[chip, :count, :]
            out_ref[start : start + count, :] = jnp.where(odd == side, mine, theirs).astype(F32)


def call(kernel, outs, args, room, scratch=(), scalars=(), outside=(), copies=0, flops=0):
    vmem = pl.BlockSpec(memory_space=pltpu.VMEM)
    scalar = pl.BlockSpec(memory_space=pltpu.SMEM)
    hbm = pl.BlockSpec(memory_space=pltpu.HBM)
    specs = [
        scalar if spot in scalars else hbm if spot in outside else vmem for spot in range(len(args))
    ]
    args = [
        pltpu.with_memory_space_constraint(value, pltpu.HBM) if spot in outside else value
        for spot, value in enumerate(args)
    ]
    moved = sum(value.size * value.dtype.itemsize for value in args)
    moved += sum(math.prod(shape) * jnp.dtype(kind).itemsize for shape, kind in outs)
    scratch = [pltpu.VMEM(shape, kind) for shape, kind in scratch]
    if copies:
        scratch.append(pltpu.SemaphoreType.DMA((copies,)))
    return pl.pallas_call(
        kernel,
        out_shape=[jax.ShapeDtypeStruct(shape, kind) for shape, kind in outs],
        in_specs=specs,
        out_specs=[vmem] * len(outs),
        scratch_shapes=scratch,
        compiler_params=pltpu.CompilerParams(vmem_limit_bytes=room * MIB),
        cost_estimate=pl.CostEstimate(flops=flops, bytes_accessed=moved, transcendentals=0),
    )(*args)


def round_up(value, unit):
    return -(-value // unit) * unit


def shards(
    nodes,
    cotangent,
    fine_weights,
    coarse_weights,
    biases,
    send_lists,
    edge_ends,
    live_blocks,
    pool_members,
    parents,
    coarse_ends,
):
    ndom = lax.axis_size("dom")
    chips = ndom // 2
    node_count, width = nodes.shape
    rim = send_lists.shape[1]
    member_count, coarse_count = pool_members.shape
    slots = edge_ends.shape[1]
    edge_count2 = coarse_ends.shape[1] * ndom
    total = coarse_count * ndom
    parents = parents.reshape(1, node_count)
    pairs = [(i, i ^ 1) for i in range(ndom)]
    across = [(i, i + 1) for i in range(1, ndom - 1, 2)]
    across = across + [(target, source) for source, target in across]
    same_core = [[2 * chip + core for chip in range(chips)] for core in range(2)]

    def swap(value):
        return lax.ppermute(value, "dom", pairs)

    def exchange(value):
        return lax.all_to_all(value, "dom", 0, 0, axis_index_groups=same_core)

    rim_rows = ((rim, width), BF16)
    square = ((width, width), BF16)
    inputs = (
        nodes,
        send_lists,
        fine_weights,
        edge_ends,
        cotangent,
        biases,
        pool_members,
        parents,
        coarse_ends,
    )
    (
        near,
        far,
        nodes,
        lists,
        fine,
        edge_ends,
        upstream,
        own_biases,
        pool_members,
        parents,
        coarse_ends,
    ) = call(
        pick_kernel,
        [rim_rows, ((4 * rim, width), BF16)] + [(value.shape, value.dtype) for value in inputs],
        inputs,
        4,
        outside=range(len(inputs)),
        copies=len(inputs),
    )
    far = lax.ppermute(far, "dom", across)
    near = swap(near)

    lanes = width // 2
    pieces = round_up(-(-edge_count2 // lanes), 2)
    link_rows = round_up(4 * pieces, 8)
    side_rows = 2 * coarse_count + link_rows
    pre, outof, into, share, family, side, upright, pooled = call(
        functools.partial(prepare_kernel, ndom, rim),
        [
            ((width, slots), F32),
            ((node_count + 2 * rim, slots), BF16),
            ((node_count, slots), BF16),
            ((node_count, coarse_count), BF16),
            ((coarse_count, node_count), BF16),
            ((side_rows, lanes), BF16),
            square,
            ((coarse_count, width), F32),
        ],
        (
            nodes,
            fine,
            own_biases,
            edge_ends,
            live_blocks,
            pool_members,
            parents,
            upstream,
            coarse_ends,
        ),
        10,
        scratch=[((link_rows, lanes), F32)],
        scalars=(4,),
        flops=2 * slots * width * (2 * node_count + 2 * rim),
    )
    summed, slopes, packet = call(
        functools.partial(forward_kernel, member_count),
        [
            ((node_count, width), BF16),
            ((width, slots), BF16),
            ((chips, 2 * coarse_count + side_rows, lanes), BF16),
        ],
        (near, far, upright, fine, pre, outof, into, share, pooled, side),
        10,
        scratch=[((width, slots), BF16)],
    )
    mine = exchange(packet)
    slopes_sum, updated, upright2 = call(
        between_kernel,
        [((node_count, width), F32), ((node_count, width), F32), ((2, width, width), BF16)],
        (into, slopes, nodes, summed, fine, coarse_weights),
        8,
        flops=2 * slots * width * node_count,
    )
    theirs = swap(mine)

    rows = round_up(-(-3 * width // ndom), ROW_TILE)
    half = rows * chips
    edges2 = pieces * lanes
    coarse_whole = ((total, width), BF16)
    (
        send,
        keep,
        far_grad,
        coarse,
        parent_all,
        into2,
        message2,
        grad_src2,
        grad_dst2,
        bias2,
        grad_updated,
        grad_src,
        grad_dst,
    ) = call(
        functools.partial(backward_kernel, ndom, edge_count2, member_count),
        [
            ((half + ROW_TILE + rim, width), BF16),
            ((half + ROW_TILE, width), BF16),
            rim_rows,
            coarse_whole,
            coarse_whole,
            ((total, edges2), BF16),
            ((width, edges2), BF16),
            coarse_whole,
            coarse_whole,
            ((1, width), F32),
            ((node_count, width), F32),
            ((node_count + 2 * rim, width), BF16),
            ((node_count, width), BF16),
        ],
        (
            mine,
            theirs,
            coarse_weights,
            upright2,
            own_biases,
            nodes,
            near,
            far,
            fine,
            share,
            upstream,
            summed,
            slopes_sum,
            slopes,
            outof,
            into,
        ),
        20 if total <= 256 else 48,
        scratch=[
            ((link_rows, lanes), F32),
            ((width, edges2), BF16),
            ((width, edges2), BF16),
            ((total, edges2), BF16),
            ((2 * half, width), BF16),
        ],
    )
    came = swap(send)
    (blocks,) = call(pair_kernel, [((chips, 2 * rows + 8, lanes), BF16)], (keep, came), 4)
    blocks = exchange(blocks)
    far_grad = lax.ppermute(far_grad, "dom", across)
    moved, coarse_grads, node_part = call(
        coarse_kernel,
        [
            ((node_count, width), F32),
            ((3, width, width), F32),
            ((node_count, width), F32),
        ],
        (
            coarse_weights,
            fine,
            coarse,
            parent_all,
            into2,
            message2,
            grad_src2,
            grad_dst2,
            updated,
            family,
            grad_updated,
            grad_src,
            grad_dst,
            lists,
            came,
        ),
        8 if total <= 256 else 24,
        scratch=[coarse_whole],
        flops=6 * total * width * width,
    )
    part, bias1 = call(
        sum_kernel,
        [((chips, rows, width), BF16), ((1, width), F32)],
        (blocks, node_part, far_grad),
        4,
    )
    mine = exchange(part)
    node_grads, bias_grads = call(
        finish_kernel,
        [((node_count, width), F32), ((2, width), F32)],
        (node_part, far_grad, lists, bias1, bias2),
        4,
    )
    theirs = swap(mine)
    (fine_grads,) = call(join_kernel, [((3 * width, width), F32)], (mine, theirs), 4)
    return moved, node_grads, fine_grads.reshape(3, width, width), coarse_grads, bias_grads


def solution(mesh):
    return jax.shard_map(
        shards,
        mesh=mesh,
        in_specs=(
            P(("groups", "dom"), None),
            P(("groups", "dom"), None),
            P(),
            P(),
            P(),
            P("groups", "dom"),
            P("groups", "dom"),
            P(("groups", "dom")),
            P("groups", "dom"),
            P(("groups", "dom")),
            P("groups", "dom"),
        ),
        out_specs=(
            P(("groups", "dom"), None),
            P(("groups", "dom"), None),
            P("groups", None, None),
            P("groups", None, None),
            P("groups", None),
        ),
        check_vma=False,
    )
```

```python
import functools
import math

import jax
import jax.numpy as jnp
from jax import lax
from jax.experimental import pallas as pl
from jax.experimental.pallas import tpu as pltpu
from jax.sharding import PartitionSpec as P

BF16 = jnp.bfloat16
F32 = jnp.float32
EDGE_BLOCK = 128
ROW_TILE = 16
MIB = 1024 * 1024


def dot(left, right):
    return jnp.dot(left, right, preferred_element_type=F32)


def dot_tn(left, right):
    return lax.dot_general(left, right, (((0,), (0,)), ((), ())), preferred_element_type=F32)


def dot_nt(left, right):
    return lax.dot_general(left, right, (((1,), (1,)), ((), ())), preferred_element_type=F32)


def split(value):
    high = value.astype(BF16)
    return high, (value - high.astype(F32)).astype(BF16)


def one_hot_rows(index_row, count):
    spots = lax.broadcasted_iota(jnp.int32, (count, index_row.shape[1]), 0)
    return jnp.where(spots == index_row, 1.0, 0.0).astype(BF16)


def column(row, lanes):
    upright = jnp.transpose(jnp.broadcast_to(row, (8, row.shape[1])))[:, :1]
    return jnp.broadcast_to(upright, (row.shape[1], lanes))


def silu_and_slope(value):
    sig = 0.5 * jnp.tanh(0.5 * value) + 0.5
    message = value * sig
    return message, sig + message * (1.0 - sig)


def membership(members, node_count):
    spots = lax.broadcasted_iota(jnp.int32, (node_count, members.shape[1]), 0)
    total = jnp.zeros(spots.shape, F32)
    for row in range(members.shape[0]):
        total = total + jnp.where(spots == members[row : row + 1], 1.0, 0.0)
    return total.astype(BF16)


def place():
    me = lax.axis_index("dom")
    return me, lax.rem(me, 2), lax.div(me, 2)


def live_rows(ends_ref, live_ref, row):
    index = ends_ref[row : row + 1, :]
    slot = lax.broadcasted_iota(jnp.int32, index.shape, 1)
    return jnp.where(slot < live_ref[0] * EDGE_BLOCK, index, -1)


def pick_kernel(*refs):
    count = (len(refs) - 3) // 2
    inputs, (near_ref, far_ref), outputs = refs[:count], refs[count : count + 2], refs[count + 2 : -1]
    copies = [
        pltpu.make_async_copy(source, target, refs[-1].at[spot])
        for spot, (source, target) in enumerate(zip(inputs, outputs, strict=True))
    ]
    for copy in copies:
        copy.start()
    for copy in copies[:2]:
        copy.wait()
    _, odd, _ = place()
    lists = outputs[1][...]
    near = jnp.where(odd == 1, lists[0:1], lists[1:2])
    far = jnp.where(odd == 1, lists[1:2], lists[0:1])
    nodes = outputs[0][...]
    rim = near_ref.shape[0]
    near = dot_tn(one_hot_rows(near, nodes.shape[0]), nodes).astype(BF16)
    near_ref[...] = near
    far = dot_tn(one_hot_rows(far, nodes.shape[0]), nodes).astype(BF16)
    for start in range(0, far_ref.shape[0], rim):
        far_ref[start : start + rim, :] = far
    for copy in copies[2:]:
        copy.wait()


def rims(near_ref, far_ref, odd):
    near = near_ref[...]
    far = far_ref[: near.shape[0], :]
    return jnp.where(odd == 1, near, far), jnp.where(odd == 1, far, near)


def prepare_kernel(
    ndom,
    rim,
    nodes_ref,
    weights_ref,
    biases_ref,
    ends_ref,
    live_ref,
    members_ref,
    parents_ref,
    cotangent_ref,
    links_ref,
    pre_ref,
    outof_ref,
    into_ref,
    share_ref,
    family_ref,
    side_ref,
    upright_ref,
    pooled_ref,
    link_ref,
):
    me, _, _ = place()
    node_count, width = nodes_ref.shape
    coarse_count = family_ref.shape[0]
    slots = ends_ref.shape[1]
    lanes = link_ref.shape[1]
    outof_ref[...] = one_hot_rows(live_rows(ends_ref, live_ref, 0), node_count + 2 * rim)
    into_ref[...] = one_hot_rows(live_rows(ends_ref, live_ref, 1), node_count)
    nodes = nodes_ref[...]
    src_proj = jnp.transpose(dot(nodes, weights_ref[0])).astype(BF16)
    dst_proj = jnp.transpose(dot(nodes, weights_ref[1])).astype(BF16)
    chunk = 2 * EDGE_BLOCK
    bias = column(biases_ref[0:1, :], chunk)
    for start in range(0, slots, chunk):
        span = slice(start, start + chunk)
        pre_ref[:, span] = (
            dot(src_proj, outof_ref[rim : rim + node_count, span])
            + dot(dst_proj, into_ref[:, span])
            + bias
        )
    upright_ref[...] = jnp.transpose(weights_ref[0].astype(F32)).astype(BF16)
    share = membership(members_ref[...], node_count)
    share_ref[...] = share
    pooled_ref[...] = dot_tn(share, nodes)
    family = one_hot_rows(parents_ref[...], coarse_count)
    family_ref[...] = family
    parent_grad = dot(family, cotangent_ref[...]).astype(BF16)
    side_ref[:coarse_count, :] = parent_grad[:, :lanes]
    side_ref[coarse_count : 2 * coarse_count, :] = parent_grad[:, lanes:]

    links = links_ref[...]
    own = links.shape[1]
    pieces = -(-own * ndom // lanes)
    spot = lax.broadcasted_iota(jnp.int32, (own, pieces * lanes), 1)
    source = lax.broadcasted_iota(jnp.int32, (own, pieces * lanes), 0)
    spread = jnp.where(spot == source + me * own, 1.0, 0.0).astype(BF16)
    coded = (
        dot((links >> 8).astype(F32).astype(BF16), spread),
        dot((links & 255).astype(F32).astype(BF16), spread),
    )
    link_ref[...] = jnp.zeros(link_ref.shape, F32)
    for part in range(2):
        for end in range(2):
            for piece in range(pieces):
                row = (part * 2 + end) * pieces + piece
                link_ref[row : row + 1, :] = coded[part][
                    end : end + 1, piece * lanes : (piece + 1) * lanes
                ]
    side_ref[2 * coarse_count :, :] = link_ref[...].astype(BF16)


def forward_kernel(
    member_count,
    near_ref,
    far_ref,
    upright_ref,
    weights_ref,
    pre_ref,
    outof_ref,
    into_ref,
    share_ref,
    pooled_ref,
    side_ref,
    summed_ref,
    slopes_ref,
    packet_ref,
    message_ref,
):
    _, odd, _ = place()
    low, high = rims(near_ref, far_ref, odd)
    rim = low.shape[0]
    node_count = into_ref.shape[0]
    rim_proj = dot_nt(upright_ref[...], jnp.concatenate([low, high], 0)).astype(BF16)
    slots = pre_ref.shape[1]
    chunk = 2 * EDGE_BLOCK
    for start in range(0, slots, chunk):
        span = slice(start, start + chunk)
        at_rim = jnp.concatenate([outof_ref[:rim, span], outof_ref[rim + node_count :, span]], 0)
        message, slope = silu_and_slope(pre_ref[:, span] + dot(rim_proj, at_rim))
        message_ref[:, span] = message.astype(BF16)
        slopes_ref[:, span] = slope.astype(BF16)
    summed = dot_nt(into_ref[...], message_ref[...]).astype(BF16)
    summed_ref[...] = summed
    high, low = split(dot_tn(share_ref[...], summed))
    pooled = pooled_ref[...] + dot(high, weights_ref[2]) + dot(low, weights_ref[2])
    coarse = (pooled / member_count).astype(BF16)
    count = coarse.shape[0]
    lanes = packet_ref.shape[2]
    side = side_ref[...]
    for chip in range(packet_ref.shape[0]):
        packet_ref[chip, :count, :] = coarse[:, :lanes]
        packet_ref[chip, count : 2 * count, :] = coarse[:, lanes:]
        packet_ref[chip, 2 * count :, :] = side


def between_kernel(
    into_ref,
    slopes_ref,
    nodes_ref,
    summed_ref,
    weights_ref,
    coarse_weights_ref,
    slopes_sum_ref,
    updated_ref,
    upright2_ref,
):
    for spot in range(2):
        upright2_ref[spot] = jnp.transpose(coarse_weights_ref[spot].astype(F32)).astype(BF16)
    slopes_sum_ref[...] = dot_nt(into_ref[...], slopes_ref[...])
    updated_ref[...] = nodes_ref[...].astype(F32) + dot(summed_ref[...], weights_ref[2])


def ordered(mine_ref, theirs_ref, odd, start, count):
    blocks = []
    for chip in range(mine_ref.shape[0]):
        halves = []
        for half in range(2):
            span = slice(start + half * count, start + (half + 1) * count)
            mine = mine_ref[chip, span, :]
            theirs = theirs_ref[chip, span, :]
            halves.append((jnp.where(odd == 1, theirs, mine), jnp.where(odd == 1, mine, theirs)))
        for core in range(2):
            blocks.append(jnp.concatenate([halves[0][core], halves[1][core]], 1))
    return jnp.concatenate(blocks, 0)


def backward_kernel(
    ndom,
    edge_count2,
    member_count,
    mine_ref,
    theirs_ref,
    coarse_weights_ref,
    upright2_ref,
    biases_ref,
    nodes_ref,
    near_ref,
    far_ref,
    weights_ref,
    share_ref,
    cotangent_ref,
    summed_ref,
    slopes_sum_ref,
    slopes_ref,
    outof_ref,
    into_ref,
    send_ref,
    keep_ref,
    coarse_ref,
    parent_ref,
    into2_ref,
    message2_ref,
    grad_src2_ref,
    grad_dst2_ref,
    bias2_ref,
    grad_updated_ref,
    grad_src_ref,
    grad_dst_ref,
    link_ref,
    slope2_ref,
    edge2_ref,
    outof2_ref,
    grads_ref,
):
    me, odd, _ = place()
    nodes = nodes_ref[...]
    node_count, width = nodes.shape
    coarse_count = share_ref.shape[1]
    total = ndom * coarse_count

    coarse = ordered(mine_ref, theirs_ref, odd, 0, coarse_count)
    parent_all = ordered(mine_ref, theirs_ref, odd, 2 * coarse_count, coarse_count)
    link_rows, lanes = link_ref.shape
    gathered = jnp.zeros(link_ref.shape, F32)
    for chip in range(mine_ref.shape[0]):
        for ref in (mine_ref, theirs_ref):
            gathered = gathered + ref[chip, 4 * coarse_count :, :].astype(F32)
    link_ref[...] = gathered
    pieces = -(-edge_count2 // lanes)
    ends2 = []
    for end in range(2):
        rows = []
        for piece in range(pieces):
            top = end * pieces + piece
            bottom = (2 + end) * pieces + piece
            code = 256.0 * link_ref[top : top + 1, :] + link_ref[bottom : bottom + 1, :]
            spot = lax.broadcasted_iota(jnp.int32, code.shape, 1) + piece * lanes
            rows.append(jnp.where(spot < edge_count2, code.astype(jnp.int32), -1))
        ends2.append(rows)
    src2 = dot_nt(upright2_ref[0], coarse).astype(BF16)
    dst2 = dot_nt(upright2_ref[1], coarse).astype(BF16)
    grad_agg2 = dot_nt(parent_all, coarse_weights_ref[2])
    grad_agg2_near = dot_nt(coarse_weights_ref[2], parent_all).astype(BF16)
    bias = column(biases_ref[1:2, :], width)
    step = 2 * lanes
    for start in range(0, message2_ref.shape[1], step):
        span = slice(start, start + step)
        first = start // lanes
        outof, into = (
            one_hot_rows(jnp.concatenate(rows[first : first + 2], 1), total) for rows in ends2
        )
        outof2_ref[:, span] = outof
        into2_ref[:, span] = into
        message, slope = silu_and_slope(dot(src2, outof) + dot(dst2, into) + bias)
        message2_ref[:, span] = message.astype(BF16)
        slope2_ref[:, span] = slope.astype(BF16)
        edge2_ref[:, span] = (dot(grad_agg2_near, into) * slope).astype(BF16)
    grad_dst2 = dot_nt(into2_ref[...], slope2_ref[...]) * grad_agg2
    grad_src2 = dot_nt(outof2_ref[...], edge2_ref[...])
    bias2_ref[...] = jnp.sum(grad_dst2, 0, keepdims=True)
    grad_src2_ref[...] = grad_src2.astype(BF16)
    grad_dst2_ref[...] = grad_dst2.astype(BF16)
    coarse_ref[...] = coarse
    parent_ref[...] = parent_all

    rows = pl.ds(pl.multiple_of(me * coarse_count, coarse_count), coarse_count)
    coarse_grad = (
        parent_ref[rows, :].astype(F32)
        + dot_nt(grad_src2_ref[rows, :], coarse_weights_ref[0])
        + dot_nt(grad_dst2_ref[rows, :], coarse_weights_ref[1])
    )
    share = share_ref[...]
    high, low = split(coarse_grad / member_count)
    grad_updated = cotangent_ref[...].astype(F32) + dot(share, high) + dot(share, low)
    grad_updated_ref[...] = grad_updated

    low, high = rims(near_ref, far_ref, odd)
    extended = jnp.concatenate([low, nodes, high], 0)
    rim = low.shape[0]
    slots = slopes_ref.shape[1]
    grad_updated_near = grad_updated.astype(BF16)
    grad_dst = slopes_sum_ref[...] * dot_nt(grad_updated_near, weights_ref[2])
    grad_summed = dot_nt(weights_ref[2], grad_updated_near).astype(BF16)
    chunk = 2 * EDGE_BLOCK
    grad_src = jnp.zeros((outof_ref.shape[0], width), F32)
    for start in range(0, slots, chunk):
        span = slice(start, start + chunk)
        slope = slopes_ref[:, span].astype(F32)
        edge = (dot(grad_summed, into_ref[:, span]) * slope).astype(BF16)
        grad_src = grad_src + dot_nt(outof_ref[:, span], edge)
    grad_src = grad_src.astype(BF16)
    bias1 = jnp.sum(grad_dst, 0, keepdims=True)
    grad_dst = grad_dst.astype(BF16)
    grad_src_ref[...] = grad_src
    grad_dst_ref[...] = grad_dst
    low = dot_nt(grad_src[:rim], weights_ref[0]).astype(BF16)
    high = dot_nt(grad_src[rim + node_count :], weights_ref[0]).astype(BF16)
    grads_ref[0:width, :] = dot_tn(extended, grad_src).astype(BF16)
    grads_ref[width : 2 * width, :] = dot_tn(nodes, grad_dst).astype(BF16)
    grads_ref[2 * width : 3 * width, :] = dot_tn(summed_ref[...], grad_updated_near).astype(BF16)
    if grads_ref.shape[0] > 3 * width:
        grads_ref[3 * width :, :] = jnp.zeros((grads_ref.shape[0] - 3 * width, width), BF16)
    half = grads_ref.shape[0] // 2
    keep_ref[:half, :] = grads_ref[pl.ds(pl.multiple_of(odd * half, ROW_TILE), half), :]
    send_ref[:half, :] = grads_ref[pl.ds(pl.multiple_of((1 - odd) * half, ROW_TILE), half), :]
    bias_rows = two_rows(bias1, ROW_TILE)
    keep_ref[half : half + ROW_TILE, :] = bias_rows
    send_ref[half : half + ROW_TILE, :] = bias_rows
    base = half + ROW_TILE
    send_ref[base : base + rim, :] = jnp.where(odd == 1, low, high)
    send_ref[base + rim :, :] = jnp.where(odd == 1, high, low)


def two_rows(value, count):
    high = value.astype(BF16).astype(F32)
    row = lax.broadcasted_iota(jnp.int32, (count, value.shape[1]), 0)
    return jnp.where(row == 0, high, jnp.where(row == 1, value - high, 0.0)).astype(BF16)


def tail_spots(rows, chips, rim):
    share = -(-rim // chips)
    chip = rows >> (share.bit_length() - 1)
    return 8 * chip + 4 + rows - share * chip, share


def pair_kernel(keep_ref, came_ref, made_ref, blocks_ref):
    half = keep_ref.shape[0] - ROW_TILE
    chips, _, lanes = blocks_ref.shape
    rows = half // chips
    rim = (came_ref.shape[0] - half - ROW_TILE) // 2
    bias = keep_ref[half:, :].astype(F32) + came_ref[half : half + ROW_TILE, :].astype(F32)
    bias = jnp.sum(bias, 0, keepdims=True)
    far = came_ref[half + ROW_TILE + rim :, :]
    spot, share = tail_spots(lax.broadcasted_iota(jnp.int32, (8 * chips, rim), 1), chips, rim)
    row = lax.broadcasted_iota(jnp.int32, (8 * chips, rim), 0)
    line = lax.broadcasted_iota(jnp.int32, (8, lanes), 0)
    tails = jnp.zeros((8 * chips, lanes), F32)
    bias_tail = jnp.zeros((8, lanes), F32)
    for side in range(2):
        span = slice(side * lanes, (side + 1) * lanes)
        pick = jnp.where(row == spot + side * share, 1.0, 0.0).astype(BF16)
        tails = tails + dot(pick, far[:, span])
        value = bias[:, span]
        high = value.astype(BF16).astype(F32)
        bias_tail = jnp.where(line == 2 * side, high, bias_tail)
        bias_tail = jnp.where(line == 2 * side + 1, value - high, bias_tail)
    for chip in range(chips):
        span = slice(chip * rows, (chip + 1) * rows)
        total = (keep_ref[span, :].astype(F32) + came_ref[span, :].astype(F32)).astype(BF16)
        blocks_ref[chip, :rows, :] = total[:, :lanes]
        blocks_ref[chip, rows : 2 * rows, :] = total[:, lanes:]
        blocks_ref[chip, 2 * rows :, :] = (tails[8 * chip : 8 * chip + 8] + bias_tail).astype(BF16)


def sum_kernel(blocks_ref, part_ref, bias1_ref):
    _, odd, _ = place()
    chips, depth, lanes = blocks_ref.shape
    rows = depth - 8
    total = blocks_ref[0].astype(F32)
    for other in range(1, chips):
        total = total + blocks_ref[other].astype(F32)
    part = total[:rows].astype(BF16)
    for other in range(chips):
        after = blocks_ref[min(other + 1, chips - 1), rows:, :]
        before = blocks_ref[max(other - 1, 0), rows:, :]
        part_ref[other, :rows, :] = part
        part_ref[other, rows:, :] = jnp.where(odd == 1, after, before)
    for side in range(2):
        row = rows + 2 * side
        bias1_ref[:, side * lanes : (side + 1) * lanes] = jnp.sum(
            total[row : row + 2], 0, keepdims=True
        )


def coarse_kernel(
    coarse_ref,
    parent_ref,
    into2_ref,
    message2_ref,
    grad_src2_ref,
    grad_dst2_ref,
    coarse_grads_ref,
    coarse_sum_ref,
):
    coarse = coarse_ref[...]
    coarse_sum = dot_nt(into2_ref[...], message2_ref[...]).astype(BF16)
    coarse_sum_ref[...] = coarse_sum
    coarse_grads_ref[0] = dot_tn(coarse, grad_src2_ref[...])
    coarse_grads_ref[1] = dot_tn(coarse, grad_dst2_ref[...])
    coarse_grads_ref[2] = dot_tn(coarse_sum, parent_ref[...])


def finish_kernel(
    coarse_weights_ref,
    weights_ref,
    coarse_ref,
    coarse_sum_ref,
    updated_ref,
    family_ref,
    grad_updated_ref,
    grad_src_ref,
    grad_dst_ref,
    lists_ref,
    came_ref,
    mine_ref,
    bias1_ref,
    bias2_ref,
    moved_ref,
    node_grads_ref,
    bias_ref,
):
    me, odd, chip = place()
    node_count = updated_ref.shape[0]
    coarse_count = family_ref.shape[0]
    chips, depth, lanes = mine_ref.shape
    rim = lists_ref.shape[1]
    rows = pl.ds(pl.multiple_of(me * coarse_count, coarse_count), coarse_count)
    coarse_new = coarse_ref[rows, :].astype(F32) + dot(
        coarse_sum_ref[rows, :], coarse_weights_ref[2]
    )
    family = family_ref[...]
    high, low = split(coarse_new)
    moved_ref[...] = updated_ref[...] + dot_tn(family, high) + dot_tn(family, low)
    both = jnp.concatenate([grad_src_ref[rim : rim + node_count, :], grad_dst_ref[...]], 1)
    node_grads_ref[...] = grad_updated_ref[...] + dot_nt(
        both, jnp.concatenate([weights_ref[0], weights_ref[1]], 1)
    )
    lists = lists_ref[...]
    near_list = jnp.where(odd == 1, lists[0:1], lists[1:2])
    far_list = jnp.where(odd == 1, lists[1:2], lists[0:1])
    inside = jnp.logical_or(jnp.logical_and(odd == 1, chip < chips - 1), jnp.logical_and(odd == 0, chip > 0))
    far_list = jnp.where(inside, far_list, -1)
    near = came_ref[came_ref.shape[0] - 2 * rim : came_ref.shape[0] - rim, :]
    node_grads_ref[...] += dot(one_hot_rows(near_list, node_count), near)
    tails = [mine_ref[other, depth - 8 :, :].astype(F32) for other in range(chips)]
    tails = jnp.concatenate(tails, 0).astype(BF16)
    spot, share = tail_spots(lax.broadcasted_iota(jnp.int32, (rim, 8 * chips), 0), chips, rim)
    column_spot = lax.broadcasted_iota(jnp.int32, (rim, 8 * chips), 1)
    into = one_hot_rows(far_list, node_count)
    for side in range(2):
        pick = jnp.where(column_spot == spot + side * share, 1.0, 0.0).astype(BF16)
        far = dot(pick, tails).astype(BF16)
        node_grads_ref[:, side * lanes : (side + 1) * lanes] += dot(into, far)
    bias_ref[0:1, :] = bias1_ref[...]
    bias_ref[1:2, :] = bias2_ref[...]


def join_kernel(mine_ref, theirs_ref, out_ref):
    _, odd, _ = place()
    chips, depth, lanes = mine_ref.shape
    rows = (depth - 8) // 2
    limit = out_ref.shape[0]
    for core in range(2):
        for chip in range(chips):
            start = (core * chips + chip) * rows
            count = min(rows, limit - start)
            if count <= 0:
                continue
            for side in range(2):
                span = slice(side * rows, side * rows + count)
                mine = mine_ref[chip, span, :]
                theirs = theirs_ref[chip, span, :]
                out_ref[start : start + count, side * lanes : (side + 1) * lanes] = jnp.where(
                    odd == core, mine, theirs
                ).astype(F32)


def call(kernel, outs, args, room, scratch=(), scalars=(), outside=(), copies=0, flops=0):
    vmem = pl.BlockSpec(memory_space=pltpu.VMEM)
    scalar = pl.BlockSpec(memory_space=pltpu.SMEM)
    hbm = pl.BlockSpec(memory_space=pltpu.HBM)
    specs = [
        scalar if spot in scalars else hbm if spot in outside else vmem for spot in range(len(args))
    ]
    args = [
        pltpu.with_memory_space_constraint(value, pltpu.HBM) if spot in outside else value
        for spot, value in enumerate(args)
    ]
    moved = sum(value.size * value.dtype.itemsize for value in args)
    moved += sum(math.prod(shape) * jnp.dtype(kind).itemsize for shape, kind in outs)
    scratch = [pltpu.VMEM(shape, kind) for shape, kind in scratch]
    if copies:
        scratch.append(pltpu.SemaphoreType.DMA((copies,)))
    return pl.pallas_call(
        kernel,
        out_shape=[jax.ShapeDtypeStruct(shape, kind) for shape, kind in outs],
        in_specs=specs,
        out_specs=[vmem] * len(outs),
        scratch_shapes=scratch,
        compiler_params=pltpu.CompilerParams(vmem_limit_bytes=room * MIB),
        cost_estimate=pl.CostEstimate(flops=flops, bytes_accessed=moved, transcendentals=0),
    )(*args)


def round_up(value, unit):
    return -(-value // unit) * unit


def shards(
    nodes,
    cotangent,
    fine_weights,
    coarse_weights,
    biases,
    send_lists,
    edge_ends,
    live_blocks,
    pool_members,
    parents,
    coarse_ends,
):
    ndom = lax.axis_size("dom")
    chips = ndom // 2
    node_count, width = nodes.shape
    rim = send_lists.shape[1]
    member_count, coarse_count = pool_members.shape
    slots = edge_ends.shape[1]
    edge_count2 = coarse_ends.shape[1] * ndom
    total = coarse_count * ndom
    parents = parents.reshape(1, node_count)
    pairs = [(i, i ^ 1) for i in range(ndom)]
    across = [(i, i + 1) for i in range(1, ndom - 1, 2)]
    across = across + [(target, source) for source, target in across]
    same_core = [[2 * chip + core for chip in range(chips)] for core in range(2)]

    def swap(value):
        return lax.ppermute(value, "dom", pairs)

    def exchange(value):
        return lax.all_to_all(value, "dom", 0, 0, axis_index_groups=same_core)

    rim_rows = ((rim, width), BF16)
    square = ((width, width), BF16)
    inputs = (
        nodes,
        send_lists,
        fine_weights,
        edge_ends,
        cotangent,
        biases,
        pool_members,
        parents,
        coarse_ends,
    )
    (
        near,
        far,
        nodes,
        lists,
        fine,
        edge_ends,
        upstream,
        own_biases,
        pool_members,
        parents,
        coarse_ends,
    ) = call(
        pick_kernel,
        [rim_rows, ((4 * rim, width), BF16)] + [(value.shape, value.dtype) for value in inputs],
        inputs,
        4,
        outside=range(len(inputs)),
        copies=len(inputs),
    )
    far = lax.ppermute(far, "dom", across)
    near = swap(near)

    lanes = width // 2
    pieces = round_up(-(-edge_count2 // lanes), 2)
    link_rows = round_up(4 * pieces, 8)
    side_rows = 2 * coarse_count + link_rows
    pre, outof, into, share, family, side, upright, pooled = call(
        functools.partial(prepare_kernel, ndom, rim),
        [
            ((width, slots), F32),
            ((node_count + 2 * rim, slots), BF16),
            ((node_count, slots), BF16),
            ((node_count, coarse_count), BF16),
            ((coarse_count, node_count), BF16),
            ((side_rows, lanes), BF16),
            square,
            ((coarse_count, width), F32),
        ],
        (
            nodes,
            fine,
            own_biases,
            edge_ends,
            live_blocks,
            pool_members,
            parents,
            upstream,
            coarse_ends,
        ),
        10,
        scratch=[((link_rows, lanes), F32)],
        scalars=(4,),
        flops=2 * slots * width * (2 * node_count + 2 * rim),
    )
    summed, slopes, packet = call(
        functools.partial(forward_kernel, member_count),
        [
            ((node_count, width), BF16),
            ((width, slots), BF16),
            ((chips, 2 * coarse_count + side_rows, lanes), BF16),
        ],
        (near, far, upright, fine, pre, outof, into, share, pooled, side),
        10,
        scratch=[((width, slots), BF16)],
    )
    mine = exchange(packet)
    slopes_sum, updated, upright2 = call(
        between_kernel,
        [((node_count, width), F32), ((node_count, width), F32), ((2, width, width), BF16)],
        (into, slopes, nodes, summed, fine, coarse_weights),
        8,
        flops=2 * slots * width * node_count,
    )
    theirs = swap(mine)

    rows = round_up(-(-3 * width // ndom), ROW_TILE)
    half = rows * chips
    edges2 = pieces * lanes
    coarse_whole = ((total, width), BF16)
    (
        send,
        keep,
        coarse,
        parent_all,
        into2,
        message2,
        grad_src2,
        grad_dst2,
        bias2,
        grad_updated,
        grad_src,
        grad_dst,
    ) = call(
        functools.partial(backward_kernel, ndom, edge_count2, member_count),
        [
            ((half + ROW_TILE + 2 * rim, width), BF16),
            ((half + ROW_TILE, width), BF16),
            coarse_whole,
            coarse_whole,
            ((total, edges2), BF16),
            ((width, edges2), BF16),
            coarse_whole,
            coarse_whole,
            ((1, width), F32),
            ((node_count, width), F32),
            ((node_count + 2 * rim, width), BF16),
            ((node_count, width), BF16),
        ],
        (
            mine,
            theirs,
            coarse_weights,
            upright2,
            own_biases,
            nodes,
            near,
            far,
            fine,
            share,
            upstream,
            summed,
            slopes_sum,
            slopes,
            outof,
            into,
        ),
        20 if total <= 256 else 48,
        scratch=[
            ((link_rows, lanes), F32),
            ((width, edges2), BF16),
            ((width, edges2), BF16),
            ((total, edges2), BF16),
            ((2 * half, width), BF16),
        ],
    )
    came = swap(send)
    coarse_grads, coarse_sum = call(
        coarse_kernel,
        [((3, width, width), F32), coarse_whole],
        (coarse, parent_all, into2, message2, grad_src2, grad_dst2),
        8 if total <= 256 else 24,
        flops=6 * total * width * width,
    )
    block = ((chips, 2 * rows + 8, lanes), BF16)
    (blocks,) = call(pair_kernel, [block], (keep, came, coarse_sum), 4)
    blocks = exchange(blocks)
    part, bias1 = call(sum_kernel, [block, ((1, width), F32)], (blocks,), 4)
    mine = exchange(part)
    moved, node_grads, bias_grads = call(
        finish_kernel,
        [((node_count, width), F32), ((node_count, width), F32), ((2, width), F32)],
        (
            coarse_weights,
            fine,
            coarse,
            coarse_sum,
            updated,
            family,
            grad_updated,
            grad_src,
            grad_dst,
            lists,
            came,
            mine,
            bias1,
            bias2,
        ),
        8,
        flops=8 * node_count * width * width,
    )
    theirs = swap(mine)
    (fine_grads,) = call(join_kernel, [((3 * width, width), F32)], (mine, theirs), 4)
    return moved, node_grads, fine_grads.reshape(3, width, width), coarse_grads, bias_grads


def solution(mesh):
    return jax.shard_map(
        shards,
        mesh=mesh,
        in_specs=(
            P(("groups", "dom"), None),
            P(("groups", "dom"), None),
            P(),
            P(),
            P(),
            P("groups", "dom"),
            P("groups", "dom"),
            P(("groups", "dom")),
            P("groups", "dom"),
            P(("groups", "dom")),
            P("groups", "dom"),
        ),
        out_specs=(
            P(("groups", "dom"), None),
            P(("groups", "dom"), None),
            P("groups", None, None),
            P("groups", None, None),
            P("groups", None),
        ),
        check_vma=False,
    )
```

```python
import functools
import math

import jax
import jax.numpy as jnp
from jax import lax
from jax.experimental import pallas as pl
from jax.experimental.pallas import tpu as pltpu
from jax.sharding import PartitionSpec as P

BF16 = jnp.bfloat16
F32 = jnp.float32
EDGE_BLOCK = 128
ROW_TILE = 16
MIB = 1024 * 1024
JOIN_COPIES = 4


def dot(left, right):
    return jnp.dot(left, right, preferred_element_type=F32)


def dot_tn(left, right):
    return lax.dot_general(left, right, (((0,), (0,)), ((), ())), preferred_element_type=F32)


def dot_nt(left, right):
    return lax.dot_general(left, right, (((1,), (1,)), ((), ())), preferred_element_type=F32)


def split(value):
    high = value.astype(BF16)
    return high, (value - high.astype(F32)).astype(BF16)


def one_hot_rows(index_row, count):
    spots = lax.broadcasted_iota(jnp.int32, (count, index_row.shape[1]), 0)
    return jnp.where(spots == index_row, 1.0, 0.0).astype(BF16)


def column(row, lanes):
    upright = jnp.transpose(jnp.broadcast_to(row, (8, row.shape[1])))[:, :1]
    return jnp.broadcast_to(upright, (row.shape[1], lanes))


def silu_and_slope(value):
    sig = 0.5 * jnp.tanh(0.5 * value) + 0.5
    message = value * sig
    return message, sig + message * (1.0 - sig)


def membership(members, node_count):
    spots = lax.broadcasted_iota(jnp.int32, (node_count, members.shape[1]), 0)
    total = jnp.zeros(spots.shape, F32)
    for row in range(members.shape[0]):
        total = total + jnp.where(spots == members[row : row + 1], 1.0, 0.0)
    return total.astype(BF16)


def place():
    me = lax.axis_index("dom")
    return me, lax.rem(me, 2), lax.div(me, 2)


def live_rows(ends_ref, live_ref, row):
    index = ends_ref[row : row + 1, :]
    slot = lax.broadcasted_iota(jnp.int32, index.shape, 1)
    return jnp.where(slot < live_ref[0] * EDGE_BLOCK, index, -1)


def pick_kernel(*refs):
    count = (len(refs) - 3) // 2
    inputs, (near_ref, far_ref), outputs = refs[:count], refs[count : count + 2], refs[count + 2 : -1]
    copies = [
        pltpu.make_async_copy(source, target, refs[-1].at[spot])
        for spot, (source, target) in enumerate(zip(inputs, outputs, strict=True))
    ]
    for copy in copies:
        copy.start()
    for copy in copies[:2]:
        copy.wait()
    _, odd, _ = place()
    lists = outputs[1][...]
    near = jnp.where(odd == 1, lists[0:1], lists[1:2])
    far = jnp.where(odd == 1, lists[1:2], lists[0:1])
    nodes = outputs[0][...]
    rim = near_ref.shape[0]
    near_ref[...] = dot_tn(one_hot_rows(near, nodes.shape[0]), nodes).astype(BF16)
    far = dot_tn(one_hot_rows(far, nodes.shape[0]), nodes).astype(BF16)
    for start in range(0, far_ref.shape[0], rim):
        far_ref[start : start + rim, :] = far
    for copy in copies[2:]:
        copy.wait()


def rims(near_ref, far_ref, odd):
    near = near_ref[...]
    far = far_ref[: near.shape[0], :]
    return jnp.where(odd == 1, near, far), jnp.where(odd == 1, far, near)


def prepare_kernel(
    ndom,
    rim,
    nodes_ref,
    weights_ref,
    biases_ref,
    ends_ref,
    live_ref,
    members_ref,
    parents_ref,
    cotangent_ref,
    links_ref,
    pre_ref,
    outof_ref,
    into_ref,
    share_ref,
    family_ref,
    side_ref,
    upright_ref,
    pooled_ref,
    link_ref,
):
    me, _, _ = place()
    node_count, width = nodes_ref.shape
    coarse_count = family_ref.shape[0]
    slots = ends_ref.shape[1]
    lanes = link_ref.shape[1]
    outof_ref[...] = one_hot_rows(live_rows(ends_ref, live_ref, 0), node_count + 2 * rim)
    into_ref[...] = one_hot_rows(live_rows(ends_ref, live_ref, 1), node_count)
    nodes = nodes_ref[...]
    src_proj = jnp.transpose(dot(nodes, weights_ref[0])).astype(BF16)
    dst_proj = jnp.transpose(dot(nodes, weights_ref[1])).astype(BF16)
    chunk = 2 * EDGE_BLOCK
    bias = column(biases_ref[0:1, :], chunk)
    for start in range(0, slots, chunk):
        span = slice(start, start + chunk)
        pre_ref[:, span] = (
            dot(src_proj, outof_ref[rim : rim + node_count, span])
            + dot(dst_proj, into_ref[:, span])
            + bias
        )
    upright_ref[...] = jnp.transpose(weights_ref[0].astype(F32)).astype(BF16)
    share = membership(members_ref[...], node_count)
    share_ref[...] = share
    pooled_ref[...] = dot_tn(share, nodes)
    family = one_hot_rows(parents_ref[...], coarse_count)
    family_ref[...] = family
    parent_grad = dot(family, cotangent_ref[...]).astype(BF16)
    side_ref[:coarse_count, :] = parent_grad[:, :lanes]
    side_ref[coarse_count : 2 * coarse_count, :] = parent_grad[:, lanes:]

    links = links_ref[...]
    own = links.shape[1]
    pieces = -(-own * ndom // lanes)
    spot = lax.broadcasted_iota(jnp.int32, (own, pieces * lanes), 1)
    source = lax.broadcasted_iota(jnp.int32, (own, pieces * lanes), 0)
    spread = jnp.where(spot == source + me * own, 1.0, 0.0).astype(BF16)
    coded = (
        dot((links >> 8).astype(F32).astype(BF16), spread),
        dot((links & 255).astype(F32).astype(BF16), spread),
    )
    link_ref[...] = jnp.zeros(link_ref.shape, F32)
    for part in range(2):
        for end in range(2):
            for piece in range(pieces):
                row = (part * 2 + end) * pieces + piece
                link_ref[row : row + 1, :] = coded[part][
                    end : end + 1, piece * lanes : (piece + 1) * lanes
                ]
    side_ref[2 * coarse_count :, :] = link_ref[...].astype(BF16)


def forward_kernel(
    member_count,
    near_ref,
    far_ref,
    upright_ref,
    weights_ref,
    pre_ref,
    outof_ref,
    into_ref,
    share_ref,
    pooled_ref,
    side_ref,
    summed_ref,
    slopes_ref,
    packet_ref,
):
    _, odd, _ = place()
    low, high = rims(near_ref, far_ref, odd)
    rim = low.shape[0]
    node_count = into_ref.shape[0]
    rim_proj = dot_nt(upright_ref[...], jnp.concatenate([low, high], 0)).astype(BF16)
    slots = pre_ref.shape[1]
    chunk = 2 * EDGE_BLOCK
    summed = jnp.zeros((node_count, pre_ref.shape[0]), F32)
    for start in range(0, slots, chunk):
        span = slice(start, start + chunk)
        at_rim = jnp.concatenate([outof_ref[:rim, span], outof_ref[rim + node_count :, span]], 0)
        message, slope = silu_and_slope(pre_ref[:, span] + dot(rim_proj, at_rim))
        summed = summed + dot_nt(into_ref[:, span], message.astype(BF16))
        slopes_ref[:, span] = slope.astype(BF16)
    summed = summed.astype(BF16)
    summed_ref[...] = summed
    high, low = split(dot_tn(share_ref[...], summed))
    pooled = pooled_ref[...] + dot(high, weights_ref[2]) + dot(low, weights_ref[2])
    coarse = (pooled / member_count).astype(BF16)
    count = coarse.shape[0]
    lanes = packet_ref.shape[2]
    side = side_ref[...]
    for chip in range(packet_ref.shape[0]):
        packet_ref[chip, :count, :] = coarse[:, :lanes]
        packet_ref[chip, count : 2 * count, :] = coarse[:, lanes:]
        packet_ref[chip, 2 * count :, :] = side


def between_kernel(
    into_ref,
    slopes_ref,
    nodes_ref,
    summed_ref,
    weights_ref,
    coarse_weights_ref,
    slopes_sum_ref,
    updated_ref,
    upright2_ref,
):
    for spot in range(2):
        upright2_ref[spot] = jnp.transpose(coarse_weights_ref[spot].astype(F32)).astype(BF16)
    slopes_sum_ref[...] = dot_nt(into_ref[...], slopes_ref[...])
    updated_ref[...] = nodes_ref[...].astype(F32) + dot(summed_ref[...], weights_ref[2])


def ordered(mine_ref, theirs_ref, odd, start, count):
    blocks = []
    for chip in range(mine_ref.shape[0]):
        halves = []
        for half in range(2):
            span = slice(start + half * count, start + (half + 1) * count)
            mine = mine_ref[chip, span, :]
            theirs = theirs_ref[chip, span, :]
            halves.append((jnp.where(odd == 1, theirs, mine), jnp.where(odd == 1, mine, theirs)))
        for core in range(2):
            blocks.append(jnp.concatenate([halves[0][core], halves[1][core]], 1))
    return jnp.concatenate(blocks, 0)


def backward_kernel(
    ndom,
    edge_count2,
    member_count,
    mine_ref,
    theirs_ref,
    coarse_weights_ref,
    upright2_ref,
    biases_ref,
    nodes_ref,
    near_ref,
    far_ref,
    weights_ref,
    share_ref,
    cotangent_ref,
    summed_ref,
    slopes_sum_ref,
    slopes_ref,
    outof_ref,
    into_ref,
    send_ref,
    keep_ref,
    coarse_ref,
    parent_ref,
    into2_ref,
    message2_ref,
    grad_src2_ref,
    grad_dst2_ref,
    bias2_ref,
    grad_updated_ref,
    grad_src_ref,
    grad_dst_ref,
    link_ref,
    slope2_ref,
    edge2_ref,
    outof2_ref,
    grads_ref,
):
    me, odd, _ = place()
    nodes = nodes_ref[...]
    node_count, width = nodes.shape
    coarse_count = share_ref.shape[1]
    total = ndom * coarse_count

    coarse = ordered(mine_ref, theirs_ref, odd, 0, coarse_count)
    parent_all = ordered(mine_ref, theirs_ref, odd, 2 * coarse_count, coarse_count)
    link_rows, lanes = link_ref.shape
    gathered = jnp.zeros(link_ref.shape, F32)
    for chip in range(mine_ref.shape[0]):
        for ref in (mine_ref, theirs_ref):
            gathered = gathered + ref[chip, 4 * coarse_count :, :].astype(F32)
    link_ref[...] = gathered
    pieces = -(-edge_count2 // lanes)
    ends2 = []
    for end in range(2):
        rows = []
        for piece in range(pieces):
            top = end * pieces + piece
            bottom = (2 + end) * pieces + piece
            code = 256.0 * link_ref[top : top + 1, :] + link_ref[bottom : bottom + 1, :]
            spot = lax.broadcasted_iota(jnp.int32, code.shape, 1) + piece * lanes
            rows.append(jnp.where(spot < edge_count2, code.astype(jnp.int32), -1))
        ends2.append(rows)
    src2 = dot_nt(upright2_ref[0], coarse).astype(BF16)
    dst2 = dot_nt(upright2_ref[1], coarse).astype(BF16)
    grad_agg2 = dot_nt(parent_all, coarse_weights_ref[2])
    grad_agg2_near = dot_nt(coarse_weights_ref[2], parent_all).astype(BF16)
    bias = column(biases_ref[1:2, :], width)
    step = 2 * lanes
    for start in range(0, message2_ref.shape[1], step):
        span = slice(start, start + step)
        first = start // lanes
        outof, into = (
            one_hot_rows(jnp.concatenate(rows[first : first + 2], 1), total) for rows in ends2
        )
        outof2_ref[:, span] = outof
        into2_ref[:, span] = into
        message, slope = silu_and_slope(dot(src2, outof) + dot(dst2, into) + bias)
        message2_ref[:, span] = message.astype(BF16)
        slope2_ref[:, span] = slope.astype(BF16)
        edge2_ref[:, span] = (dot(grad_agg2_near, into) * slope).astype(BF16)
    grad_dst2 = dot_nt(into2_ref[...], slope2_ref[...]) * grad_agg2
    grad_src2 = dot_nt(outof2_ref[...], edge2_ref[...])
    bias2_ref[...] = jnp.sum(grad_dst2, 0, keepdims=True)
    grad_src2_ref[...] = grad_src2.astype(BF16)
    grad_dst2_ref[...] = grad_dst2.astype(BF16)
    coarse_ref[...] = coarse
    parent_ref[...] = parent_all

    rows = pl.ds(pl.multiple_of(me * coarse_count, coarse_count), coarse_count)
    coarse_grad = (
        parent_ref[rows, :].astype(F32)
        + dot_nt(grad_src2_ref[rows, :], coarse_weights_ref[0])
        + dot_nt(grad_dst2_ref[rows, :], coarse_weights_ref[1])
    )
    share = share_ref[...]
    high, low = split(coarse_grad / member_count)
    grad_updated = cotangent_ref[...].astype(F32) + dot(share, high) + dot(share, low)
    grad_updated_ref[...] = grad_updated

    low, high = rims(near_ref, far_ref, odd)
    extended = jnp.concatenate([low, nodes, high], 0)
    rim = low.shape[0]
    slots = slopes_ref.shape[1]
    grad_updated_near = grad_updated.astype(BF16)
    grad_dst = slopes_sum_ref[...] * dot_nt(grad_updated_near, weights_ref[2])
    grad_summed = dot_nt(weights_ref[2], grad_updated_near).astype(BF16)
    chunk = 2 * EDGE_BLOCK
    grad_src = jnp.zeros((outof_ref.shape[0], width), F32)
    for start in range(0, slots, chunk):
        span = slice(start, start + chunk)
        slope = slopes_ref[:, span].astype(F32)
        edge = (dot(grad_summed, into_ref[:, span]) * slope).astype(BF16)
        grad_src = grad_src + dot_nt(outof_ref[:, span], edge)
    grad_src = grad_src.astype(BF16)
    bias1 = jnp.sum(grad_dst, 0, keepdims=True)
    grad_dst = grad_dst.astype(BF16)
    grad_src_ref[...] = grad_src
    grad_dst_ref[...] = grad_dst
    low = dot_nt(grad_src[:rim], weights_ref[0]).astype(BF16)
    high = dot_nt(grad_src[rim + node_count :], weights_ref[0]).astype(BF16)
    grads_ref[0:width, :] = dot_tn(extended, grad_src).astype(BF16)
    grads_ref[width : 2 * width, :] = dot_tn(nodes, grad_dst).astype(BF16)
    grads_ref[2 * width : 3 * width, :] = dot_tn(summed_ref[...], grad_updated_near).astype(BF16)
    if grads_ref.shape[0] > 3 * width:
        grads_ref[3 * width :, :] = jnp.zeros((grads_ref.shape[0] - 3 * width, width), BF16)
    half = grads_ref.shape[0] // 2
    keep_ref[:half, :] = grads_ref[pl.ds(pl.multiple_of(odd * half, ROW_TILE), half), :]
    send_ref[:half, :] = grads_ref[pl.ds(pl.multiple_of((1 - odd) * half, ROW_TILE), half), :]
    bias_rows = two_rows(bias1, ROW_TILE)
    keep_ref[half : half + ROW_TILE, :] = bias_rows
    send_ref[half : half + ROW_TILE, :] = bias_rows
    base = half + ROW_TILE
    send_ref[base : base + rim, :] = jnp.where(odd == 1, low, high)
    send_ref[base + rim :, :] = jnp.where(odd == 1, high, low)


def two_rows(value, count):
    high = value.astype(BF16).astype(F32)
    row = lax.broadcasted_iota(jnp.int32, (count, value.shape[1]), 0)
    return jnp.where(row == 0, high, jnp.where(row == 1, value - high, 0.0)).astype(BF16)


def tail_spots(rows, chips, rim):
    share = -(-rim // chips)
    chip = rows >> (share.bit_length() - 1)
    return 8 * chip + 4 + rows - share * chip, share


def pair_kernel(keep_ref, came_ref, made_ref, blocks_ref):
    half = keep_ref.shape[0] - ROW_TILE
    chips, _, lanes = blocks_ref.shape
    rows = half // chips
    rim = (came_ref.shape[0] - half - ROW_TILE) // 2
    bias = keep_ref[half:, :].astype(F32) + came_ref[half : half + ROW_TILE, :].astype(F32)
    bias = jnp.sum(bias, 0, keepdims=True)
    far = came_ref[half + ROW_TILE + rim :, :]
    spot, share = tail_spots(lax.broadcasted_iota(jnp.int32, (8 * chips, rim), 1), chips, rim)
    row = lax.broadcasted_iota(jnp.int32, (8 * chips, rim), 0)
    line = lax.broadcasted_iota(jnp.int32, (8, lanes), 0)
    tails = jnp.zeros((8 * chips, lanes), F32)
    bias_tail = jnp.zeros((8, lanes), F32)
    for side in range(2):
        span = slice(side * lanes, (side + 1) * lanes)
        pick = jnp.where(row == spot + side * share, 1.0, 0.0).astype(BF16)
        tails = tails + dot(pick, far[:, span])
        value = bias[:, span]
        high = value.astype(BF16).astype(F32)
        bias_tail = jnp.where(line == 2 * side, high, bias_tail)
        bias_tail = jnp.where(line == 2 * side + 1, value - high, bias_tail)
    for chip in range(chips):
        span = slice(chip * rows, (chip + 1) * rows)
        total = (keep_ref[span, :].astype(F32) + came_ref[span, :].astype(F32)).astype(BF16)
        blocks_ref[chip, :rows, :] = total[:, :lanes]
        blocks_ref[chip, rows : 2 * rows, :] = total[:, lanes:]
        blocks_ref[chip, 2 * rows :, :] = (tails[8 * chip : 8 * chip + 8] + bias_tail).astype(BF16)


def sum_kernel(blocks_ref, part_ref, bias1_ref):
    _, odd, _ = place()
    chips, depth, lanes = blocks_ref.shape
    rows = depth - 8
    total = blocks_ref[0].astype(F32)
    for other in range(1, chips):
        total = total + blocks_ref[other].astype(F32)
    part = total[:rows].astype(BF16)
    for other in range(chips):
        after = blocks_ref[min(other + 1, chips - 1), rows:, :]
        before = blocks_ref[max(other - 1, 0), rows:, :]
        part_ref[other, :rows, :] = part
        part_ref[other, rows:, :] = jnp.where(odd == 1, after, before)
    for side in range(2):
        row = rows + 2 * side
        bias1_ref[:, side * lanes : (side + 1) * lanes] = jnp.sum(
            total[row : row + 2], 0, keepdims=True
        )


def coarse_kernel(
    coarse_ref,
    parent_ref,
    into2_ref,
    message2_ref,
    grad_src2_ref,
    grad_dst2_ref,
    coarse_grads_ref,
    coarse_sum_ref,
):
    coarse = coarse_ref[...]
    coarse_sum = dot_nt(into2_ref[...], message2_ref[...]).astype(BF16)
    coarse_sum_ref[...] = coarse_sum
    coarse_grads_ref[0] = dot_tn(coarse, grad_src2_ref[...])
    coarse_grads_ref[1] = dot_tn(coarse, grad_dst2_ref[...])
    coarse_grads_ref[2] = dot_tn(coarse_sum, parent_ref[...])


def finish_kernel(
    coarse_weights_ref,
    weights_ref,
    coarse_ref,
    coarse_sum_ref,
    updated_ref,
    family_ref,
    grad_updated_ref,
    grad_src_ref,
    grad_dst_ref,
    lists_ref,
    came_ref,
    mine_ref,
    bias1_ref,
    bias2_ref,
    coarse_grads_ref,
    moved_ref,
    node_grads_ref,
    bias_ref,
    coarse_grads_hbm,
    sems,
):
    copy = pltpu.make_async_copy(coarse_grads_ref, coarse_grads_hbm, sems.at[0])
    copy.start()
    bias_ref[0:1, :] = bias1_ref[...]
    bias_ref[1:2, :] = bias2_ref[...]
    me, odd, chip = place()
    node_count = updated_ref.shape[0]
    coarse_count = family_ref.shape[0]
    chips, depth, lanes = mine_ref.shape
    rim = lists_ref.shape[1]
    rows = pl.ds(pl.multiple_of(me * coarse_count, coarse_count), coarse_count)
    coarse_new = coarse_ref[rows, :].astype(F32) + dot(
        coarse_sum_ref[rows, :], coarse_weights_ref[2]
    )
    family = family_ref[...]
    high, low = split(coarse_new)
    moved_ref[...] = updated_ref[...] + dot_tn(family, high) + dot_tn(family, low)
    both = jnp.concatenate([grad_src_ref[rim : rim + node_count, :], grad_dst_ref[...]], 1)
    node_grads_ref[...] = grad_updated_ref[...] + dot_nt(
        both, jnp.concatenate([weights_ref[0], weights_ref[1]], 1)
    )
    lists = lists_ref[...]
    near_list = jnp.where(odd == 1, lists[0:1], lists[1:2])
    far_list = jnp.where(odd == 1, lists[1:2], lists[0:1])
    inside = jnp.logical_or(jnp.logical_and(odd == 1, chip < chips - 1), jnp.logical_and(odd == 0, chip > 0))
    far_list = jnp.where(inside, far_list, -1)
    near = came_ref[came_ref.shape[0] - 2 * rim : came_ref.shape[0] - rim, :]
    node_grads_ref[...] += dot(one_hot_rows(near_list, node_count), near)
    tails = [mine_ref[other, depth - 8 :, :].astype(F32) for other in range(chips)]
    tails = jnp.concatenate(tails, 0).astype(BF16)
    spot, share = tail_spots(lax.broadcasted_iota(jnp.int32, (rim, 8 * chips), 0), chips, rim)
    column_spot = lax.broadcasted_iota(jnp.int32, (rim, 8 * chips), 1)
    into = one_hot_rows(far_list, node_count)
    for side in range(2):
        pick = jnp.where(column_spot == spot + side * share, 1.0, 0.0).astype(BF16)
        far = dot(pick, tails).astype(BF16)
        node_grads_ref[:, side * lanes : (side + 1) * lanes] += dot(into, far)
    copy.wait()


def join_kernel(
    mine_ref,
    theirs_ref,
    moved_ref,
    node_grads_ref,
    bias_ref,
    out_hbm,
    moved_hbm,
    node_grads_hbm,
    bias_hbm,
    out_ref,
    sems,
):
    ready = (
        (bias_ref, bias_hbm),
        (moved_ref, moved_hbm),
        (node_grads_ref, node_grads_hbm),
    )
    copies = [
        pltpu.make_async_copy(source, target, sems.at[spot])
        for spot, (source, target) in enumerate(ready)
    ]
    for copy in copies:
        copy.start()
    _, odd, _ = place()
    chips, depth, lanes = mine_ref.shape
    rows = (depth - 8) // 2
    limit = out_ref.shape[0]
    pieces = 0
    done = 0
    for block in range(2 * chips):
        core, chip = divmod(block, chips)
        start = block * rows
        count = min(rows, limit - start)
        if count <= 0:
            break
        for side in range(2):
            span = slice(side * rows, side * rows + count)
            mine = mine_ref[chip, span, :]
            theirs = theirs_ref[chip, span, :]
            out_ref[start : start + count, side * lanes : (side + 1) * lanes] = jnp.where(
                odd == core, mine, theirs
            ).astype(F32)
        end = start + count
        if end == limit or end >= (pieces + 1) * limit // JOIN_COPIES:
            pieces += 1
            span = pl.ds(done, end - done)
            copies.append(
                pltpu.make_async_copy(
                    out_ref.at[span, :], out_hbm.at[span, :], sems.at[len(copies)]
                )
            )
            copies[-1].start()
            done = end
    for copy in copies:
        copy.wait()


def call(
    kernel, outs, args, room, scratch=(), scalars=(), outside=(), copies=0, flops=0, outgoing=()
):
    vmem = pl.BlockSpec(memory_space=pltpu.VMEM)
    scalar = pl.BlockSpec(memory_space=pltpu.SMEM)
    hbm = pl.BlockSpec(memory_space=pltpu.HBM)
    specs = [
        scalar if spot in scalars else hbm if spot in outside else vmem for spot in range(len(args))
    ]
    args = [
        pltpu.with_memory_space_constraint(value, pltpu.HBM) if spot in outside else value
        for spot, value in enumerate(args)
    ]
    moved = sum(value.size * value.dtype.itemsize for value in args)
    moved += sum(math.prod(shape) * jnp.dtype(kind).itemsize for shape, kind in outs)
    scratch = [pltpu.VMEM(shape, kind) for shape, kind in scratch]
    if copies:
        scratch.append(pltpu.SemaphoreType.DMA((copies,)))
    return pl.pallas_call(
        kernel,
        out_shape=[jax.ShapeDtypeStruct(shape, kind) for shape, kind in outs],
        in_specs=specs,
        out_specs=[hbm if spot in outgoing else vmem for spot in range(len(outs))],
        scratch_shapes=scratch,
        compiler_params=pltpu.CompilerParams(vmem_limit_bytes=room * MIB),
        cost_estimate=pl.CostEstimate(flops=flops, bytes_accessed=moved, transcendentals=0),
    )(*args)


def round_up(value, unit):
    return -(-value // unit) * unit


def shards(
    nodes,
    cotangent,
    fine_weights,
    coarse_weights,
    biases,
    send_lists,
    edge_ends,
    live_blocks,
    pool_members,
    parents,
    coarse_ends,
):
    ndom = lax.axis_size("dom")
    chips = ndom // 2
    node_count, width = nodes.shape
    rim = send_lists.shape[1]
    member_count, coarse_count = pool_members.shape
    slots = edge_ends.shape[1]
    edge_count2 = coarse_ends.shape[1] * ndom
    total = coarse_count * ndom
    parents = parents.reshape(1, node_count)
    pairs = [(i, i ^ 1) for i in range(ndom)]
    across = [(i, i + 1) for i in range(1, ndom - 1, 2)]
    across = across + [(target, source) for source, target in across]
    same_core = [[2 * chip + core for chip in range(chips)] for core in range(2)]

    def swap(value):
        return lax.ppermute(value, "dom", pairs)

    def exchange(value):
        return lax.all_to_all(value, "dom", 0, 0, axis_index_groups=same_core)

    rim_rows = ((rim, width), BF16)
    square = ((width, width), BF16)
    inputs = (
        nodes,
        send_lists,
        fine_weights,
        edge_ends,
        cotangent,
        biases,
        pool_members,
        parents,
        coarse_ends,
    )
    (
        near,
        far,
        nodes,
        lists,
        fine,
        edge_ends,
        upstream,
        own_biases,
        pool_members,
        parents,
        coarse_ends,
    ) = call(
        pick_kernel,
        [rim_rows, ((4 * rim, width), BF16)] + [(value.shape, value.dtype) for value in inputs],
        inputs,
        4,
        outside=range(len(inputs)),
        copies=len(inputs),
    )
    far = lax.ppermute(far, "dom", across)
    near = swap(near)

    lanes = width // 2
    pieces = round_up(-(-edge_count2 // lanes), 2)
    link_rows = round_up(4 * pieces, 8)
    side_rows = 2 * coarse_count + link_rows
    pre, outof, into, share, family, side, upright, pooled = call(
        functools.partial(prepare_kernel, ndom, rim),
        [
            ((width, slots), F32),
            ((node_count + 2 * rim, slots), BF16),
            ((node_count, slots), BF16),
            ((node_count, coarse_count), BF16),
            ((coarse_count, node_count), BF16),
            ((side_rows, lanes), BF16),
            square,
            ((coarse_count, width), F32),
        ],
        (
            nodes,
            fine,
            own_biases,
            edge_ends,
            live_blocks,
            pool_members,
            parents,
            upstream,
            coarse_ends,
        ),
        10,
        scratch=[((link_rows, lanes), F32)],
        scalars=(4,),
        flops=2 * slots * width * (2 * node_count + 2 * rim),
    )
    summed, slopes, packet = call(
        functools.partial(forward_kernel, member_count),
        [
            ((node_count, width), BF16),
            ((width, slots), BF16),
            ((chips, 2 * coarse_count + side_rows, lanes), BF16),
        ],
        (near, far, upright, fine, pre, outof, into, share, pooled, side),
        10,
    )
    mine = exchange(packet)
    slopes_sum, updated, upright2 = call(
        between_kernel,
        [((node_count, width), F32), ((node_count, width), F32), ((2, width, width), BF16)],
        (into, slopes, nodes, summed, fine, coarse_weights),
        8,
        flops=2 * slots * width * node_count,
    )
    theirs = swap(mine)

    rows = round_up(-(-3 * width // ndom), ROW_TILE)
    half = rows * chips
    edges2 = pieces * lanes
    coarse_whole = ((total, width), BF16)
    (
        send,
        keep,
        coarse,
        parent_all,
        into2,
        message2,
        grad_src2,
        grad_dst2,
        bias2,
        grad_updated,
        grad_src,
        grad_dst,
    ) = call(
        functools.partial(backward_kernel, ndom, edge_count2, member_count),
        [
            ((half + ROW_TILE + 2 * rim, width), BF16),
            ((half + ROW_TILE, width), BF16),
            coarse_whole,
            coarse_whole,
            ((total, edges2), BF16),
            ((width, edges2), BF16),
            coarse_whole,
            coarse_whole,
            ((1, width), F32),
            ((node_count, width), F32),
            ((node_count + 2 * rim, width), BF16),
            ((node_count, width), BF16),
        ],
        (
            mine,
            theirs,
            coarse_weights,
            upright2,
            own_biases,
            nodes,
            near,
            far,
            fine,
            share,
            upstream,
            summed,
            slopes_sum,
            slopes,
            outof,
            into,
        ),
        20 if total <= 256 else 48,
        scratch=[
            ((link_rows, lanes), F32),
            ((width, edges2), BF16),
            ((width, edges2), BF16),
            ((total, edges2), BF16),
            ((2 * half, width), BF16),
        ],
    )
    came = swap(send)
    coarse_grads, coarse_sum = call(
        coarse_kernel,
        [((3, width, width), F32), coarse_whole],
        (coarse, parent_all, into2, message2, grad_src2, grad_dst2),
        8 if total <= 256 else 24,
        flops=6 * total * width * width,
    )
    block = ((chips, 2 * rows + 8, lanes), BF16)
    (blocks,) = call(pair_kernel, [block], (keep, came, coarse_sum), 4)
    blocks = exchange(blocks)
    part, bias1 = call(sum_kernel, [block, ((1, width), F32)], (blocks,), 4)
    mine = exchange(part)
    coarse_grads_shape = ((3, width, width), F32)
    node_shape = ((node_count, width), F32)
    bias_shape = ((2, width), F32)
    moved, node_grads, bias_grads, coarse_grads = call(
        finish_kernel,
        [node_shape, node_shape, bias_shape, coarse_grads_shape],
        (
            coarse_weights,
            fine,
            coarse,
            coarse_sum,
            updated,
            family,
            grad_updated,
            grad_src,
            grad_dst,
            lists,
            came,
            mine,
            bias1,
            bias2,
            coarse_grads,
        ),
        8,
        copies=1,
        outgoing=(3,),
        flops=8 * node_count * width * width,
    )
    theirs = swap(mine)
    fine_grads, moved, node_grads, bias_grads = call(
        join_kernel,
        [((3 * width, width), F32), node_shape, node_shape, bias_shape],
        (mine, theirs, moved, node_grads, bias_grads),
        4,
        scratch=[((3 * width, width), F32)],
        copies=3 + JOIN_COPIES,
        outgoing=range(4),
    )
    return moved, node_grads, fine_grads.reshape(3, width, width), coarse_grads, bias_grads


def solution(mesh):
    return jax.shard_map(
        shards,
        mesh=mesh,
        in_specs=(
            P(("groups", "dom"), None),
            P(("groups", "dom"), None),
            P(),
            P(),
            P(),
            P("groups", "dom"),
            P("groups", "dom"),
            P(("groups", "dom")),
            P("groups", "dom"),
            P(("groups", "dom")),
            P("groups", "dom"),
        ),
        out_specs=(
            P(("groups", "dom"), None),
            P(("groups", "dom"), None),
            P("groups", None, None),
            P("groups", None, None),
            P("groups", None),
        ),
        check_vma=False,
    )
```

```python
import functools
import math

import jax
import jax.numpy as jnp
from jax import lax
from jax.experimental import pallas as pl
from jax.experimental.pallas import tpu as pltpu
from jax.sharding import PartitionSpec as P

BF16 = jnp.bfloat16
F32 = jnp.float32
EDGE_BLOCK = 128
ROW_TILE = 16
MIB = 1024 * 1024
JOIN_COPIES = 4


def dot(left, right):
    return jnp.dot(left, right, preferred_element_type=F32)


def dot_tn(left, right):
    return lax.dot_general(left, right, (((0,), (0,)), ((), ())), preferred_element_type=F32)


def dot_nt(left, right):
    return lax.dot_general(left, right, (((1,), (1,)), ((), ())), preferred_element_type=F32)


def split(value):
    high = value.astype(BF16)
    return high, (value - high.astype(F32)).astype(BF16)


def one_hot_rows(index_row, count):
    spots = lax.broadcasted_iota(jnp.int32, (count, index_row.shape[1]), 0)
    return jnp.where(spots == index_row, 1.0, 0.0).astype(BF16)


def column(row, lanes):
    upright = jnp.transpose(jnp.broadcast_to(row, (8, row.shape[1])))[:, :1]
    return jnp.broadcast_to(upright, (row.shape[1], lanes))


def silu_and_slope(value):
    sig = 0.5 * jnp.tanh(0.5 * value) + 0.5
    message = value * sig
    return message, sig + message * (1.0 - sig)


def membership(members, node_count):
    spots = lax.broadcasted_iota(jnp.int32, (node_count, members.shape[1]), 0)
    total = jnp.zeros(spots.shape, F32)
    for row in range(members.shape[0]):
        total = total + jnp.where(spots == members[row : row + 1], 1.0, 0.0)
    return total.astype(BF16)


def place():
    me = lax.axis_index("dom")
    return me, lax.rem(me, 2), lax.div(me, 2)


def live_rows(ends_ref, live_ref, row):
    index = ends_ref[row : row + 1, :]
    slot = lax.broadcasted_iota(jnp.int32, index.shape, 1)
    return jnp.where(slot < live_ref[0] * EDGE_BLOCK, index, -1)


def pick_kernel(*refs):
    count = (len(refs) - 3) // 2
    inputs, (near_ref, far_ref), outputs = refs[:count], refs[count : count + 2], refs[count + 2 : -1]
    copies = [
        pltpu.make_async_copy(source, target, refs[-1].at[spot])
        for spot, (source, target) in enumerate(zip(inputs, outputs, strict=True))
    ]
    for copy in copies:
        copy.start()
    for copy in copies[:2]:
        copy.wait()
    _, odd, _ = place()
    lists = outputs[1][...]
    near = jnp.where(odd == 1, lists[0:1], lists[1:2])
    far = jnp.where(odd == 1, lists[1:2], lists[0:1])
    nodes = outputs[0][...]
    rim = near_ref.shape[0]
    near_ref[...] = dot_tn(one_hot_rows(near, nodes.shape[0]), nodes).astype(BF16)
    far = dot_tn(one_hot_rows(far, nodes.shape[0]), nodes).astype(BF16)
    for start in range(0, far_ref.shape[0], rim):
        far_ref[start : start + rim, :] = far
    for copy in copies[2:]:
        copy.wait()


def rims(near_ref, far_ref, odd):
    near = near_ref[...]
    far = far_ref[: near.shape[0], :]
    return jnp.where(odd == 1, near, far), jnp.where(odd == 1, far, near)


def prepare_kernel(
    rim,
    nodes_ref,
    weights_ref,
    biases_ref,
    ends_ref,
    live_ref,
    members_ref,
    parents_ref,
    cotangent_ref,
    links_ref,
    pre_ref,
    outof_ref,
    into_ref,
    share_ref,
    family_ref,
    side_ref,
    upright_ref,
    pooled_ref,
    link_ref,
):
    node_count, width = nodes_ref.shape
    coarse_count = family_ref.shape[0]
    slots = ends_ref.shape[1]
    lanes = link_ref.shape[1]
    outof_ref[...] = one_hot_rows(live_rows(ends_ref, live_ref, 0), node_count + 2 * rim)
    into_ref[...] = one_hot_rows(live_rows(ends_ref, live_ref, 1), node_count)
    nodes = nodes_ref[...]
    src_proj = jnp.transpose(dot(nodes, weights_ref[0])).astype(BF16)
    dst_proj = jnp.transpose(dot(nodes, weights_ref[1])).astype(BF16)
    chunk = 2 * EDGE_BLOCK
    bias = column(biases_ref[0:1, :], chunk)
    for start in range(0, slots, chunk):
        span = slice(start, start + chunk)
        pre_ref[:, span] = (
            dot(src_proj, outof_ref[rim : rim + node_count, span])
            + dot(dst_proj, into_ref[:, span])
            + bias
        )
    upright_ref[...] = jnp.transpose(weights_ref[0].astype(F32)).astype(BF16)
    share = membership(members_ref[...], node_count)
    share_ref[...] = share
    pooled_ref[...] = dot_tn(share, nodes)
    family = one_hot_rows(parents_ref[...], coarse_count)
    family_ref[...] = family
    parent_grad = dot(family, cotangent_ref[...]).astype(BF16)
    side_ref[:coarse_count, :] = parent_grad[:, :lanes]
    side_ref[coarse_count : 2 * coarse_count, :] = parent_grad[:, lanes:]

    links = links_ref[...]
    own = links.shape[1]
    link_ref[...] = jnp.zeros(link_ref.shape, F32)
    link_ref[0:2, :own] = (links >> 8).astype(F32)
    link_ref[2:4, :own] = (links & 255).astype(F32)
    side_ref[2 * coarse_count :, :] = link_ref[...].astype(BF16)


def forward_kernel(
    member_count,
    near_ref,
    far_ref,
    upright_ref,
    weights_ref,
    pre_ref,
    outof_ref,
    into_ref,
    share_ref,
    pooled_ref,
    side_ref,
    summed_ref,
    slopes_ref,
    packet_ref,
):
    _, odd, _ = place()
    low, high = rims(near_ref, far_ref, odd)
    rim = low.shape[0]
    node_count = into_ref.shape[0]
    rim_proj = dot_nt(upright_ref[...], jnp.concatenate([low, high], 0)).astype(BF16)
    slots = pre_ref.shape[1]
    chunk = 2 * EDGE_BLOCK
    summed = jnp.zeros((node_count, pre_ref.shape[0]), F32)
    for start in range(0, slots, chunk):
        span = slice(start, start + chunk)
        at_rim = jnp.concatenate([outof_ref[:rim, span], outof_ref[rim + node_count :, span]], 0)
        message, slope = silu_and_slope(pre_ref[:, span] + dot(rim_proj, at_rim))
        summed = summed + dot_nt(into_ref[:, span], message.astype(BF16))
        slopes_ref[:, span] = slope.astype(BF16)
    summed = summed.astype(BF16)
    summed_ref[...] = summed
    high, low = split(dot_tn(share_ref[...], summed))
    pooled = pooled_ref[...] + dot(high, weights_ref[2]) + dot(low, weights_ref[2])
    coarse = (pooled / member_count).astype(BF16)
    count = coarse.shape[0]
    lanes = packet_ref.shape[2]
    side = side_ref[...]
    for chip in range(packet_ref.shape[0]):
        packet_ref[chip, :count, :] = coarse[:, :lanes]
        packet_ref[chip, count : 2 * count, :] = coarse[:, lanes:]
        packet_ref[chip, 2 * count :, :] = side


def edge_ends2(packet_ref, repeat_ref, block_ref):
    links = [packet_ref[chip, packet_ref.shape[1] - 8 :, :] for chip in range(packet_ref.shape[0])]
    links = jnp.concatenate([link.astype(F32) for link in links], 0).astype(BF16)
    code = dot(links, repeat_ref[...]) * block_ref[...]
    code = jnp.sum(code.reshape(packet_ref.shape[0], 8, code.shape[1]), 0)
    return (256.0 * code[0:2] + code[2:4]).astype(jnp.int32)


def between_kernel(
    own,
    mine_ref,
    into_ref,
    slopes_ref,
    nodes_ref,
    summed_ref,
    weights_ref,
    coarse_weights_ref,
    slopes_sum_ref,
    updated_ref,
    upright2_ref,
    repeat_ref,
    block_ref,
    ends2_ref,
):
    edge = lax.broadcasted_iota(jnp.int32, repeat_ref.shape, 1)
    owner = ((edge.astype(F32) + 0.5) * (1.0 / own)).astype(jnp.int32)
    spot = lax.broadcasted_iota(jnp.int32, repeat_ref.shape, 0)
    repeat_ref[...] = jnp.where(edge - own * owner == spot, 1.0, 0.0).astype(BF16)
    edge = lax.broadcasted_iota(jnp.int32, block_ref.shape, 1)
    owner = ((edge.astype(F32) + 0.5) * (1.0 / own)).astype(jnp.int32)
    block = lax.broadcasted_iota(jnp.int32, block_ref.shape, 0) >> 3
    block_ref[...] = jnp.where(block == owner, 1.0, 0.0)
    ends2_ref[...] = edge_ends2(mine_ref, repeat_ref, block_ref)
    for spot in range(2):
        upright2_ref[spot] = jnp.transpose(coarse_weights_ref[spot].astype(F32)).astype(BF16)
    slopes_sum_ref[...] = dot_nt(into_ref[...], slopes_ref[...])
    updated_ref[...] = nodes_ref[...].astype(F32) + dot(summed_ref[...], weights_ref[2])


def ordered(mine_ref, theirs_ref, odd, start, count):
    blocks = []
    for chip in range(mine_ref.shape[0]):
        halves = []
        for half in range(2):
            span = slice(start + half * count, start + (half + 1) * count)
            mine = mine_ref[chip, span, :]
            theirs = theirs_ref[chip, span, :]
            halves.append((jnp.where(odd == 1, theirs, mine), jnp.where(odd == 1, mine, theirs)))
        for core in range(2):
            blocks.append(jnp.concatenate([halves[0][core], halves[1][core]], 1))
    return jnp.concatenate(blocks, 0)


def backward_kernel(
    ndom,
    member_count,
    mine_ref,
    theirs_ref,
    coarse_weights_ref,
    upright2_ref,
    repeat_ref,
    block_ref,
    ends2_ref,
    biases_ref,
    nodes_ref,
    near_ref,
    far_ref,
    weights_ref,
    share_ref,
    cotangent_ref,
    summed_ref,
    slopes_sum_ref,
    slopes_ref,
    outof_ref,
    into_ref,
    send_ref,
    keep_ref,
    coarse_ref,
    parent_ref,
    into2_ref,
    message2_ref,
    grad_src2_ref,
    grad_dst2_ref,
    bias2_ref,
    grad_updated_ref,
    grad_src_ref,
    grad_dst_ref,
    slope2_ref,
    edge2_ref,
    outof2_ref,
    grads_ref,
):
    me, odd, _ = place()
    nodes = nodes_ref[...]
    node_count, width = nodes.shape
    coarse_count = share_ref.shape[1]
    total = ndom * coarse_count

    coarse = ordered(mine_ref, theirs_ref, odd, 0, coarse_count)
    parent_all = ordered(mine_ref, theirs_ref, odd, 2 * coarse_count, coarse_count)
    ends2 = jnp.concatenate([ends2_ref[...], edge_ends2(theirs_ref, repeat_ref, block_ref)], 1)
    src2 = dot_nt(upright2_ref[0], coarse).astype(BF16)
    dst2 = dot_nt(upright2_ref[1], coarse).astype(BF16)
    grad_agg2 = dot_nt(parent_all, coarse_weights_ref[2])
    grad_agg2_near = dot_nt(coarse_weights_ref[2], parent_all).astype(BF16)
    bias = column(biases_ref[1:2, :], width)
    step = width
    for start in range(0, message2_ref.shape[1], step):
        span = slice(start, start + step)
        outof = one_hot_rows(ends2[0:1, span], total)
        into = one_hot_rows(ends2[1:2, span], total)
        outof2_ref[:, span] = outof
        into2_ref[:, span] = into
        message, slope = silu_and_slope(dot(src2, outof) + dot(dst2, into) + bias)
        message2_ref[:, span] = message.astype(BF16)
        slope2_ref[:, span] = slope.astype(BF16)
        edge2_ref[:, span] = (dot(grad_agg2_near, into) * slope).astype(BF16)
    grad_dst2 = dot_nt(into2_ref[...], slope2_ref[...]) * grad_agg2
    grad_src2 = dot_nt(outof2_ref[...], edge2_ref[...])
    bias2_ref[...] = jnp.sum(grad_dst2, 0, keepdims=True)
    grad_src2_ref[...] = grad_src2.astype(BF16)
    grad_dst2_ref[...] = grad_dst2.astype(BF16)
    coarse_ref[...] = coarse
    parent_ref[...] = parent_all

    rows = pl.ds(pl.multiple_of(me * coarse_count, coarse_count), coarse_count)
    coarse_grad = (
        parent_ref[rows, :].astype(F32)
        + dot_nt(grad_src2_ref[rows, :], coarse_weights_ref[0])
        + dot_nt(grad_dst2_ref[rows, :], coarse_weights_ref[1])
    )
    share = share_ref[...]
    high, low = split(coarse_grad / member_count)
    grad_updated = cotangent_ref[...].astype(F32) + dot(share, high) + dot(share, low)
    grad_updated_ref[...] = grad_updated

    low, high = rims(near_ref, far_ref, odd)
    extended = jnp.concatenate([low, nodes, high], 0)
    rim = low.shape[0]
    slots = slopes_ref.shape[1]
    grad_updated_near = grad_updated.astype(BF16)
    grad_dst = slopes_sum_ref[...] * dot_nt(grad_updated_near, weights_ref[2])
    grad_summed = dot_nt(weights_ref[2], grad_updated_near).astype(BF16)
    chunk = 2 * EDGE_BLOCK
    grad_src = jnp.zeros((outof_ref.shape[0], width), F32)
    for start in range(0, slots, chunk):
        span = slice(start, start + chunk)
        slope = slopes_ref[:, span].astype(F32)
        edge = (dot(grad_summed, into_ref[:, span]) * slope).astype(BF16)
        grad_src = grad_src + dot_nt(outof_ref[:, span], edge)
    grad_src = grad_src.astype(BF16)
    bias1 = jnp.sum(grad_dst, 0, keepdims=True)
    grad_dst = grad_dst.astype(BF16)
    grad_src_ref[...] = grad_src
    grad_dst_ref[...] = grad_dst
    low = dot_nt(grad_src[:rim], weights_ref[0]).astype(BF16)
    high = dot_nt(grad_src[rim + node_count :], weights_ref[0]).astype(BF16)
    grads_ref[0:width, :] = dot_tn(extended, grad_src).astype(BF16)
    grads_ref[width : 2 * width, :] = dot_tn(nodes, grad_dst).astype(BF16)
    grads_ref[2 * width : 3 * width, :] = dot_tn(summed_ref[...], grad_updated_near).astype(BF16)
    if grads_ref.shape[0] > 3 * width:
        grads_ref[3 * width :, :] = jnp.zeros((grads_ref.shape[0] - 3 * width, width), BF16)
    half = grads_ref.shape[0] // 2
    keep_ref[:half, :] = grads_ref[pl.ds(pl.multiple_of(odd * half, ROW_TILE), half), :]
    send_ref[:half, :] = grads_ref[pl.ds(pl.multiple_of((1 - odd) * half, ROW_TILE), half), :]
    bias_rows = two_rows(bias1, ROW_TILE)
    keep_ref[half : half + ROW_TILE, :] = bias_rows
    send_ref[half : half + ROW_TILE, :] = bias_rows
    base = half + ROW_TILE
    send_ref[base : base + rim, :] = jnp.where(odd == 1, low, high)
    send_ref[base + rim :, :] = jnp.where(odd == 1, high, low)


def two_rows(value, count):
    high = value.astype(BF16).astype(F32)
    row = lax.broadcasted_iota(jnp.int32, (count, value.shape[1]), 0)
    return jnp.where(row == 0, high, jnp.where(row == 1, value - high, 0.0)).astype(BF16)


def tail_spots(rows, chips, rim):
    share = -(-rim // chips)
    chip = rows >> (share.bit_length() - 1)
    return 8 * chip + 4 + rows - share * chip, share


def pair_kernel(keep_ref, came_ref, made_ref, blocks_ref):
    half = keep_ref.shape[0] - ROW_TILE
    chips, _, lanes = blocks_ref.shape
    rows = half // chips
    rim = (came_ref.shape[0] - half - ROW_TILE) // 2
    bias = keep_ref[half:, :].astype(F32) + came_ref[half : half + ROW_TILE, :].astype(F32)
    bias = jnp.sum(bias, 0, keepdims=True)
    far = came_ref[half + ROW_TILE + rim :, :]
    spot, share = tail_spots(lax.broadcasted_iota(jnp.int32, (8 * chips, rim), 1), chips, rim)
    row = lax.broadcasted_iota(jnp.int32, (8 * chips, rim), 0)
    line = lax.broadcasted_iota(jnp.int32, (8, lanes), 0)
    tails = jnp.zeros((8 * chips, lanes), F32)
    bias_tail = jnp.zeros((8, lanes), F32)
    for side in range(2):
        span = slice(side * lanes, (side + 1) * lanes)
        pick = jnp.where(row == spot + side * share, 1.0, 0.0).astype(BF16)
        tails = tails + dot(pick, far[:, span])
        value = bias[:, span]
        high = value.astype(BF16).astype(F32)
        bias_tail = jnp.where(line == 2 * side, high, bias_tail)
        bias_tail = jnp.where(line == 2 * side + 1, value - high, bias_tail)
    for chip in range(chips):
        span = slice(chip * rows, (chip + 1) * rows)
        total = (keep_ref[span, :].astype(F32) + came_ref[span, :].astype(F32)).astype(BF16)
        blocks_ref[chip, :rows, :] = total[:, :lanes]
        blocks_ref[chip, rows : 2 * rows, :] = total[:, lanes:]
        blocks_ref[chip, 2 * rows :, :] = (tails[8 * chip : 8 * chip + 8] + bias_tail).astype(BF16)


def sum_kernel(blocks_ref, part_ref, bias1_ref):
    _, odd, _ = place()
    chips, depth, lanes = blocks_ref.shape
    rows = depth - 8
    total = blocks_ref[0].astype(F32)
    for other in range(1, chips):
        total = total + blocks_ref[other].astype(F32)
    part = total[:rows].astype(BF16)
    for other in range(chips):
        after = blocks_ref[min(other + 1, chips - 1), rows:, :]
        before = blocks_ref[max(other - 1, 0), rows:, :]
        part_ref[other, :rows, :] = part
        part_ref[other, rows:, :] = jnp.where(odd == 1, after, before)
    for side in range(2):
        row = rows + 2 * side
        bias1_ref[:, side * lanes : (side + 1) * lanes] = jnp.sum(
            total[row : row + 2], 0, keepdims=True
        )


def coarse_kernel(
    coarse_ref,
    parent_ref,
    into2_ref,
    message2_ref,
    grad_src2_ref,
    grad_dst2_ref,
    coarse_grads_ref,
    coarse_sum_ref,
):
    coarse = coarse_ref[...]
    coarse_sum = dot_nt(into2_ref[...], message2_ref[...]).astype(BF16)
    coarse_sum_ref[...] = coarse_sum
    coarse_grads_ref[0] = dot_tn(coarse, grad_src2_ref[...])
    coarse_grads_ref[1] = dot_tn(coarse, grad_dst2_ref[...])
    coarse_grads_ref[2] = dot_tn(coarse_sum, parent_ref[...])


def finish_kernel(
    coarse_weights_ref,
    weights_ref,
    coarse_ref,
    coarse_sum_ref,
    updated_ref,
    family_ref,
    grad_updated_ref,
    grad_src_ref,
    grad_dst_ref,
    lists_ref,
    came_ref,
    mine_ref,
    bias1_ref,
    bias2_ref,
    coarse_grads_ref,
    moved_ref,
    node_grads_ref,
    bias_ref,
    coarse_grads_hbm,
    sems,
):
    copy = pltpu.make_async_copy(coarse_grads_ref, coarse_grads_hbm, sems.at[0])
    copy.start()
    bias_ref[0:1, :] = bias1_ref[...]
    bias_ref[1:2, :] = bias2_ref[...]
    me, odd, chip = place()
    node_count = updated_ref.shape[0]
    coarse_count = family_ref.shape[0]
    chips, depth, lanes = mine_ref.shape
    rim = lists_ref.shape[1]
    rows = pl.ds(pl.multiple_of(me * coarse_count, coarse_count), coarse_count)
    coarse_new = coarse_ref[rows, :].astype(F32) + dot(
        coarse_sum_ref[rows, :], coarse_weights_ref[2]
    )
    family = family_ref[...]
    high, low = split(coarse_new)
    moved_ref[...] = updated_ref[...] + dot_tn(family, high) + dot_tn(family, low)
    both = jnp.concatenate([grad_src_ref[rim : rim + node_count, :], grad_dst_ref[...]], 1)
    node_grads_ref[...] = grad_updated_ref[...] + dot_nt(
        both, jnp.concatenate([weights_ref[0], weights_ref[1]], 1)
    )
    lists = lists_ref[...]
    near_list = jnp.where(odd == 1, lists[0:1], lists[1:2])
    far_list = jnp.where(odd == 1, lists[1:2], lists[0:1])
    inside = jnp.logical_or(jnp.logical_and(odd == 1, chip < chips - 1), jnp.logical_and(odd == 0, chip > 0))
    far_list = jnp.where(inside, far_list, -1)
    near = came_ref[came_ref.shape[0] - 2 * rim : came_ref.shape[0] - rim, :]
    node_grads_ref[...] += dot(one_hot_rows(near_list, node_count), near)
    tails = [mine_ref[other, depth - 8 :, :].astype(F32) for other in range(chips)]
    tails = jnp.concatenate(tails, 0).astype(BF16)
    spot, share = tail_spots(lax.broadcasted_iota(jnp.int32, (rim, 8 * chips), 0), chips, rim)
    column_spot = lax.broadcasted_iota(jnp.int32, (rim, 8 * chips), 1)
    into = one_hot_rows(far_list, node_count)
    for side in range(2):
        pick = jnp.where(column_spot == spot + side * share, 1.0, 0.0).astype(BF16)
        far = dot(pick, tails).astype(BF16)
        node_grads_ref[:, side * lanes : (side + 1) * lanes] += dot(into, far)
    copy.wait()


def join_kernel(
    mine_ref,
    theirs_ref,
    moved_ref,
    node_grads_ref,
    bias_ref,
    out_hbm,
    moved_hbm,
    node_grads_hbm,
    bias_hbm,
    out_ref,
    sems,
):
    ready = (
        (bias_ref, bias_hbm),
        (moved_ref, moved_hbm),
        (node_grads_ref, node_grads_hbm),
    )
    copies = [
        pltpu.make_async_copy(source, target, sems.at[spot])
        for spot, (source, target) in enumerate(ready)
    ]
    for copy in copies:
        copy.start()
    _, odd, _ = place()
    chips, depth, lanes = mine_ref.shape
    rows = (depth - 8) // 2
    limit = out_ref.shape[0]
    pieces = 0
    done = 0
    for block in range(2 * chips):
        core, chip = divmod(block, chips)
        start = block * rows
        count = min(rows, limit - start)
        if count <= 0:
            break
        for side in range(2):
            span = slice(side * rows, side * rows + count)
            mine = mine_ref[chip, span, :]
            theirs = theirs_ref[chip, span, :]
            out_ref[start : start + count, side * lanes : (side + 1) * lanes] = jnp.where(
                odd == core, mine, theirs
            ).astype(F32)
        end = start + count
        if end == limit or end >= (pieces + 1) * limit // JOIN_COPIES:
            pieces += 1
            span = pl.ds(done, end - done)
            copies.append(
                pltpu.make_async_copy(
                    out_ref.at[span, :], out_hbm.at[span, :], sems.at[len(copies)]
                )
            )
            copies[-1].start()
            done = end
    for copy in copies:
        copy.wait()


def call(
    kernel, outs, args, room, scratch=(), scalars=(), outside=(), copies=0, flops=0, outgoing=()
):
    vmem = pl.BlockSpec(memory_space=pltpu.VMEM)
    scalar = pl.BlockSpec(memory_space=pltpu.SMEM)
    hbm = pl.BlockSpec(memory_space=pltpu.HBM)
    specs = [
        scalar if spot in scalars else hbm if spot in outside else vmem for spot in range(len(args))
    ]
    args = [
        pltpu.with_memory_space_constraint(value, pltpu.HBM) if spot in outside else value
        for spot, value in enumerate(args)
    ]
    moved = sum(value.size * value.dtype.itemsize for value in args)
    moved += sum(math.prod(shape) * jnp.dtype(kind).itemsize for shape, kind in outs)
    scratch = [pltpu.VMEM(shape, kind) for shape, kind in scratch]
    if copies:
        scratch.append(pltpu.SemaphoreType.DMA((copies,)))
    return pl.pallas_call(
        kernel,
        out_shape=[jax.ShapeDtypeStruct(shape, kind) for shape, kind in outs],
        in_specs=specs,
        out_specs=[hbm if spot in outgoing else vmem for spot in range(len(outs))],
        scratch_shapes=scratch,
        compiler_params=pltpu.CompilerParams(vmem_limit_bytes=room * MIB),
        cost_estimate=pl.CostEstimate(flops=flops, bytes_accessed=moved, transcendentals=0),
    )(*args)


def round_up(value, unit):
    return -(-value // unit) * unit


def shards(
    nodes,
    cotangent,
    fine_weights,
    coarse_weights,
    biases,
    send_lists,
    edge_ends,
    live_blocks,
    pool_members,
    parents,
    coarse_ends,
):
    ndom = lax.axis_size("dom")
    chips = ndom // 2
    node_count, width = nodes.shape
    rim = send_lists.shape[1]
    member_count, coarse_count = pool_members.shape
    slots = edge_ends.shape[1]
    edge_count2 = coarse_ends.shape[1] * ndom
    total = coarse_count * ndom
    parents = parents.reshape(1, node_count)
    pairs = [(i, i ^ 1) for i in range(ndom)]
    across = [(i, i + 1) for i in range(1, ndom - 1, 2)]
    across = across + [(target, source) for source, target in across]
    same_core = [[2 * chip + core for chip in range(chips)] for core in range(2)]

    def swap(value):
        return lax.ppermute(value, "dom", pairs)

    def exchange(value):
        return lax.all_to_all(value, "dom", 0, 0, axis_index_groups=same_core)

    rim_rows = ((rim, width), BF16)
    square = ((width, width), BF16)
    inputs = (
        nodes,
        send_lists,
        fine_weights,
        edge_ends,
        cotangent,
        biases,
        pool_members,
        parents,
        coarse_ends,
    )
    (
        near,
        far,
        nodes,
        lists,
        fine,
        edge_ends,
        upstream,
        own_biases,
        pool_members,
        parents,
        coarse_ends,
    ) = call(
        pick_kernel,
        [rim_rows, ((4 * rim, width), BF16)] + [(value.shape, value.dtype) for value in inputs],
        inputs,
        4,
        outside=range(len(inputs)),
        copies=len(inputs),
    )
    far = lax.ppermute(far, "dom", across)
    near = swap(near)

    lanes = width // 2
    side_rows = 2 * coarse_count + 8
    pre, outof, into, share, family, side, upright, pooled = call(
        functools.partial(prepare_kernel, rim),
        [
            ((width, slots), F32),
            ((node_count + 2 * rim, slots), BF16),
            ((node_count, slots), BF16),
            ((node_count, coarse_count), BF16),
            ((coarse_count, node_count), BF16),
            ((side_rows, lanes), BF16),
            square,
            ((coarse_count, width), F32),
        ],
        (
            nodes,
            fine,
            own_biases,
            edge_ends,
            live_blocks,
            pool_members,
            parents,
            upstream,
            coarse_ends,
        ),
        10,
        scratch=[((8, lanes), F32)],
        scalars=(4,),
        flops=2 * slots * width * (2 * node_count + 2 * rim),
    )
    summed, slopes, packet = call(
        functools.partial(forward_kernel, member_count),
        [
            ((node_count, width), BF16),
            ((width, slots), BF16),
            ((chips, 2 * coarse_count + side_rows, lanes), BF16),
        ],
        (near, far, upright, fine, pre, outof, into, share, pooled, side),
        10,
    )
    mine = exchange(packet)
    edges2 = edge_count2 // 2
    slopes_sum, updated, upright2, repeat, block, ends2 = call(
        functools.partial(between_kernel, coarse_ends.shape[1]),
        [
            ((node_count, width), F32),
            ((node_count, width), F32),
            ((2, width, width), BF16),
            ((lanes, edges2), BF16),
            ((8 * chips, edges2), F32),
            ((2, edges2), jnp.int32),
        ],
        (mine, into, slopes, nodes, summed, fine, coarse_weights),
        8,
        flops=2 * slots * width * node_count,
    )
    theirs = swap(mine)

    rows = round_up(-(-3 * width // ndom), ROW_TILE)
    half = rows * chips
    coarse_whole = ((total, width), BF16)
    (
        send,
        keep,
        coarse,
        parent_all,
        into2,
        message2,
        grad_src2,
        grad_dst2,
        bias2,
        grad_updated,
        grad_src,
        grad_dst,
    ) = call(
        functools.partial(backward_kernel, ndom, member_count),
        [
            ((half + ROW_TILE + 2 * rim, width), BF16),
            ((half + ROW_TILE, width), BF16),
            coarse_whole,
            coarse_whole,
            ((total, edge_count2), BF16),
            ((width, edge_count2), BF16),
            coarse_whole,
            coarse_whole,
            ((1, width), F32),
            ((node_count, width), F32),
            ((node_count + 2 * rim, width), BF16),
            ((node_count, width), BF16),
        ],
        (
            mine,
            theirs,
            coarse_weights,
            upright2,
            repeat,
            block,
            ends2,
            own_biases,
            nodes,
            near,
            far,
            fine,
            share,
            upstream,
            summed,
            slopes_sum,
            slopes,
            outof,
            into,
        ),
        20 if total <= 256 else 48,
        scratch=[
            ((width, edge_count2), BF16),
            ((width, edge_count2), BF16),
            ((total, edge_count2), BF16),
            ((2 * half, width), BF16),
        ],
    )
    came = swap(send)
    coarse_grads, coarse_sum = call(
        coarse_kernel,
        [((3, width, width), F32), coarse_whole],
        (coarse, parent_all, into2, message2, grad_src2, grad_dst2),
        8 if total <= 256 else 24,
        flops=6 * total * width * width,
    )
    packet = ((chips, 2 * rows + 8, lanes), BF16)
    (blocks,) = call(pair_kernel, [packet], (keep, came, coarse_sum), 4)
    blocks = exchange(blocks)
    part, bias1 = call(sum_kernel, [packet, ((1, width), F32)], (blocks,), 4)
    mine = exchange(part)
    coarse_grads_shape = ((3, width, width), F32)
    node_shape = ((node_count, width), F32)
    bias_shape = ((2, width), F32)
    moved, node_grads, bias_grads, coarse_grads = call(
        finish_kernel,
        [node_shape, node_shape, bias_shape, coarse_grads_shape],
        (
            coarse_weights,
            fine,
            coarse,
            coarse_sum,
            updated,
            family,
            grad_updated,
            grad_src,
            grad_dst,
            lists,
            came,
            mine,
            bias1,
            bias2,
            coarse_grads,
        ),
        8,
        copies=1,
        outgoing=(3,),
        flops=8 * node_count * width * width,
    )
    theirs = swap(mine)
    fine_grads, moved, node_grads, bias_grads = call(
        join_kernel,
        [((3 * width, width), F32), node_shape, node_shape, bias_shape],
        (mine, theirs, moved, node_grads, bias_grads),
        4,
        scratch=[((3 * width, width), F32)],
        copies=3 + JOIN_COPIES,
        outgoing=range(4),
    )
    return moved, node_grads, fine_grads.reshape(3, width, width), coarse_grads, bias_grads


def solution(mesh):
    return jax.shard_map(
        shards,
        mesh=mesh,
        in_specs=(
            P(("groups", "dom"), None),
            P(("groups", "dom"), None),
            P(),
            P(),
            P(),
            P("groups", "dom"),
            P("groups", "dom"),
            P(("groups", "dom")),
            P("groups", "dom"),
            P(("groups", "dom")),
            P("groups", "dom"),
        ),
        out_specs=(
            P(("groups", "dom"), None),
            P(("groups", "dom"), None),
            P("groups", None, None),
            P("groups", None, None),
            P("groups", None),
        ),
        check_vma=False,
    )
```

```python
import functools
import math

import jax
import jax.numpy as jnp
from jax import lax
from jax.experimental import pallas as pl
from jax.experimental.pallas import tpu as pltpu
from jax.sharding import PartitionSpec as P

BF16 = jnp.bfloat16
F32 = jnp.float32
EDGE_BLOCK = 128
ROW_TILE = 16
MIB = 1024 * 1024
JOIN_COPIES = 4


def dot(left, right):
    return jnp.dot(left, right, preferred_element_type=F32)


def dot_tn(left, right):
    return lax.dot_general(left, right, (((0,), (0,)), ((), ())), preferred_element_type=F32)


def dot_nt(left, right):
    return lax.dot_general(left, right, (((1,), (1,)), ((), ())), preferred_element_type=F32)


def split(value):
    high = value.astype(BF16)
    return high, (value - high.astype(F32)).astype(BF16)


def one_hot_rows(index_row, count):
    spots = lax.broadcasted_iota(jnp.int32, (count, index_row.shape[1]), 0)
    return jnp.where(spots == index_row, 1.0, 0.0).astype(BF16)


def column(row, lanes):
    upright = jnp.transpose(jnp.broadcast_to(row, (8, row.shape[1])))[:, :1]
    return jnp.broadcast_to(upright, (row.shape[1], lanes))


def silu_and_slope(value):
    sig = 0.5 * jnp.tanh(0.5 * value) + 0.5
    message = value * sig
    return message, sig + message * (1.0 - sig)


def membership(members, node_count):
    spots = lax.broadcasted_iota(jnp.int32, (node_count, members.shape[1]), 0)
    total = jnp.zeros(spots.shape, F32)
    for row in range(members.shape[0]):
        total = total + jnp.where(spots == members[row : row + 1], 1.0, 0.0)
    return total.astype(BF16)


def place():
    me = lax.axis_index("dom")
    return me, lax.rem(me, 2), lax.div(me, 2)


def live_rows(ends_ref, live_ref, row):
    index = ends_ref[row : row + 1, :]
    slot = lax.broadcasted_iota(jnp.int32, index.shape, 1)
    return jnp.where(slot < live_ref[0] * EDGE_BLOCK, index, -1)


def pick_kernel(*refs):
    count = (len(refs) - 3) // 2
    inputs, (near_ref, far_ref), outputs = refs[:count], refs[count : count + 2], refs[count + 2 : -1]
    copies = [
        pltpu.make_async_copy(source, target, refs[-1].at[spot])
        for spot, (source, target) in enumerate(zip(inputs, outputs, strict=True))
    ]
    for copy in copies:
        copy.start()
    for copy in copies[:2]:
        copy.wait()
    _, odd, _ = place()
    lists = outputs[1][...]
    near = jnp.where(odd == 1, lists[0:1], lists[1:2])
    far = jnp.where(odd == 1, lists[1:2], lists[0:1])
    nodes = outputs[0][...]
    rim = near_ref.shape[0]
    near_ref[...] = dot_tn(one_hot_rows(near, nodes.shape[0]), nodes).astype(BF16)
    far = dot_tn(one_hot_rows(far, nodes.shape[0]), nodes).astype(BF16)
    for start in range(0, far_ref.shape[0], rim):
        far_ref[start : start + rim, :] = far
    for copy in copies[2:]:
        copy.wait()


def rims(near_ref, far_ref, odd):
    near = near_ref[...]
    far = far_ref[: near.shape[0], :]
    return jnp.where(odd == 1, near, far), jnp.where(odd == 1, far, near)


def prepare_kernel(
    rim,
    nodes_ref,
    weights_ref,
    biases_ref,
    ends_ref,
    live_ref,
    members_ref,
    parents_ref,
    cotangent_ref,
    links_ref,
    pre_ref,
    outof_ref,
    into_ref,
    share_ref,
    family_ref,
    side_ref,
    upright_ref,
    pooled_ref,
    link_ref,
):
    node_count, width = nodes_ref.shape
    coarse_count = family_ref.shape[0]
    slots = ends_ref.shape[1]
    lanes = link_ref.shape[1]
    outof_ref[...] = one_hot_rows(live_rows(ends_ref, live_ref, 0), node_count + 2 * rim)
    into_ref[...] = one_hot_rows(live_rows(ends_ref, live_ref, 1), node_count)
    nodes = nodes_ref[...]
    src_proj = jnp.transpose(dot(nodes, weights_ref[0])).astype(BF16)
    dst_proj = jnp.transpose(dot(nodes, weights_ref[1])).astype(BF16)
    chunk = 2 * EDGE_BLOCK
    bias = column(biases_ref[0:1, :], chunk)
    for start in range(0, slots, chunk):
        span = slice(start, start + chunk)
        pre_ref[:, span] = (
            dot(src_proj, outof_ref[rim : rim + node_count, span])
            + dot(dst_proj, into_ref[:, span])
            + bias
        )
    upright_ref[...] = jnp.transpose(weights_ref[0].astype(F32)).astype(BF16)
    share = membership(members_ref[...], node_count)
    share_ref[...] = share
    pooled_ref[...] = dot_tn(share, nodes)
    family = one_hot_rows(parents_ref[...], coarse_count)
    family_ref[...] = family
    parent_grad = dot(family, cotangent_ref[...]).astype(BF16)
    side_ref[:coarse_count, :] = parent_grad[:, :lanes]
    side_ref[coarse_count : 2 * coarse_count, :] = parent_grad[:, lanes:]

    links = links_ref[...]
    own = links.shape[1]
    link_ref[...] = jnp.zeros(link_ref.shape, F32)
    link_ref[0:2, :own] = (links >> 8).astype(F32)
    link_ref[2:4, :own] = (links & 255).astype(F32)
    side_ref[2 * coarse_count :, :] = link_ref[...].astype(BF16)


def forward_kernel(
    member_count,
    near_ref,
    far_ref,
    upright_ref,
    weights_ref,
    pre_ref,
    outof_ref,
    into_ref,
    share_ref,
    pooled_ref,
    side_ref,
    summed_ref,
    slopes_ref,
    packet_ref,
):
    _, odd, _ = place()
    low, high = rims(near_ref, far_ref, odd)
    rim = low.shape[0]
    node_count = into_ref.shape[0]
    rim_proj = dot_nt(upright_ref[...], jnp.concatenate([low, high], 0)).astype(BF16)
    slots = pre_ref.shape[1]
    chunk = 2 * EDGE_BLOCK
    summed = jnp.zeros((node_count, pre_ref.shape[0]), F32)
    for start in range(0, slots, chunk):
        span = slice(start, start + chunk)
        at_rim = jnp.concatenate([outof_ref[:rim, span], outof_ref[rim + node_count :, span]], 0)
        message, slope = silu_and_slope(pre_ref[:, span] + dot(rim_proj, at_rim))
        summed = summed + dot_nt(into_ref[:, span], message.astype(BF16))
        slopes_ref[:, span] = slope.astype(BF16)
    summed = summed.astype(BF16)
    summed_ref[...] = summed
    high, low = split(dot_tn(share_ref[...], summed))
    pooled = pooled_ref[...] + dot(high, weights_ref[2]) + dot(low, weights_ref[2])
    coarse = (pooled / member_count).astype(BF16)
    count = coarse.shape[0]
    lanes = packet_ref.shape[2]
    side = side_ref[...]
    for chip in range(packet_ref.shape[0]):
        packet_ref[chip, :count, :] = coarse[:, :lanes]
        packet_ref[chip, count : 2 * count, :] = coarse[:, lanes:]
        packet_ref[chip, 2 * count :, :] = side


def edge_ends2(packet_ref, repeat_ref, block_ref):
    links = [packet_ref[chip, packet_ref.shape[1] - 8 :, :] for chip in range(packet_ref.shape[0])]
    links = jnp.concatenate([link.astype(F32) for link in links], 0).astype(BF16)
    code = dot(links, repeat_ref[...]) * block_ref[...]
    code = jnp.sum(code.reshape(packet_ref.shape[0], 8, code.shape[1]), 0)
    return (256.0 * code[0:2] + code[2:4]).astype(jnp.int32)


def between_kernel(
    own,
    mine_ref,
    into_ref,
    slopes_ref,
    nodes_ref,
    summed_ref,
    weights_ref,
    coarse_weights_ref,
    slopes_sum_ref,
    updated_ref,
    upright2_ref,
    repeat_ref,
    block_ref,
    ends2_ref,
):
    edge = lax.broadcasted_iota(jnp.int32, repeat_ref.shape, 1)
    owner = ((edge.astype(F32) + 0.5) * (1.0 / own)).astype(jnp.int32)
    spot = lax.broadcasted_iota(jnp.int32, repeat_ref.shape, 0)
    repeat_ref[...] = jnp.where(edge - own * owner == spot, 1.0, 0.0).astype(BF16)
    edge = lax.broadcasted_iota(jnp.int32, block_ref.shape, 1)
    owner = ((edge.astype(F32) + 0.5) * (1.0 / own)).astype(jnp.int32)
    block = lax.broadcasted_iota(jnp.int32, block_ref.shape, 0) >> 3
    block_ref[...] = jnp.where(block == owner, 1.0, 0.0)
    ends2_ref[...] = edge_ends2(mine_ref, repeat_ref, block_ref)
    for spot in range(2):
        upright2_ref[spot] = jnp.transpose(coarse_weights_ref[spot].astype(F32)).astype(BF16)
    slopes_sum_ref[...] = dot_nt(into_ref[...], slopes_ref[...])
    updated_ref[...] = nodes_ref[...].astype(F32) + dot(summed_ref[...], weights_ref[2])


def ordered(mine_ref, theirs_ref, odd, start, count):
    blocks = []
    for chip in range(mine_ref.shape[0]):
        halves = []
        for half in range(2):
            span = slice(start + half * count, start + (half + 1) * count)
            mine = mine_ref[chip, span, :]
            theirs = theirs_ref[chip, span, :]
            halves.append((jnp.where(odd == 1, theirs, mine), jnp.where(odd == 1, mine, theirs)))
        for core in range(2):
            blocks.append(jnp.concatenate([halves[0][core], halves[1][core]], 1))
    return jnp.concatenate(blocks, 0)


def backward_kernel(
    ndom,
    member_count,
    mine_ref,
    theirs_ref,
    coarse_weights_ref,
    upright2_ref,
    repeat_ref,
    block_ref,
    ends2_ref,
    biases_ref,
    nodes_ref,
    near_ref,
    far_ref,
    weights_ref,
    share_ref,
    cotangent_ref,
    summed_ref,
    slopes_sum_ref,
    slopes_ref,
    outof_ref,
    into_ref,
    send_ref,
    keep_ref,
    coarse_ref,
    parent_ref,
    into2_ref,
    message2_ref,
    grad_src2_ref,
    grad_dst2_ref,
    bias2_ref,
    grad_updated_ref,
    grad_src_ref,
    grad_dst_ref,
    slope2_ref,
    edge2_ref,
    outof2_ref,
    grads_ref,
):
    me, odd, _ = place()
    nodes = nodes_ref[...]
    node_count, width = nodes.shape
    coarse_count = share_ref.shape[1]
    total = ndom * coarse_count

    coarse = ordered(mine_ref, theirs_ref, odd, 0, coarse_count)
    parent_all = ordered(mine_ref, theirs_ref, odd, 2 * coarse_count, coarse_count)
    ends2 = jnp.concatenate([ends2_ref[...], edge_ends2(theirs_ref, repeat_ref, block_ref)], 1)
    src2 = dot_nt(upright2_ref[0], coarse).astype(BF16)
    dst2 = dot_nt(upright2_ref[1], coarse).astype(BF16)
    grad_agg2 = dot_nt(parent_all, coarse_weights_ref[2])
    grad_agg2_near = dot_nt(coarse_weights_ref[2], parent_all).astype(BF16)
    bias = column(biases_ref[1:2, :], width)
    step = width
    for start in range(0, message2_ref.shape[1], step):
        span = slice(start, start + step)
        outof = one_hot_rows(ends2[0:1, span], total)
        into = one_hot_rows(ends2[1:2, span], total)
        outof2_ref[:, span] = outof
        into2_ref[:, span] = into
        message, slope = silu_and_slope(dot(src2, outof) + dot(dst2, into) + bias)
        message2_ref[:, span] = message.astype(BF16)
        slope2_ref[:, span] = slope.astype(BF16)
        edge2_ref[:, span] = (dot(grad_agg2_near, into) * slope).astype(BF16)
    grad_dst2 = dot_nt(into2_ref[...], slope2_ref[...]) * grad_agg2
    grad_src2 = dot_nt(outof2_ref[...], edge2_ref[...])
    bias2_ref[...] = jnp.sum(grad_dst2, 0, keepdims=True)
    grad_src2_ref[...] = grad_src2.astype(BF16)
    grad_dst2_ref[...] = grad_dst2.astype(BF16)
    coarse_ref[...] = coarse
    parent_ref[...] = parent_all

    rows = pl.ds(pl.multiple_of(me * coarse_count, coarse_count), coarse_count)
    coarse_grad = (
        parent_ref[rows, :].astype(F32)
        + dot_nt(grad_src2_ref[rows, :], coarse_weights_ref[0])
        + dot_nt(grad_dst2_ref[rows, :], coarse_weights_ref[1])
    )
    share = share_ref[...]
    high, low = split(coarse_grad / member_count)
    grad_updated = cotangent_ref[...].astype(F32) + dot(share, high) + dot(share, low)
    grad_updated_ref[...] = grad_updated

    low, high = rims(near_ref, far_ref, odd)
    extended = jnp.concatenate([low, nodes, high], 0)
    rim = low.shape[0]
    slots = slopes_ref.shape[1]
    grad_updated_near = grad_updated.astype(BF16)
    grad_dst = slopes_sum_ref[...] * dot_nt(grad_updated_near, weights_ref[2])
    grad_summed = dot_nt(weights_ref[2], grad_updated_near).astype(BF16)
    bias1 = jnp.sum(grad_dst, 0, keepdims=True)
    grad_dst = grad_dst.astype(BF16)
    grads_ref[width : 2 * width, :] = dot_tn(nodes, grad_dst).astype(BF16)
    grads_ref[2 * width : 3 * width, :] = dot_tn(summed_ref[...], grad_updated_near).astype(BF16)
    chunk = 2 * EDGE_BLOCK
    grad_src = jnp.zeros((outof_ref.shape[0], width), F32)
    for start in range(0, slots, chunk):
        span = slice(start, start + chunk)
        slope = slopes_ref[:, span].astype(F32)
        edge = (dot(grad_summed, into_ref[:, span]) * slope).astype(BF16)
        grad_src = grad_src + dot_nt(outof_ref[:, span], edge)
    grad_src = grad_src.astype(BF16)
    grad_src_ref[...] = grad_src
    grad_dst_ref[...] = grad_dst
    low = dot_nt(grad_src[:rim], weights_ref[0]).astype(BF16)
    high = dot_nt(grad_src[rim + node_count :], weights_ref[0]).astype(BF16)
    grads_ref[0:width, :] = dot_tn(extended, grad_src).astype(BF16)
    if grads_ref.shape[0] > 3 * width:
        grads_ref[3 * width :, :] = jnp.zeros((grads_ref.shape[0] - 3 * width, width), BF16)
    half = grads_ref.shape[0] // 2
    keep_ref[:half, :] = grads_ref[pl.ds(pl.multiple_of(odd * half, ROW_TILE), half), :]
    send_ref[:half, :] = grads_ref[pl.ds(pl.multiple_of((1 - odd) * half, ROW_TILE), half), :]
    bias_rows = two_rows(bias1, ROW_TILE)
    keep_ref[half : half + ROW_TILE, :] = bias_rows
    send_ref[half : half + ROW_TILE, :] = bias_rows
    base = half + ROW_TILE
    send_ref[base : base + rim, :] = jnp.where(odd == 1, low, high)
    send_ref[base + rim :, :] = jnp.where(odd == 1, high, low)


def two_rows(value, count):
    high = value.astype(BF16).astype(F32)
    row = lax.broadcasted_iota(jnp.int32, (count, value.shape[1]), 0)
    return jnp.where(row == 0, high, jnp.where(row == 1, value - high, 0.0)).astype(BF16)


def tail_spots(rows, chips, rim):
    share = -(-rim // chips)
    chip = rows >> (share.bit_length() - 1)
    return 8 * chip + 4 + rows - share * chip, share


def pair_kernel(keep_ref, came_ref, made_ref, blocks_ref):
    half = keep_ref.shape[0] - ROW_TILE
    chips, _, lanes = blocks_ref.shape
    rows = half // chips
    rim = (came_ref.shape[0] - half - ROW_TILE) // 2
    bias = keep_ref[half:, :].astype(F32) + came_ref[half : half + ROW_TILE, :].astype(F32)
    bias = jnp.sum(bias, 0, keepdims=True)
    far = came_ref[half + ROW_TILE + rim :, :]
    spot, share = tail_spots(lax.broadcasted_iota(jnp.int32, (8 * chips, rim), 1), chips, rim)
    row = lax.broadcasted_iota(jnp.int32, (8 * chips, rim), 0)
    line = lax.broadcasted_iota(jnp.int32, (8, lanes), 0)
    tails = jnp.zeros((8 * chips, lanes), F32)
    bias_tail = jnp.zeros((8, lanes), F32)
    for side in range(2):
        span = slice(side * lanes, (side + 1) * lanes)
        pick = jnp.where(row == spot + side * share, 1.0, 0.0).astype(BF16)
        tails = tails + dot(pick, far[:, span])
        value = bias[:, span]
        high = value.astype(BF16).astype(F32)
        bias_tail = jnp.where(line == 2 * side, high, bias_tail)
        bias_tail = jnp.where(line == 2 * side + 1, value - high, bias_tail)
    for chip in range(chips):
        span = slice(chip * rows, (chip + 1) * rows)
        total = (keep_ref[span, :].astype(F32) + came_ref[span, :].astype(F32)).astype(BF16)
        blocks_ref[chip, :rows, :] = total[:, :lanes]
        blocks_ref[chip, rows : 2 * rows, :] = total[:, lanes:]
        blocks_ref[chip, 2 * rows :, :] = (tails[8 * chip : 8 * chip + 8] + bias_tail).astype(BF16)


def sum_kernel(blocks_ref, part_ref, bias1_ref):
    _, odd, _ = place()
    chips, depth, lanes = blocks_ref.shape
    rows = depth - 8
    total = blocks_ref[0].astype(F32)
    for other in range(1, chips):
        total = total + blocks_ref[other].astype(F32)
    part = total[:rows].astype(BF16)
    for other in range(chips):
        after = blocks_ref[min(other + 1, chips - 1), rows:, :]
        before = blocks_ref[max(other - 1, 0), rows:, :]
        part_ref[other, :rows, :] = part
        part_ref[other, rows:, :] = jnp.where(odd == 1, after, before)
    for side in range(2):
        row = rows + 2 * side
        bias1_ref[:, side * lanes : (side + 1) * lanes] = jnp.sum(
            total[row : row + 2], 0, keepdims=True
        )


def coarse_kernel(
    coarse_ref,
    parent_ref,
    into2_ref,
    message2_ref,
    grad_src2_ref,
    grad_dst2_ref,
    coarse_grads_ref,
    coarse_sum_ref,
):
    coarse = coarse_ref[...]
    coarse_sum = dot_nt(into2_ref[...], message2_ref[...]).astype(BF16)
    coarse_sum_ref[...] = coarse_sum
    coarse_grads_ref[0] = dot_tn(coarse, grad_src2_ref[...])
    coarse_grads_ref[1] = dot_tn(coarse, grad_dst2_ref[...])
    coarse_grads_ref[2] = dot_tn(coarse_sum, parent_ref[...])


def finish_kernel(
    coarse_weights_ref,
    weights_ref,
    coarse_ref,
    coarse_sum_ref,
    updated_ref,
    family_ref,
    grad_updated_ref,
    grad_src_ref,
    grad_dst_ref,
    lists_ref,
    came_ref,
    mine_ref,
    bias1_ref,
    bias2_ref,
    coarse_grads_ref,
    moved_ref,
    node_grads_ref,
    bias_ref,
    coarse_grads_hbm,
    sems,
):
    copy = pltpu.make_async_copy(coarse_grads_ref, coarse_grads_hbm, sems.at[0])
    copy.start()
    bias_ref[0:1, :] = bias1_ref[...]
    bias_ref[1:2, :] = bias2_ref[...]
    me, odd, chip = place()
    node_count = updated_ref.shape[0]
    coarse_count = family_ref.shape[0]
    chips, depth, lanes = mine_ref.shape
    rim = lists_ref.shape[1]
    rows = pl.ds(pl.multiple_of(me * coarse_count, coarse_count), coarse_count)
    coarse_new = coarse_ref[rows, :].astype(F32) + dot(
        coarse_sum_ref[rows, :], coarse_weights_ref[2]
    )
    family = family_ref[...]
    high, low = split(coarse_new)
    moved_ref[...] = updated_ref[...] + dot_tn(family, high) + dot_tn(family, low)
    both = jnp.concatenate([grad_src_ref[rim : rim + node_count, :], grad_dst_ref[...]], 1)
    node_grads_ref[...] = grad_updated_ref[...] + dot_nt(
        both, jnp.concatenate([weights_ref[0], weights_ref[1]], 1)
    )
    lists = lists_ref[...]
    near_list = jnp.where(odd == 1, lists[0:1], lists[1:2])
    far_list = jnp.where(odd == 1, lists[1:2], lists[0:1])
    inside = jnp.logical_or(jnp.logical_and(odd == 1, chip < chips - 1), jnp.logical_and(odd == 0, chip > 0))
    far_list = jnp.where(inside, far_list, -1)
    near = came_ref[came_ref.shape[0] - 2 * rim : came_ref.shape[0] - rim, :]
    node_grads_ref[...] += dot(one_hot_rows(near_list, node_count), near)
    tails = [mine_ref[other, depth - 8 :, :].astype(F32) for other in range(chips)]
    tails = jnp.concatenate(tails, 0).astype(BF16)
    spot, share = tail_spots(lax.broadcasted_iota(jnp.int32, (rim, 8 * chips), 0), chips, rim)
    column_spot = lax.broadcasted_iota(jnp.int32, (rim, 8 * chips), 1)
    into = one_hot_rows(far_list, node_count)
    for side in range(2):
        pick = jnp.where(column_spot == spot + side * share, 1.0, 0.0).astype(BF16)
        far = dot(pick, tails).astype(BF16)
        node_grads_ref[:, side * lanes : (side + 1) * lanes] += dot(into, far)
    copy.wait()


def join_kernel(
    mine_ref,
    theirs_ref,
    moved_ref,
    node_grads_ref,
    bias_ref,
    out_hbm,
    moved_hbm,
    node_grads_hbm,
    bias_hbm,
    out_ref,
    sems,
):
    ready = (
        (bias_ref, bias_hbm),
        (moved_ref, moved_hbm),
        (node_grads_ref, node_grads_hbm),
    )
    copies = [
        pltpu.make_async_copy(source, target, sems.at[spot])
        for spot, (source, target) in enumerate(ready)
    ]
    for copy in copies:
        copy.start()
    _, odd, _ = place()
    chips, depth, lanes = mine_ref.shape
    rows = (depth - 8) // 2
    limit = out_ref.shape[0]
    pieces = 0
    done = 0
    for block in range(2 * chips):
        core, chip = divmod(block, chips)
        start = block * rows
        count = min(rows, limit - start)
        if count <= 0:
            break
        for side in range(2):
            span = slice(side * rows, side * rows + count)
            mine = mine_ref[chip, span, :]
            theirs = theirs_ref[chip, span, :]
            out_ref[start : start + count, side * lanes : (side + 1) * lanes] = jnp.where(
                odd == core, mine, theirs
            ).astype(F32)
        end = start + count
        if end == limit or end >= (pieces + 1) * limit // JOIN_COPIES:
            pieces += 1
            span = pl.ds(done, end - done)
            copies.append(
                pltpu.make_async_copy(
                    out_ref.at[span, :], out_hbm.at[span, :], sems.at[len(copies)]
                )
            )
            copies[-1].start()
            done = end
    for copy in copies:
        copy.wait()


def call(
    kernel, outs, args, room, scratch=(), scalars=(), outside=(), copies=0, flops=0, outgoing=()
):
    vmem = pl.BlockSpec(memory_space=pltpu.VMEM)
    scalar = pl.BlockSpec(memory_space=pltpu.SMEM)
    hbm = pl.BlockSpec(memory_space=pltpu.HBM)
    specs = [
        scalar if spot in scalars else hbm if spot in outside else vmem for spot in range(len(args))
    ]
    args = [
        pltpu.with_memory_space_constraint(value, pltpu.HBM) if spot in outside else value
        for spot, value in enumerate(args)
    ]
    moved = sum(value.size * value.dtype.itemsize for value in args)
    moved += sum(math.prod(shape) * jnp.dtype(kind).itemsize for shape, kind in outs)
    scratch = [pltpu.VMEM(shape, kind) for shape, kind in scratch]
    if copies:
        scratch.append(pltpu.SemaphoreType.DMA((copies,)))
    return pl.pallas_call(
        kernel,
        out_shape=[jax.ShapeDtypeStruct(shape, kind) for shape, kind in outs],
        in_specs=specs,
        out_specs=[hbm if spot in outgoing else vmem for spot in range(len(outs))],
        scratch_shapes=scratch,
        compiler_params=pltpu.CompilerParams(vmem_limit_bytes=room * MIB),
        cost_estimate=pl.CostEstimate(flops=flops, bytes_accessed=moved, transcendentals=0),
    )(*args)


def round_up(value, unit):
    return -(-value // unit) * unit


def shards(
    nodes,
    cotangent,
    fine_weights,
    coarse_weights,
    biases,
    send_lists,
    edge_ends,
    live_blocks,
    pool_members,
    parents,
    coarse_ends,
):
    ndom = lax.axis_size("dom")
    chips = ndom // 2
    node_count, width = nodes.shape
    rim = send_lists.shape[1]
    member_count, coarse_count = pool_members.shape
    slots = edge_ends.shape[1]
    edge_count2 = coarse_ends.shape[1] * ndom
    total = coarse_count * ndom
    parents = parents.reshape(1, node_count)
    pairs = [(i, i ^ 1) for i in range(ndom)]
    across = [(i, i + 1) for i in range(1, ndom - 1, 2)]
    across = across + [(target, source) for source, target in across]
    same_core = [[2 * chip + core for chip in range(chips)] for core in range(2)]

    def swap(value):
        return lax.ppermute(value, "dom", pairs)

    def exchange(value):
        return lax.all_to_all(value, "dom", 0, 0, axis_index_groups=same_core)

    rim_rows = ((rim, width), BF16)
    square = ((width, width), BF16)
    inputs = (
        nodes,
        send_lists,
        fine_weights,
        edge_ends,
        cotangent,
        biases,
        pool_members,
        parents,
        coarse_ends,
    )
    (
        near,
        far,
        nodes,
        lists,
        fine,
        edge_ends,
        upstream,
        own_biases,
        pool_members,
        parents,
        coarse_ends,
    ) = call(
        pick_kernel,
        [rim_rows, ((3 * rim, width), BF16)] + [(value.shape, value.dtype) for value in inputs],
        inputs,
        4,
        outside=range(len(inputs)),
        copies=len(inputs),
    )
    far = lax.ppermute(far, "dom", across)
    near = swap(near)

    lanes = width // 2
    side_rows = 2 * coarse_count + 8
    pre, outof, into, share, family, side, upright, pooled = call(
        functools.partial(prepare_kernel, rim),
        [
            ((width, slots), F32),
            ((node_count + 2 * rim, slots), BF16),
            ((node_count, slots), BF16),
            ((node_count, coarse_count), BF16),
            ((coarse_count, node_count), BF16),
            ((side_rows, lanes), BF16),
            square,
            ((coarse_count, width), F32),
        ],
        (
            nodes,
            fine,
            own_biases,
            edge_ends,
            live_blocks,
            pool_members,
            parents,
            upstream,
            coarse_ends,
        ),
        10,
        scratch=[((8, lanes), F32)],
        scalars=(4,),
        flops=2 * slots * width * (2 * node_count + 2 * rim),
    )
    summed, slopes, packet = call(
        functools.partial(forward_kernel, member_count),
        [
            ((node_count, width), BF16),
            ((width, slots), BF16),
            ((chips, 2 * coarse_count + side_rows, lanes), BF16),
        ],
        (near, far, upright, fine, pre, outof, into, share, pooled, side),
        10,
    )
    mine = exchange(packet)
    edges2 = edge_count2 // 2
    slopes_sum, updated, upright2, repeat, block, ends2 = call(
        functools.partial(between_kernel, coarse_ends.shape[1]),
        [
            ((node_count, width), F32),
            ((node_count, width), F32),
            ((2, width, width), BF16),
            ((lanes, edges2), BF16),
            ((8 * chips, edges2), F32),
            ((2, edges2), jnp.int32),
        ],
        (mine, into, slopes, nodes, summed, fine, coarse_weights),
        8,
        flops=2 * slots * width * node_count,
    )
    theirs = swap(mine)

    rows = round_up(-(-3 * width // ndom), ROW_TILE)
    half = rows * chips
    coarse_whole = ((total, width), BF16)
    (
        send,
        keep,
        coarse,
        parent_all,
        into2,
        message2,
        grad_src2,
        grad_dst2,
        bias2,
        grad_updated,
        grad_src,
        grad_dst,
    ) = call(
        functools.partial(backward_kernel, ndom, member_count),
        [
            ((half + ROW_TILE + 2 * rim, width), BF16),
            ((half + ROW_TILE, width), BF16),
            coarse_whole,
            coarse_whole,
            ((total, edge_count2), BF16),
            ((width, edge_count2), BF16),
            coarse_whole,
            coarse_whole,
            ((1, width), F32),
            ((node_count, width), F32),
            ((node_count + 2 * rim, width), BF16),
            ((node_count, width), BF16),
        ],
        (
            mine,
            theirs,
            coarse_weights,
            upright2,
            repeat,
            block,
            ends2,
            own_biases,
            nodes,
            near,
            far,
            fine,
            share,
            upstream,
            summed,
            slopes_sum,
            slopes,
            outof,
            into,
        ),
        20 if total <= 256 else 48,
        scratch=[
            ((width, edge_count2), BF16),
            ((width, edge_count2), BF16),
            ((total, edge_count2), BF16),
            ((2 * half, width), BF16),
        ],
    )
    came = swap(send)
    coarse_grads, coarse_sum = call(
        coarse_kernel,
        [((3, width, width), F32), coarse_whole],
        (coarse, parent_all, into2, message2, grad_src2, grad_dst2),
        8 if total <= 256 else 24,
        flops=6 * total * width * width,
    )
    packet = ((chips, 2 * rows + 8, lanes), BF16)
    (blocks,) = call(pair_kernel, [packet], (keep, came, coarse_sum), 4)
    blocks = exchange(blocks)
    part, bias1 = call(sum_kernel, [packet, ((1, width), F32)], (blocks,), 4)
    mine = exchange(part)
    coarse_grads_shape = ((3, width, width), F32)
    node_shape = ((node_count, width), F32)
    bias_shape = ((2, width), F32)
    moved, node_grads, bias_grads, coarse_grads = call(
        finish_kernel,
        [node_shape, node_shape, bias_shape, coarse_grads_shape],
        (
            coarse_weights,
            fine,
            coarse,
            coarse_sum,
            updated,
            family,
            grad_updated,
            grad_src,
            grad_dst,
            lists,
            came,
            mine,
            bias1,
            bias2,
            coarse_grads,
        ),
        8,
        copies=1,
        outgoing=(3,),
        flops=8 * node_count * width * width,
    )
    theirs = swap(mine)
    fine_grads, moved, node_grads, bias_grads = call(
        join_kernel,
        [((3 * width, width), F32), node_shape, node_shape, bias_shape],
        (mine, theirs, moved, node_grads, bias_grads),
        4,
        scratch=[((3 * width, width), F32)],
        copies=3 + JOIN_COPIES,
        outgoing=range(4),
    )
    return moved, node_grads, fine_grads.reshape(3, width, width), coarse_grads, bias_grads


def solution(mesh):
    return jax.shard_map(
        shards,
        mesh=mesh,
        in_specs=(
            P(("groups", "dom"), None),
            P(("groups", "dom"), None),
            P(),
            P(),
            P(),
            P("groups", "dom"),
            P("groups", "dom"),
            P(("groups", "dom")),
            P("groups", "dom"),
            P(("groups", "dom")),
            P("groups", "dom"),
        ),
        out_specs=(
            P(("groups", "dom"), None),
            P(("groups", "dom"), None),
            P("groups", None, None),
            P("groups", None, None),
            P("groups", None),
        ),
        check_vma=False,
    )
```

```python
import functools
import math

import jax
import jax.numpy as jnp
from jax import lax
from jax.experimental import pallas as pl
from jax.experimental.pallas import tpu as pltpu
from jax.sharding import PartitionSpec as P

BF16 = jnp.bfloat16
F32 = jnp.float32
EDGE_BLOCK = 128
ROW_TILE = 16
MIB = 1024 * 1024
JOIN_COPIES = 4


def dot(left, right):
    return jnp.dot(left, right, preferred_element_type=F32)


def dot_tn(left, right):
    return lax.dot_general(left, right, (((0,), (0,)), ((), ())), preferred_element_type=F32)


def dot_nt(left, right):
    return lax.dot_general(left, right, (((1,), (1,)), ((), ())), preferred_element_type=F32)


def split(value):
    high = value.astype(BF16)
    return high, (value - high.astype(F32)).astype(BF16)


def one_hot_rows(index_row, count):
    spots = lax.broadcasted_iota(jnp.int32, (count, index_row.shape[1]), 0)
    return jnp.where(spots == index_row, 1.0, 0.0).astype(BF16)


def column(row, lanes):
    upright = jnp.transpose(jnp.broadcast_to(row, (8, row.shape[1])))[:, :1]
    return jnp.broadcast_to(upright, (row.shape[1], lanes))


def silu_and_slope(value):
    sig = 0.5 * jnp.tanh(0.5 * value) + 0.5
    message = value * sig
    return message, sig + message * (1.0 - sig)


def membership(members, node_count):
    spots = lax.broadcasted_iota(jnp.int32, (node_count, members.shape[1]), 0)
    total = jnp.zeros(spots.shape, F32)
    for row in range(members.shape[0]):
        total = total + jnp.where(spots == members[row : row + 1], 1.0, 0.0)
    return total.astype(BF16)


def place():
    me = lax.axis_index("dom")
    return me, lax.rem(me, 2), lax.div(me, 2)


def live_rows(ends_ref, live_ref, row):
    index = ends_ref[row : row + 1, :]
    slot = lax.broadcasted_iota(jnp.int32, index.shape, 1)
    return jnp.where(slot < live_ref[0] * EDGE_BLOCK, index, -1)


def pick_kernel(*refs):
    count = (len(refs) - 3) // 2
    inputs, (near_ref, far_ref), outputs = refs[:count], refs[count : count + 2], refs[count + 2 : -1]
    copies = [
        pltpu.make_async_copy(source, target, refs[-1].at[spot])
        for spot, (source, target) in enumerate(zip(inputs, outputs, strict=True))
    ]
    for copy in copies:
        copy.start()
    for copy in copies[:2]:
        copy.wait()
    _, odd, _ = place()
    lists = outputs[1][...]
    near = jnp.where(odd == 1, lists[0:1], lists[1:2])
    far = jnp.where(odd == 1, lists[1:2], lists[0:1])
    nodes = outputs[0][...]
    rim = near_ref.shape[0]
    near_ref[...] = dot_tn(one_hot_rows(near, nodes.shape[0]), nodes).astype(BF16)
    far = dot_tn(one_hot_rows(far, nodes.shape[0]), nodes).astype(BF16)
    for start in range(0, far_ref.shape[0], rim):
        far_ref[start : start + rim, :] = far
    for copy in copies[2:]:
        copy.wait()


def rims(near_ref, far_ref, odd):
    near = near_ref[...]
    far = far_ref[: near.shape[0], :]
    return jnp.where(odd == 1, near, far), jnp.where(odd == 1, far, near)


def prepare_kernel(
    rim,
    nodes_ref,
    weights_ref,
    biases_ref,
    ends_ref,
    live_ref,
    members_ref,
    parents_ref,
    cotangent_ref,
    links_ref,
    pre_ref,
    outof_ref,
    into_ref,
    share_ref,
    family_ref,
    side_ref,
    upright_ref,
    pooled_ref,
    link_ref,
):
    node_count, width = nodes_ref.shape
    coarse_count = family_ref.shape[0]
    slots = ends_ref.shape[1]
    lanes = link_ref.shape[1]
    outof_ref[...] = one_hot_rows(live_rows(ends_ref, live_ref, 0), node_count + 2 * rim)
    into_ref[...] = one_hot_rows(live_rows(ends_ref, live_ref, 1), node_count)
    nodes = nodes_ref[...]
    src_proj = jnp.transpose(dot(nodes, weights_ref[0])).astype(BF16)
    dst_proj = jnp.transpose(dot(nodes, weights_ref[1])).astype(BF16)
    chunk = 2 * EDGE_BLOCK
    bias = column(biases_ref[0:1, :], chunk)
    for start in range(0, slots, chunk):
        span = slice(start, start + chunk)
        pre_ref[:, span] = (
            dot(src_proj, outof_ref[rim : rim + node_count, span])
            + dot(dst_proj, into_ref[:, span])
            + bias
        )
    upright_ref[...] = jnp.transpose(weights_ref[0].astype(F32)).astype(BF16)
    share = membership(members_ref[...], node_count)
    share_ref[...] = share
    pooled_ref[...] = dot_tn(share, nodes)
    family = one_hot_rows(parents_ref[...], coarse_count)
    family_ref[...] = family
    parent_grad = dot(family, cotangent_ref[...]).astype(BF16)
    side_ref[:coarse_count, :] = parent_grad[:, :lanes]
    side_ref[coarse_count : 2 * coarse_count, :] = parent_grad[:, lanes:]

    links = links_ref[...]
    own = links.shape[1]
    link_ref[...] = jnp.zeros(link_ref.shape, F32)
    link_ref[0:2, :own] = (links >> 8).astype(F32)
    link_ref[2:4, :own] = (links & 255).astype(F32)
    side_ref[2 * coarse_count :, :] = link_ref[...].astype(BF16)


def forward_kernel(
    member_count,
    near_ref,
    far_ref,
    upright_ref,
    weights_ref,
    pre_ref,
    outof_ref,
    into_ref,
    share_ref,
    pooled_ref,
    side_ref,
    summed_ref,
    slopes_ref,
    packet_ref,
):
    _, odd, _ = place()
    low, high = rims(near_ref, far_ref, odd)
    rim = low.shape[0]
    node_count = into_ref.shape[0]
    rim_proj = dot_nt(upright_ref[...], jnp.concatenate([low, high], 0)).astype(BF16)
    slots = pre_ref.shape[1]
    chunk = 2 * EDGE_BLOCK
    summed = jnp.zeros((node_count, pre_ref.shape[0]), F32)
    for start in range(0, slots, chunk):
        span = slice(start, start + chunk)
        at_rim = jnp.concatenate([outof_ref[:rim, span], outof_ref[rim + node_count :, span]], 0)
        message, slope = silu_and_slope(pre_ref[:, span] + dot(rim_proj, at_rim))
        summed = summed + dot_nt(into_ref[:, span], message.astype(BF16))
        slopes_ref[:, span] = slope.astype(BF16)
    summed = summed.astype(BF16)
    summed_ref[...] = summed
    high, low = split(dot_tn(share_ref[...], summed))
    pooled = pooled_ref[...] + dot(high, weights_ref[2]) + dot(low, weights_ref[2])
    coarse = (pooled / member_count).astype(BF16)
    count = coarse.shape[0]
    lanes = packet_ref.shape[2]
    side = side_ref[...]
    for chip in range(packet_ref.shape[0]):
        packet_ref[chip, :count, :] = coarse[:, :lanes]
        packet_ref[chip, count : 2 * count, :] = coarse[:, lanes:]
        packet_ref[chip, 2 * count :, :] = side


def edge_ends2(packet_ref, repeat_ref, block_ref):
    links = [packet_ref[chip, packet_ref.shape[1] - 8 :, :] for chip in range(packet_ref.shape[0])]
    links = jnp.concatenate([link.astype(F32) for link in links], 0).astype(BF16)
    code = dot(links, repeat_ref[...]) * block_ref[...]
    code = jnp.sum(code.reshape(packet_ref.shape[0], 8, code.shape[1]), 0)
    return (256.0 * code[0:2] + code[2:4]).astype(jnp.int32)


def between_kernel(
    own,
    mine_ref,
    into_ref,
    slopes_ref,
    nodes_ref,
    summed_ref,
    weights_ref,
    coarse_weights_ref,
    slopes_sum_ref,
    updated_ref,
    upright2_ref,
    repeat_ref,
    block_ref,
    ends2_ref,
):
    edge = lax.broadcasted_iota(jnp.int32, repeat_ref.shape, 1)
    owner = ((edge.astype(F32) + 0.5) * (1.0 / own)).astype(jnp.int32)
    spot = lax.broadcasted_iota(jnp.int32, repeat_ref.shape, 0)
    repeat_ref[...] = jnp.where(edge - own * owner == spot, 1.0, 0.0).astype(BF16)
    edge = lax.broadcasted_iota(jnp.int32, block_ref.shape, 1)
    owner = ((edge.astype(F32) + 0.5) * (1.0 / own)).astype(jnp.int32)
    block = lax.broadcasted_iota(jnp.int32, block_ref.shape, 0) >> 3
    block_ref[...] = jnp.where(block == owner, 1.0, 0.0)
    ends2_ref[...] = edge_ends2(mine_ref, repeat_ref, block_ref)
    for spot in range(2):
        upright2_ref[spot] = jnp.transpose(coarse_weights_ref[spot].astype(F32)).astype(BF16)
    slopes_sum_ref[...] = dot_nt(into_ref[...], slopes_ref[...])
    updated_ref[...] = nodes_ref[...].astype(F32) + dot(summed_ref[...], weights_ref[2])


def ordered(mine_ref, theirs_ref, odd, start, count):
    blocks = []
    for chip in range(mine_ref.shape[0]):
        halves = []
        for half in range(2):
            span = slice(start + half * count, start + (half + 1) * count)
            mine = mine_ref[chip, span, :]
            theirs = theirs_ref[chip, span, :]
            halves.append((jnp.where(odd == 1, theirs, mine), jnp.where(odd == 1, mine, theirs)))
        for core in range(2):
            blocks.append(jnp.concatenate([halves[0][core], halves[1][core]], 1))
    return jnp.concatenate(blocks, 0)


def backward_kernel(
    ndom,
    member_count,
    mine_ref,
    theirs_ref,
    coarse_weights_ref,
    upright2_ref,
    repeat_ref,
    block_ref,
    ends2_ref,
    biases_ref,
    nodes_ref,
    near_ref,
    far_ref,
    weights_ref,
    share_ref,
    cotangent_ref,
    summed_ref,
    slopes_sum_ref,
    slopes_ref,
    outof_ref,
    into_ref,
    send_ref,
    keep_ref,
    coarse_ref,
    parent_ref,
    into2_ref,
    message2_ref,
    grad_src2_ref,
    grad_dst2_ref,
    bias2_ref,
    grad_updated_ref,
    grad_src_ref,
    grad_dst_ref,
    slope2_ref,
    edge2_ref,
    outof2_ref,
    grads_ref,
):
    me, odd, _ = place()
    nodes = nodes_ref[...]
    node_count, width = nodes.shape
    coarse_count = share_ref.shape[1]
    total = ndom * coarse_count

    coarse = ordered(mine_ref, theirs_ref, odd, 0, coarse_count)
    parent_all = ordered(mine_ref, theirs_ref, odd, 2 * coarse_count, coarse_count)
    ends2 = jnp.concatenate([ends2_ref[...], edge_ends2(theirs_ref, repeat_ref, block_ref)], 1)
    src2 = dot_nt(upright2_ref[0], coarse).astype(BF16)
    dst2 = dot_nt(upright2_ref[1], coarse).astype(BF16)
    grad_agg2 = dot_nt(parent_all, coarse_weights_ref[2])
    grad_agg2_near = dot_nt(coarse_weights_ref[2], parent_all).astype(BF16)
    bias = column(biases_ref[1:2, :], width)
    step = width
    for start in range(0, message2_ref.shape[1], step):
        span = slice(start, start + step)
        outof = one_hot_rows(ends2[0:1, span], total)
        into = one_hot_rows(ends2[1:2, span], total)
        outof2_ref[:, span] = outof
        into2_ref[:, span] = into
        message, slope = silu_and_slope(dot(src2, outof) + dot(dst2, into) + bias)
        message2_ref[:, span] = message.astype(BF16)
        slope2_ref[:, span] = slope.astype(BF16)
        edge2_ref[:, span] = (dot(grad_agg2_near, into) * slope).astype(BF16)
    grad_src2 = dot_nt(outof2_ref[...], edge2_ref[...])
    grad_dst2 = dot_nt(into2_ref[...], slope2_ref[...]) * grad_agg2
    bias2_ref[...] = jnp.sum(grad_dst2, 0, keepdims=True)
    grad_src2_ref[...] = grad_src2.astype(BF16)
    grad_dst2_ref[...] = grad_dst2.astype(BF16)
    coarse_ref[...] = coarse
    parent_ref[...] = parent_all

    rows = pl.ds(pl.multiple_of(me * coarse_count, coarse_count), coarse_count)
    coarse_grad = (
        parent_ref[rows, :].astype(F32)
        + dot_nt(grad_src2_ref[rows, :], coarse_weights_ref[0])
        + dot_nt(grad_dst2_ref[rows, :], coarse_weights_ref[1])
    )
    share = share_ref[...]
    high, low = split(coarse_grad / member_count)
    grad_updated = cotangent_ref[...].astype(F32) + dot(share, high) + dot(share, low)
    grad_updated_ref[...] = grad_updated

    low, high = rims(near_ref, far_ref, odd)
    extended = jnp.concatenate([low, nodes, high], 0)
    rim = low.shape[0]
    slots = slopes_ref.shape[1]
    grad_updated_near = grad_updated.astype(BF16)
    grad_dst = slopes_sum_ref[...] * dot_nt(grad_updated_near, weights_ref[2])
    grad_summed = dot_nt(weights_ref[2], grad_updated_near).astype(BF16)
    bias1 = jnp.sum(grad_dst, 0, keepdims=True)
    grad_dst = grad_dst.astype(BF16)
    grads_ref[width : 2 * width, :] = dot_tn(nodes, grad_dst).astype(BF16)
    grads_ref[2 * width : 3 * width, :] = dot_tn(summed_ref[...], grad_updated_near).astype(BF16)
    chunk = 2 * EDGE_BLOCK
    grad_src = jnp.zeros((outof_ref.shape[0], width), F32)
    for start in range(0, slots, chunk):
        span = slice(start, start + chunk)
        slope = slopes_ref[:, span].astype(F32)
        edge = (dot(grad_summed, into_ref[:, span]) * slope).astype(BF16)
        grad_src = grad_src + dot_nt(outof_ref[:, span], edge)
    grad_src = grad_src.astype(BF16)
    grad_src_ref[...] = grad_src
    grad_dst_ref[...] = grad_dst
    low = dot_nt(grad_src[:rim], weights_ref[0]).astype(BF16)
    high = dot_nt(grad_src[rim + node_count :], weights_ref[0]).astype(BF16)
    grads_ref[0:width, :] = dot_tn(extended, grad_src).astype(BF16)
    if grads_ref.shape[0] > 3 * width:
        grads_ref[3 * width :, :] = jnp.zeros((grads_ref.shape[0] - 3 * width, width), BF16)
    half = grads_ref.shape[0] // 2
    keep_ref[:half, :] = grads_ref[pl.ds(pl.multiple_of(odd * half, ROW_TILE), half), :]
    send_ref[:half, :] = grads_ref[pl.ds(pl.multiple_of((1 - odd) * half, ROW_TILE), half), :]
    bias_rows = two_rows(bias1, ROW_TILE)
    keep_ref[half : half + ROW_TILE, :] = bias_rows
    send_ref[half : half + ROW_TILE, :] = bias_rows
    base = half + ROW_TILE
    send_ref[base : base + rim, :] = jnp.where(odd == 1, low, high)
    send_ref[base + rim :, :] = jnp.where(odd == 1, high, low)


def two_rows(value, count):
    high = value.astype(BF16).astype(F32)
    row = lax.broadcasted_iota(jnp.int32, (count, value.shape[1]), 0)
    return jnp.where(row == 0, high, jnp.where(row == 1, value - high, 0.0)).astype(BF16)


def tail_spots(rows, chips, rim):
    share = -(-rim // chips)
    chip = rows >> (share.bit_length() - 1)
    return 8 * chip + 4 + rows - share * chip, share


def pair_kernel(keep_ref, came_ref, made_ref, blocks_ref):
    half = keep_ref.shape[0] - ROW_TILE
    chips, _, lanes = blocks_ref.shape
    rows = half // chips
    rim = (came_ref.shape[0] - half - ROW_TILE) // 2
    bias = keep_ref[half:, :].astype(F32) + came_ref[half : half + ROW_TILE, :].astype(F32)
    bias = jnp.sum(bias, 0, keepdims=True)
    far = came_ref[half + ROW_TILE + rim :, :]
    spot, share = tail_spots(lax.broadcasted_iota(jnp.int32, (8 * chips, rim), 1), chips, rim)
    row = lax.broadcasted_iota(jnp.int32, (8 * chips, rim), 0)
    line = lax.broadcasted_iota(jnp.int32, (8, lanes), 0)
    tails = jnp.zeros((8 * chips, lanes), F32)
    bias_tail = jnp.zeros((8, lanes), F32)
    for side in range(2):
        span = slice(side * lanes, (side + 1) * lanes)
        pick = jnp.where(row == spot + side * share, 1.0, 0.0).astype(BF16)
        tails = tails + dot(pick, far[:, span])
        value = bias[:, span]
        high = value.astype(BF16).astype(F32)
        bias_tail = jnp.where(line == 2 * side, high, bias_tail)
        bias_tail = jnp.where(line == 2 * side + 1, value - high, bias_tail)
    for chip in range(chips):
        span = slice(chip * rows, (chip + 1) * rows)
        total = (keep_ref[span, :].astype(F32) + came_ref[span, :].astype(F32)).astype(BF16)
        blocks_ref[chip, :rows, :] = total[:, :lanes]
        blocks_ref[chip, rows : 2 * rows, :] = total[:, lanes:]
        blocks_ref[chip, 2 * rows :, :] = (tails[8 * chip : 8 * chip + 8] + bias_tail).astype(BF16)


def sum_kernel(blocks_ref, part_ref, bias1_ref):
    _, odd, _ = place()
    chips, depth, lanes = blocks_ref.shape
    rows = depth - 8
    total = blocks_ref[0].astype(F32)
    for other in range(1, chips):
        total = total + blocks_ref[other].astype(F32)
    part = total[:rows].astype(BF16)
    for other in range(chips):
        after = blocks_ref[min(other + 1, chips - 1), rows:, :]
        before = blocks_ref[max(other - 1, 0), rows:, :]
        part_ref[other, :rows, :] = part
        part_ref[other, rows:, :] = jnp.where(odd == 1, after, before)
    for side in range(2):
        row = rows + 2 * side
        bias1_ref[:, side * lanes : (side + 1) * lanes] = jnp.sum(
            total[row : row + 2], 0, keepdims=True
        )


def coarse_kernel(
    coarse_ref,
    parent_ref,
    into2_ref,
    message2_ref,
    grad_src2_ref,
    grad_dst2_ref,
    coarse_grads_ref,
    coarse_sum_ref,
):
    coarse = coarse_ref[...]
    coarse_sum = dot_nt(into2_ref[...], message2_ref[...]).astype(BF16)
    coarse_sum_ref[...] = coarse_sum
    coarse_grads_ref[0] = dot_tn(coarse, grad_src2_ref[...])
    coarse_grads_ref[1] = dot_tn(coarse, grad_dst2_ref[...])
    coarse_grads_ref[2] = dot_tn(coarse_sum, parent_ref[...])


def finish_kernel(
    coarse_weights_ref,
    weights_ref,
    coarse_ref,
    coarse_sum_ref,
    updated_ref,
    family_ref,
    grad_updated_ref,
    grad_src_ref,
    grad_dst_ref,
    lists_ref,
    came_ref,
    mine_ref,
    bias1_ref,
    bias2_ref,
    coarse_grads_ref,
    moved_ref,
    node_grads_ref,
    bias_ref,
    coarse_grads_hbm,
    sems,
):
    copy = pltpu.make_async_copy(coarse_grads_ref, coarse_grads_hbm, sems.at[0])
    copy.start()
    bias_ref[0:1, :] = bias1_ref[...]
    bias_ref[1:2, :] = bias2_ref[...]
    me, odd, chip = place()
    node_count = updated_ref.shape[0]
    coarse_count = family_ref.shape[0]
    chips, depth, lanes = mine_ref.shape
    rim = lists_ref.shape[1]
    rows = pl.ds(pl.multiple_of(me * coarse_count, coarse_count), coarse_count)
    coarse_new = coarse_ref[rows, :].astype(F32) + dot(
        coarse_sum_ref[rows, :], coarse_weights_ref[2]
    )
    family = family_ref[...]
    high, low = split(coarse_new)
    moved_ref[...] = updated_ref[...] + dot_tn(family, high) + dot_tn(family, low)
    both = jnp.concatenate([grad_src_ref[rim : rim + node_count, :], grad_dst_ref[...]], 1)
    node_grads_ref[...] = grad_updated_ref[...] + dot_nt(
        both, jnp.concatenate([weights_ref[0], weights_ref[1]], 1)
    )
    lists = lists_ref[...]
    near_list = jnp.where(odd == 1, lists[0:1], lists[1:2])
    far_list = jnp.where(odd == 1, lists[1:2], lists[0:1])
    inside = jnp.logical_or(jnp.logical_and(odd == 1, chip < chips - 1), jnp.logical_and(odd == 0, chip > 0))
    far_list = jnp.where(inside, far_list, -1)
    near = came_ref[came_ref.shape[0] - 2 * rim : came_ref.shape[0] - rim, :]
    node_grads_ref[...] += dot(one_hot_rows(near_list, node_count), near)
    tails = [mine_ref[other, depth - 8 :, :].astype(F32) for other in range(chips)]
    tails = jnp.concatenate(tails, 0).astype(BF16)
    spot, share = tail_spots(lax.broadcasted_iota(jnp.int32, (rim, 8 * chips), 0), chips, rim)
    column_spot = lax.broadcasted_iota(jnp.int32, (rim, 8 * chips), 1)
    into = one_hot_rows(far_list, node_count)
    for side in range(2):
        pick = jnp.where(column_spot == spot + side * share, 1.0, 0.0).astype(BF16)
        far = dot(pick, tails).astype(BF16)
        node_grads_ref[:, side * lanes : (side + 1) * lanes] += dot(into, far)
    copy.wait()


def join_kernel(
    mine_ref,
    theirs_ref,
    moved_ref,
    node_grads_ref,
    bias_ref,
    out_hbm,
    moved_hbm,
    node_grads_hbm,
    bias_hbm,
    out_ref,
    sems,
):
    ready = (
        (bias_ref, bias_hbm),
        (moved_ref, moved_hbm),
        (node_grads_ref, node_grads_hbm),
    )
    copies = [
        pltpu.make_async_copy(source, target, sems.at[spot])
        for spot, (source, target) in enumerate(ready)
    ]
    for copy in copies:
        copy.start()
    _, odd, _ = place()
    chips, depth, lanes = mine_ref.shape
    rows = (depth - 8) // 2
    limit = out_ref.shape[0]
    pieces = 0
    done = 0
    for block in range(2 * chips):
        core, chip = divmod(block, chips)
        start = block * rows
        count = min(rows, limit - start)
        if count <= 0:
            break
        for side in range(2):
            span = slice(side * rows, side * rows + count)
            mine = mine_ref[chip, span, :]
            theirs = theirs_ref[chip, span, :]
            out_ref[start : start + count, side * lanes : (side + 1) * lanes] = jnp.where(
                odd == core, mine, theirs
            ).astype(F32)
        end = start + count
        if end == limit or end >= (pieces + 1) * limit // JOIN_COPIES:
            pieces += 1
            span = pl.ds(done, end - done)
            copies.append(
                pltpu.make_async_copy(
                    out_ref.at[span, :], out_hbm.at[span, :], sems.at[len(copies)]
                )
            )
            copies[-1].start()
            done = end
    for copy in copies:
        copy.wait()


def call(
    kernel, outs, args, room, scratch=(), scalars=(), outside=(), copies=0, flops=0, outgoing=()
):
    vmem = pl.BlockSpec(memory_space=pltpu.VMEM)
    scalar = pl.BlockSpec(memory_space=pltpu.SMEM)
    hbm = pl.BlockSpec(memory_space=pltpu.HBM)
    specs = [
        scalar if spot in scalars else hbm if spot in outside else vmem for spot in range(len(args))
    ]
    args = [
        pltpu.with_memory_space_constraint(value, pltpu.HBM) if spot in outside else value
        for spot, value in enumerate(args)
    ]
    moved = sum(value.size * value.dtype.itemsize for value in args)
    moved += sum(math.prod(shape) * jnp.dtype(kind).itemsize for shape, kind in outs)
    scratch = [pltpu.VMEM(shape, kind) for shape, kind in scratch]
    if copies:
        scratch.append(pltpu.SemaphoreType.DMA((copies,)))
    return pl.pallas_call(
        kernel,
        out_shape=[jax.ShapeDtypeStruct(shape, kind) for shape, kind in outs],
        in_specs=specs,
        out_specs=[hbm if spot in outgoing else vmem for spot in range(len(outs))],
        scratch_shapes=scratch,
        compiler_params=pltpu.CompilerParams(vmem_limit_bytes=room * MIB),
        cost_estimate=pl.CostEstimate(flops=flops, bytes_accessed=moved, transcendentals=0),
    )(*args)


def round_up(value, unit):
    return -(-value // unit) * unit


def shards(
    nodes,
    cotangent,
    fine_weights,
    coarse_weights,
    biases,
    send_lists,
    edge_ends,
    live_blocks,
    pool_members,
    parents,
    coarse_ends,
):
    ndom = lax.axis_size("dom")
    chips = ndom // 2
    node_count, width = nodes.shape
    rim = send_lists.shape[1]
    member_count, coarse_count = pool_members.shape
    slots = edge_ends.shape[1]
    edge_count2 = coarse_ends.shape[1] * ndom
    total = coarse_count * ndom
    parents = parents.reshape(1, node_count)
    pairs = [(i, i ^ 1) for i in range(ndom)]
    across = [(i, i + 1) for i in range(1, ndom - 1, 2)]
    across = across + [(target, source) for source, target in across]
    same_core = [[2 * chip + core for chip in range(chips)] for core in range(2)]

    def swap(value):
        return lax.ppermute(value, "dom", pairs)

    def exchange(value):
        return lax.all_to_all(value, "dom", 0, 0, axis_index_groups=same_core)

    rim_rows = ((rim, width), BF16)
    square = ((width, width), BF16)
    inputs = (
        nodes,
        send_lists,
        fine_weights,
        edge_ends,
        cotangent,
        biases,
        pool_members,
        parents,
        coarse_ends,
    )
    (
        near,
        far,
        nodes,
        lists,
        fine,
        edge_ends,
        upstream,
        own_biases,
        pool_members,
        parents,
        coarse_ends,
    ) = call(
        pick_kernel,
        [rim_rows, ((3 * rim, width), BF16)] + [(value.shape, value.dtype) for value in inputs],
        inputs,
        4,
        outside=range(len(inputs)),
        copies=len(inputs),
    )
    far = lax.ppermute(far, "dom", across)
    near = swap(near)

    lanes = width // 2
    side_rows = 2 * coarse_count + 8
    pre, outof, into, share, family, side, upright, pooled = call(
        functools.partial(prepare_kernel, rim),
        [
            ((width, slots), F32),
            ((node_count + 2 * rim, slots), BF16),
            ((node_count, slots), BF16),
            ((node_count, coarse_count), BF16),
            ((coarse_count, node_count), BF16),
            ((side_rows, lanes), BF16),
            square,
            ((coarse_count, width), F32),
        ],
        (
            nodes,
            fine,
            own_biases,
            edge_ends,
            live_blocks,
            pool_members,
            parents,
            upstream,
            coarse_ends,
        ),
        10,
        scratch=[((8, lanes), F32)],
        scalars=(4,),
        flops=2 * slots * width * (2 * node_count + 2 * rim),
    )
    summed, slopes, packet = call(
        functools.partial(forward_kernel, member_count),
        [
            ((node_count, width), BF16),
            ((width, slots), BF16),
            ((chips, 2 * coarse_count + side_rows, lanes), BF16),
        ],
        (near, far, upright, fine, pre, outof, into, share, pooled, side),
        10,
    )
    mine = exchange(packet)
    edges2 = edge_count2 // 2
    slopes_sum, updated, upright2, repeat, block, ends2 = call(
        functools.partial(between_kernel, coarse_ends.shape[1]),
        [
            ((node_count, width), F32),
            ((node_count, width), F32),
            ((2, width, width), BF16),
            ((lanes, edges2), BF16),
            ((8 * chips, edges2), F32),
            ((2, edges2), jnp.int32),
        ],
        (mine, into, slopes, nodes, summed, fine, coarse_weights),
        8,
        flops=2 * slots * width * node_count,
    )
    theirs = swap(mine)

    rows = round_up(-(-3 * width // ndom), ROW_TILE)
    half = rows * chips
    coarse_whole = ((total, width), BF16)
    (
        send,
        keep,
        coarse,
        parent_all,
        into2,
        message2,
        grad_src2,
        grad_dst2,
        bias2,
        grad_updated,
        grad_src,
        grad_dst,
    ) = call(
        functools.partial(backward_kernel, ndom, member_count),
        [
            ((half + ROW_TILE + 2 * rim, width), BF16),
            ((half + ROW_TILE, width), BF16),
            coarse_whole,
            coarse_whole,
            ((total, edge_count2), BF16),
            ((width, edge_count2), BF16),
            coarse_whole,
            coarse_whole,
            ((1, width), F32),
            ((node_count, width), F32),
            ((node_count + 2 * rim, width), BF16),
            ((node_count, width), BF16),
        ],
        (
            mine,
            theirs,
            coarse_weights,
            upright2,
            repeat,
            block,
            ends2,
            own_biases,
            nodes,
            near,
            far,
            fine,
            share,
            upstream,
            summed,
            slopes_sum,
            slopes,
            outof,
            into,
        ),
        20 if total <= 256 else 48,
        scratch=[
            ((width, edge_count2), BF16),
            ((width, edge_count2), BF16),
            ((total, edge_count2), BF16),
            ((2 * half, width), BF16),
        ],
    )
    came = swap(send)
    coarse_grads, coarse_sum = call(
        coarse_kernel,
        [((3, width, width), F32), coarse_whole],
        (coarse, parent_all, into2, message2, grad_src2, grad_dst2),
        8 if total <= 256 else 24,
        flops=6 * total * width * width,
    )
    packet = ((chips, 2 * rows + 8, lanes), BF16)
    (blocks,) = call(pair_kernel, [packet], (keep, came, coarse_sum), 4)
    blocks = exchange(blocks)
    part, bias1 = call(sum_kernel, [packet, ((1, width), F32)], (blocks,), 4)
    mine = exchange(part)
    coarse_grads_shape = ((3, width, width), F32)
    node_shape = ((node_count, width), F32)
    bias_shape = ((2, width), F32)
    moved, node_grads, bias_grads, coarse_grads = call(
        finish_kernel,
        [node_shape, node_shape, bias_shape, coarse_grads_shape],
        (
            coarse_weights,
            fine,
            coarse,
            coarse_sum,
            updated,
            family,
            grad_updated,
            grad_src,
            grad_dst,
            lists,
            came,
            mine,
            bias1,
            bias2,
            coarse_grads,
        ),
        8,
        copies=1,
        outgoing=(3,),
        flops=8 * node_count * width * width,
    )
    theirs = swap(mine)
    fine_grads, moved, node_grads, bias_grads = call(
        join_kernel,
        [((3 * width, width), F32), node_shape, node_shape, bias_shape],
        (mine, theirs, moved, node_grads, bias_grads),
        4,
        scratch=[((3 * width, width), F32)],
        copies=3 + JOIN_COPIES,
        outgoing=range(4),
    )
    return moved, node_grads, fine_grads.reshape(3, width, width), coarse_grads, bias_grads


def solution(mesh):
    return jax.shard_map(
        shards,
        mesh=mesh,
        in_specs=(
            P(("groups", "dom"), None),
            P(("groups", "dom"), None),
            P(),
            P(),
            P(),
            P("groups", "dom"),
            P("groups", "dom"),
            P(("groups", "dom")),
            P("groups", "dom"),
            P(("groups", "dom")),
            P("groups", "dom"),
        ),
        out_specs=(
            P(("groups", "dom"), None),
            P(("groups", "dom"), None),
            P("groups", None, None),
            P("groups", None, None),
            P("groups", None),
        ),
        check_vma=False,
    )
```
